32 devices in a mesh: seq: 16 (over z, y, core), dp: 2 (over x).
Axes of the slice: x: 2, y: 2, z: 4, core: 2. Of those that a mesh axis runs over, the one named last changes fastest.
Arguments:
- bases: int32 [2, 2816], P('dp', 'seq'), may hold values from 0 to 3
- embed: bfloat16 [4, 768], replicated, may hold values from -6 to 6
- conv_weight: bfloat16 [3, 2304, 384], replicated, may hold values from -0.125 to 0.125
- point_weight: bfloat16 [3, 384, 768], replicated, may hold values from -0.3125 to 0.3125
- cotangent: bfloat16 [2, 2816, 768], P('dp', 'seq'), may hold values from -6 to 6
Outputs:
- features: float32 [2, 2816, 768], P('dp', 'seq')
- conv_grad: float32 [3, 2304, 384], P(None, 'seq')
- point_grad: float32 [3, 384, 768], P(None, None, 'seq')
- embed_grad: float32 [4, 768], P(None, 'seq')
The draws below stay inside these ranges and needn't reach their ends.
All inputs are finite; a program needn't handle non-finite values.
Results may differ from the reference program's by a relative error of at most 0.012.
Values may be sent and summed in bfloat16 or wider, within the bound.
No kernel may reach another device: no remote copies, remote signals or barrier semaphores. Data moves between devices by JAX's collectives and lax.ppermute only.
A program may use at most 128 MiB of HBM per device.

```python
import math
import jax
import jax.numpy as jnp
from jax import lax

D = 768
MID = 384
LAYERS = 3
LENGTH = 2816
SEQS = 2
DILATION_FIRST = 22
DILATION_SECOND = 352
DILATION_THIRD = 1408


def with_ends(values, stream_key, low, largest):
    shape = values.shape
    place = [jax.random.randint(jax.random.fold_in(stream_key, axis), (), 0, shape[axis]) for axis in range(len(shape))]
    values = values.at[tuple(place)].set(low)
    longest = shape.index(max(shape))
    place[longest] = (place[longest] + 1) % shape[longest]
    return values.at[tuple(place)].set(largest)


def spiked(array, stream_key, source, target, shards_of, factor):
    owner, partner = [(jnp.arange(array.shape[dim]) // (array.shape[dim] // shards_of)).reshape([-1 if axis == dim else 1 for axis in range(array.ndim)]) for dim in (source, target)]
    chosen = jax.random.permutation(stream_key, shards_of)[partner]
    strong = (owner == chosen) | (owner == (partner + shards_of // 2) % shards_of)
    return jnp.where(strong, factor * array, array)


def shard_levels(stream_key, extent, shards, smallest, largest):
    factor_of = 1.0
    for axis_at, shards_of in shards:
        draws = jax.random.uniform(jax.random.fold_in(jax.random.fold_in(stream_key, 6), axis_at), (shards_of,), jnp.float32, smallest / len(shards), largest / len(shards))
        factor_of = factor_of * jnp.repeat(jnp.exp(draws), extent[axis_at] // shards_of).reshape((-1,) + (1,) * (len(extent) - 1 - axis_at))
    return factor_of


def centred(own_key, shape, spread, limit, shards=(), held_as=jnp.bfloat16):
    entries = spread * jax.random.normal(own_key, shape, jnp.float32)
    if shards:
        entries = entries * shard_levels(own_key, shape, shards, -0.22, 0.18)
    return jnp.clip(entries, -limit, limit).astype(held_as)


def heavy_noise(rng, extent, scale, reach, split, heavy, kind=jnp.bfloat16):
    array = scale * jax.random.normal(rng, extent, jnp.float32)
    if split:
        array = array * shard_levels(rng, extent, split, -0.22, 0.18)
    return jnp.clip(spiked(array, jax.random.fold_in(rng, 3), *heavy), -reach, reach).astype(kind)


def setup_inputs(seed: int = 0) -> dict:
    keys = jax.random.split(jax.random.key(seed), 6)
    bases = with_ends(jax.random.randint(keys[0], (SEQS, LENGTH), 0, 4), jax.random.fold_in(keys[0], 1), 0, 3).astype(jnp.int32)
    embed = centred(keys[1], (4, D), 1.0, 6.0)
    conv_weight = centred(keys[2], (LAYERS, 3 * D, MID), (3 * D) ** -0.5, 0.125)
    point_weight = centred(keys[3], (LAYERS, MID, D), MID ** -0.5, 0.3125)
    cotangent = heavy_noise(keys[4], (SEQS, LENGTH, D), 1.0, 6.0, ((0, 2), (1, 16)), (1, 2, 16, 2.0))
    return dict(bases=bases, embed=embed, conv_weight=conv_weight, point_weight=point_weight, cotangent=cotangent)


def gelu_pair(value_entry):
    coef = math.sqrt(2.0 / math.pi)
    inner = coef * (value_entry + 0.044715 * value_entry * value_entry * value_entry)
    tanh_val = jnp.tanh(inner)
    result = 0.5 * value_entry * (1.0 + tanh_val)
    slope = 0.5 * (1.0 + tanh_val) + 0.5 * value_entry * (1.0 - tanh_val * tanh_val) * coef * (1.0 + 3.0 * 0.044715 * value_entry * value_entry)
    return (result, slope)

def moved_kernel_taps(value_entry, dilation_step):
    zero_padding = jnp.zeros((dilation_step, value_entry.shape[1]), value_entry.dtype)
    lower_window = jnp.concatenate([zero_padding, value_entry[:-dilation_step]], axis=0)
    upper_window = jnp.concatenate([value_entry[dilation_step:], zero_padding], axis=0)
    return jnp.concatenate([lower_window, value_entry, upper_window], axis=1)

def one_sequence(bases_row, cot_row, embed, conv_weight, point_weight):
    dilation_list = [DILATION_FIRST, DILATION_SECOND, DILATION_THIRD]
    residual_state = embed[bases_row].astype(jnp.float32)
    saved = []
    for layer in range(LAYERS):
        scale = lax.rsqrt(lax.optimization_barrier(jnp.mean(residual_state * residual_state, axis=-1, keepdims=True)) + 1e-06)
        normalized_rows = (residual_state * scale).astype(jnp.bfloat16)
        kernel_taps = moved_kernel_taps(normalized_rows, dilation_list[layer])
        pre = jnp.dot(kernel_taps, conv_weight[layer], preferred_element_type=jnp.float32)
        act_f, slope = gelu_pair(pre)
        act = act_f.astype(jnp.bfloat16)
        saved.append((residual_state, scale, kernel_taps, act, slope))
        residual_state = residual_state + jnp.dot(act, point_weight[layer], preferred_element_type=jnp.float32)
    features = residual_state
    back = cot_row.astype(jnp.float32)
    conv_list = []
    point_list = []
    for layer in reversed(range(LAYERS)):
        stream_in, scale, kernel_taps, act, slope = saved[layer]
        back_rounded = back.astype(jnp.bfloat16)
        point_list.append(jnp.dot(act.T, back_rounded, preferred_element_type=jnp.float32))
        pre_grad = (jnp.dot(back_rounded, point_weight[layer].T, preferred_element_type=jnp.float32) * slope).astype(jnp.bfloat16)
        conv_list.append(jnp.dot(kernel_taps.T, pre_grad, preferred_element_type=jnp.float32))
        weight_arrays = conv_weight[layer]
        flip = jnp.concatenate([weight_arrays[2 * D:].T, weight_arrays[D:2 * D].T, weight_arrays[:D].T], axis=0)
        grad_taps = moved_kernel_taps(pre_grad, dilation_list[layer])
        normed_grad = jnp.dot(grad_taps, flip, preferred_element_type=jnp.float32)
        inner = lax.optimization_barrier(jnp.mean(normed_grad * stream_in, axis=-1, keepdims=True))
        back = back + scale * (normed_grad - stream_in * scale * scale * inner)
    conv_grad = jnp.stack(conv_list[::-1])
    point_grad = jnp.stack(point_list[::-1])
    onehot = (bases_row[:, None] == jnp.arange(4, dtype=jnp.int32)[None, :]).astype(jnp.float32)
    embed_grad = jnp.dot(onehot.T, back, precision=lax.Precision.HIGHEST)
    return (features, conv_grad, point_grad, embed_grad)

def reference(bases, embed, conv_weight, point_weight, cotangent):

    def step(carry, inputs):
        features, conv_g, point_g, embed_g = one_sequence(inputs[0], inputs[1], embed, conv_weight, point_weight)
        return ((carry[0] + conv_g, carry[1] + point_g, carry[2] + embed_g), features)
    init = (jnp.zeros((LAYERS, 3 * D, MID), jnp.float32), jnp.zeros((LAYERS, MID, D), jnp.float32), jnp.zeros((4, D), jnp.float32))
    totals, features = lax.scan(step, init, (bases, cotangent))
    return (features, totals[0], totals[1], totals[2])
```

```python
import math

import jax
import jax.numpy as jnp
import numpy as np
from jax import lax
from jax.sharding import PartitionSpec as P

BF16 = jnp.bfloat16
F32 = jnp.float32
CLASSES = 128
STRIDE = 8


def gelu_pair(v):
    coef = math.sqrt(2.0 / math.pi)
    inner = coef * (v + 0.044715 * v * v * v)
    t = jnp.tanh(inner)
    slope = 0.5 * (1.0 + t) + 0.5 * v * (1.0 - t * t) * coef * (1.0 + 3.0 * 0.044715 * v * v)
    return 0.5 * v * (1.0 + t), slope


def mm(a, b):
    return jnp.dot(a, b, preferred_element_type=F32)


def mm_tn(a, b):
    return lax.dot_general(a, b, (((0,), (0,)), ((), ())), preferred_element_type=F32)


def mm_nt(a, b):
    return lax.dot_general(a, b, (((1,), (1,)), ((), ())), preferred_element_type=F32)


def halves(v):
    high = lax.reduce_precision(v, 8, 7)
    return high.astype(BF16), (v - high).astype(BF16)


def selectors():
    c = np.arange(CLASSES)
    digits = (c // 20, (c // 5) % 4, c % 5)
    valid = (c < 100)[:, None]
    return [((d[:, None] == np.arange(4)[None, :]) & valid).astype(np.float32) for d in digits]


def norm_scale(v):
    return lax.rsqrt(jnp.mean(v * v, axis=-1, keepdims=True) + 1e-06)


def tables(embed, conv_weight, point_weight):
    sel = [jnp.asarray(s, BF16) for s in selectors()]
    stream = embed.astype(F32)
    scale_e = norm_scale(stream)
    normed_e = (stream * scale_e).astype(BF16)
    taps = jnp.concatenate([mm(s, normed_e).astype(BF16) for s in sel], axis=1)
    act0, slope0 = gelu_pair(mm(taps, conv_weight[0]))
    act0 = act0.astype(BF16)
    stab = mm(sel[1], embed) + mm(act0, point_weight[0])
    scale1 = norm_scale(stab)
    ntab = (stab * scale1).astype(BF16)
    width = embed.shape[1]
    u = jnp.concatenate([mm(ntab, conv_weight[1, j * width : (j + 1) * width]) for j in range(3)])
    return stream, scale_e, normed_e, act0, slope0, stab, scale1, ntab, u


def classes(gathered, dil):
    n, rb = gathered.shape
    edge = jnp.full((1, dil), 4, jnp.int32)
    left = jnp.concatenate(
        [jnp.concatenate([edge, gathered[:-1, rb - dil :]]), gathered[:, : rb - dil]], axis=1
    )
    right = jnp.concatenate(
        [gathered[:, dil:], jnp.concatenate([gathered[1:, :dil], edge])], axis=1
    )
    cls = left * 20 + gathered * 5 + right
    none = jnp.full((2, rb), -1, jnp.int32)
    return jnp.concatenate([none, cls, none])


def on_device(bases, embed, conv_weight, point_weight, cotangent):
    n, dp = lax.axis_size("seq"), lax.axis_size("dp")
    rb, width, mid = bases.shape[1], embed.shape[1], conv_weight.shape[2]
    group = n // STRIDE
    k, x = lax.axis_index("seq"), lax.axis_index("dp")
    zh, r = k // STRIDE, k % STRIDE
    m, core = r // 2, r % 2
    rows = group * rb
    w1, w2 = conv_weight[1], conv_weight[2]
    p0, p1, p2 = point_weight[0], point_weight[1], point_weight[2]

    gathered = lax.all_to_all(jnp.broadcast_to(bases, (n, rb)), "seq", 0, 0, tiled=True)
    own = cotangent[0]
    parts = [own]
    for i in range(1, group):
        parts.append(lax.ppermute(own, "seq", [(s, (s - STRIDE * i) % n) for s in range(n)]))
    cot = lax.dynamic_slice_in_dim(
        jnp.concatenate(parts + parts), ((group - zh) % group) * rb, rows
    )

    stream_e, scale_e, normed_e, act0, slope0, stab, scale1, ntab, u = tables(
        embed, conv_weight, point_weight
    )
    u_high, u_low = halves(u)
    s_high, s_low = halves(stab)

    cls = classes(gathered, rb // 8)
    hots = []
    for j in range(3):
        index = jnp.concatenate(
            [lax.dynamic_slice(cls, (a * STRIDE + r + 2 * j, 0), (1, rb)) for a in range(group)],
            axis=1,
        )
        hots.append((jnp.arange(CLASSES, dtype=jnp.int32)[:, None] == index).astype(BF16))
    hot = jnp.concatenate(hots)

    pre1 = mm_tn(hot, u_high) + mm_tn(hot, u_low)
    act1, slope1 = gelu_pair(pre1)
    act1 = act1.astype(BF16)
    stream2 = mm_tn(hots[1], s_high) + mm_tn(hots[1], s_low) + mm(act1, p1)
    scale2 = norm_scale(stream2)
    normed2 = (stream2 * scale2).astype(BF16)
    nothing = jnp.zeros((rb, width), BF16)
    taps2 = jnp.concatenate(
        [
            jnp.concatenate([nothing, normed2[: rows - rb]]),
            normed2,
            jnp.concatenate([normed2[rb:], nothing]),
        ],
        axis=1,
    )
    pre2 = mm(taps2, w2)
    act2, slope2 = gelu_pair(pre2)
    act2 = act2.astype(BF16)
    features = lax.dynamic_slice_in_dim(stream2, zh * rb, rb) + mm(
        lax.dynamic_slice_in_dim(act2, zh * rb, rb), p2
    )

    grad2 = (mm_nt(cot, p2) * slope2).astype(BF16)
    nothing = jnp.zeros((rb, mid), BF16)
    above = jnp.concatenate([grad2[rb:], nothing])
    below = jnp.concatenate([nothing, grad2[: rows - rb]])
    ng2 = (
        mm_nt(above, w2[:width]) + mm_nt(grad2, w2[width : 2 * width]) + mm_nt(below, w2[2 * width :])
    )
    inner = jnp.mean(ng2 * stream2, axis=-1, keepdims=True)
    back2 = cot.astype(F32) + scale2 * (ng2 - stream2 * scale2 * scale2 * inner)
    back2 = back2.astype(BF16)
    grad1 = (mm_nt(back2, p1) * slope1).astype(BF16)

    h = mm(hot, grad1).astype(BF16)
    ng1 = sum(
        mm_nt(h[j * CLASSES : (j + 1) * CLASSES], w1[j * width : (j + 1) * width]) for j in range(3)
    )
    inner = jnp.mean(ng1 * stab, axis=-1, keepdims=True)
    b = mm(hots[1], back2) + scale1 * (ng1 - stab * scale1 * scale1 * inner)
    b16 = b.astype(BF16)
    s = (mm_nt(b16, p0) * slope0).astype(BF16)
    sel = selectors()
    g = mm(jnp.asarray(np.concatenate([v.T for v in sel]), BF16), s)
    bt = mm(jnp.asarray(sel[1].T, BF16), b16)
    small = jnp.concatenate([g, bt.reshape(2 * 4, mid)])

    crow, prow = 3 * width // n, width // n
    conv1 = jnp.concatenate(
        [mm_tn(ntab, h[j * CLASSES : (j + 1) * CLASSES]) for j in range(3)]
    )
    conv1 = lax.dynamic_slice_in_dim(conv1, zh * STRIDE * crow, STRIDE * crow)
    conv2 = mm_tn(lax.dynamic_slice_in_dim(taps2, zh * STRIDE * crow, STRIDE * crow, axis=1), grad2)

    def share(v):
        return lax.dynamic_slice_in_dim(v, zh * STRIDE * prow, STRIDE * prow, axis=1)

    point = [mm_tn(share(b16), act0), mm_tn(share(back2), act1), mm_tn(share(cot), act2)]
    tile = jnp.concatenate(
        [conv1.reshape(STRIDE, crow, mid), conv2.reshape(STRIDE, crow, mid)]
        + [v.reshape(STRIDE, prow, mid) for v in point],
        axis=1,
    )
    trow = 2 * crow + 3 * prow
    half = STRIDE // 2
    tile = tile.reshape(half, 2, trow, mid)

    swap = [(s, s ^ 1) for s in range(n)]
    mine = lax.dynamic_index_in_dim(tile, core, axis=1, keepdims=False)
    other = lax.dynamic_index_in_dim(tile, 1 - core, axis=1, keepdims=False)
    mine = mine + lax.ppermute(other.astype(BF16), "seq", swap).astype(F32)
    small = small + lax.ppermute(small.astype(BF16), "seq", swap).astype(F32)

    drow = trow // dp
    mine = mine.reshape(half, dp, drow, mid)
    small16 = small.astype(BF16)
    total = lax.dynamic_slice(mine, (m, x, 0, 0), (1, 1, drow, mid))[0, 0]
    for mask in range(half * dp - 1, 0, -1):
        mm_, mx = mask // dp, mask % dp
        piece = lax.dynamic_slice(mine, (m ^ mm_, x ^ mx, 0, 0), (1, 1, drow, mid))[0, 0]
        message = jnp.concatenate([piece.astype(BF16), small16])
        route = [
            (s * dp + d, (s ^ (2 * mm_)) * dp + (d ^ mx)) for s in range(n) for d in range(dp)
        ]
        got = lax.ppermute(message, ("seq", "dp"), route).astype(F32)
        total = total + got[:drow]
        small = small + got[drow:]

    total16 = total.astype(BF16)
    pieces = [total16] + [
        lax.ppermute(total16, "dp", [(d, d ^ i) for d in range(dp)]) for i in range(1, dp)
    ]
    full = jnp.concatenate(
        [
            sum(jnp.where((x ^ i) == d, pieces[i].astype(F32), 0.0) for i in range(dp))
            for d in range(dp)
        ]
    )

    g, bt = small[:12], small[12:].reshape(4, width)
    ng0 = sum(
        mm_nt(g[4 * j : 4 * j + 4].astype(BF16), conv_weight[0, j * width : (j + 1) * width])
        for j in range(3)
    )
    inner = jnp.mean(ng0 * stream_e, axis=-1, keepdims=True)
    embed_grad = bt + scale_e * (ng0 - stream_e * scale_e * scale_e * inner)
    embed_grad = lax.dynamic_slice_in_dim(embed_grad, k * prow, prow, axis=1)
    spread = jnp.concatenate(
        [
            jnp.pad(normed_e, ((4 * j, 8 - 4 * j), (0, 0))) for j in range(3)
        ],
        axis=1,
    )
    spread = lax.dynamic_slice_in_dim(spread, k * crow, crow, axis=1)
    conv0 = mm_tn(spread, g.astype(BF16))
    conv_grad = jnp.stack([conv0, full[:crow], full[crow : 2 * crow]])
    point_grad = full[2 * crow :].reshape(3, prow, mid).transpose(0, 2, 1)
    return features[None], conv_grad, point_grad, embed_grad


def solution(mesh):
    in_specs = (P("dp", "seq"), P(), P(), P(), P("dp", "seq", None))
    out_specs = (P("dp", "seq", None), P(None, "seq", None), P(None, None, "seq"), P(None, "seq"))
    return jax.shard_map(
        on_device, mesh=mesh, in_specs=in_specs, out_specs=out_specs, check_vma=False
    )
```

```python
import math

import jax
import jax.numpy as jnp
import numpy as np
from jax import lax
from jax.experimental import pallas as pl
from jax.experimental.pallas import tpu as pltpu
from jax.sharding import PartitionSpec as P

BF16 = jnp.bfloat16
F32 = jnp.float32
CLASSES = 128
STRIDE = 8


def gelu_pair(v):
    coef = math.sqrt(2.0 / math.pi)
    inner = coef * (v + 0.044715 * v * v * v)
    t = jnp.tanh(inner)
    slope = 0.5 * (1.0 + t) + 0.5 * v * (1.0 - t * t) * coef * (1.0 + 3.0 * 0.044715 * v * v)
    return 0.5 * v * (1.0 + t), slope


def mm(a, b):
    return jnp.dot(a, b, preferred_element_type=F32)


def mm_tn(a, b):
    return lax.dot_general(a, b, (((0,), (0,)), ((), ())), preferred_element_type=F32)


def mm_nt(a, b):
    return lax.dot_general(a, b, (((1,), (1,)), ((), ())), preferred_element_type=F32)


def halves(v):
    high = lax.reduce_precision(v, 8, 7)
    return high.astype(BF16), (v - high).astype(BF16)


def selectors():
    c = np.arange(CLASSES)
    digits = (c // 20, (c // 5) % 4, c % 5)
    valid = (c < 100)[:, None]
    return [((d[:, None] == np.arange(4)[None, :]) & valid).astype(np.float32) for d in digits]


def norm_scale(v):
    return lax.rsqrt(jnp.mean(v * v, axis=-1, keepdims=True) + 1e-06)


def tables(embed, conv_weight, point_weight):
    sel = [jnp.asarray(s, BF16) for s in selectors()]
    stream = embed.astype(F32)
    scale_e = norm_scale(stream)
    normed_e = (stream * scale_e).astype(BF16)
    taps = jnp.concatenate([mm(s, normed_e).astype(BF16) for s in sel], axis=1)
    act0, slope0 = gelu_pair(mm(taps, conv_weight[0]))
    act0 = act0.astype(BF16)
    stab = mm(sel[1], embed) + mm(act0, point_weight[0])
    scale1 = norm_scale(stab)
    ntab = (stab * scale1).astype(BF16)
    width = embed.shape[1]
    u = jnp.concatenate([mm(ntab, conv_weight[1, j * width : (j + 1) * width]) for j in range(3)])
    return stream, scale_e, normed_e, act0, slope0, stab, scale1, ntab, u


def classes(gathered, dil):
    n, rb = gathered.shape
    edge = jnp.full((1, dil), 4, jnp.int32)
    left = jnp.concatenate(
        [jnp.concatenate([edge, gathered[:-1, rb - dil :]]), gathered[:, : rb - dil]], axis=1
    )
    right = jnp.concatenate(
        [gathered[:, dil:], jnp.concatenate([gathered[1:, :dil], edge])], axis=1
    )
    cls = left * 20 + gathered * 5 + right
    none = jnp.full((2, rb), -1, jnp.int32)
    return jnp.concatenate([none, cls, none])


def general(bases, embed, conv_weight, point_weight, cotangent):
    n, dp = lax.axis_size("seq"), lax.axis_size("dp")
    rb, width, mid = bases.shape[1], embed.shape[1], conv_weight.shape[2]
    group = n // STRIDE
    k, x = lax.axis_index("seq"), lax.axis_index("dp")
    zh, r = k // STRIDE, k % STRIDE
    m, core = r // 2, r % 2
    rows = group * rb
    w1, w2 = conv_weight[1], conv_weight[2]
    p0, p1, p2 = point_weight[0], point_weight[1], point_weight[2]

    gathered = lax.all_to_all(jnp.broadcast_to(bases, (n, rb)), "seq", 0, 0, tiled=True)
    own = cotangent[0]
    parts = [own]
    for i in range(1, group):
        parts.append(lax.ppermute(own, "seq", [(s, (s - STRIDE * i) % n) for s in range(n)]))
    cot = lax.dynamic_slice_in_dim(
        jnp.concatenate(parts + parts), ((group - zh) % group) * rb, rows
    )

    stream_e, scale_e, normed_e, act0, slope0, stab, scale1, ntab, u = tables(
        embed, conv_weight, point_weight
    )
    u_high, u_low = halves(u)
    s_high, s_low = halves(stab)

    cls = classes(gathered, rb // 8)
    hots = []
    for j in range(3):
        index = jnp.concatenate(
            [lax.dynamic_slice(cls, (a * STRIDE + r + 2 * j, 0), (1, rb)) for a in range(group)],
            axis=1,
        )
        hots.append((jnp.arange(CLASSES, dtype=jnp.int32)[:, None] == index).astype(BF16))
    hot = jnp.concatenate(hots)

    pre1 = mm_tn(hot, u_high) + mm_tn(hot, u_low)
    act1, slope1 = gelu_pair(pre1)
    act1 = act1.astype(BF16)
    stream2 = mm_tn(hots[1], s_high) + mm_tn(hots[1], s_low) + mm(act1, p1)
    scale2 = norm_scale(stream2)
    normed2 = (stream2 * scale2).astype(BF16)
    nothing = jnp.zeros((rb, width), BF16)
    taps2 = jnp.concatenate(
        [
            jnp.concatenate([nothing, normed2[: rows - rb]]),
            normed2,
            jnp.concatenate([normed2[rb:], nothing]),
        ],
        axis=1,
    )
    pre2 = mm(taps2, w2)
    act2, slope2 = gelu_pair(pre2)
    act2 = act2.astype(BF16)
    features = lax.dynamic_slice_in_dim(stream2, zh * rb, rb) + mm(
        lax.dynamic_slice_in_dim(act2, zh * rb, rb), p2
    )

    grad2 = (mm_nt(cot, p2) * slope2).astype(BF16)
    nothing = jnp.zeros((rb, mid), BF16)
    above = jnp.concatenate([grad2[rb:], nothing])
    below = jnp.concatenate([nothing, grad2[: rows - rb]])
    ng2 = (
        mm_nt(above, w2[:width]) + mm_nt(grad2, w2[width : 2 * width]) + mm_nt(below, w2[2 * width :])
    )
    inner = jnp.mean(ng2 * stream2, axis=-1, keepdims=True)
    back2 = cot.astype(F32) + scale2 * (ng2 - stream2 * scale2 * scale2 * inner)
    back2 = back2.astype(BF16)
    grad1 = (mm_nt(back2, p1) * slope1).astype(BF16)

    h = mm(hot, grad1).astype(BF16)
    ng1 = sum(
        mm_nt(h[j * CLASSES : (j + 1) * CLASSES], w1[j * width : (j + 1) * width]) for j in range(3)
    )
    inner = jnp.mean(ng1 * stab, axis=-1, keepdims=True)
    b = mm(hots[1], back2) + scale1 * (ng1 - stab * scale1 * scale1 * inner)
    b16 = b.astype(BF16)
    s = (mm_nt(b16, p0) * slope0).astype(BF16)
    sel = selectors()
    g = mm(jnp.asarray(np.concatenate([v.T for v in sel]), BF16), s)
    bt = mm(jnp.asarray(sel[1].T, BF16), b16)
    small = jnp.concatenate([g, bt.reshape(2 * 4, mid)])

    crow, prow = 3 * width // n, width // n
    conv1 = jnp.concatenate(
        [mm_tn(ntab, h[j * CLASSES : (j + 1) * CLASSES]) for j in range(3)]
    )
    conv1 = lax.dynamic_slice_in_dim(conv1, zh * STRIDE * crow, STRIDE * crow)
    conv2 = mm_tn(lax.dynamic_slice_in_dim(taps2, zh * STRIDE * crow, STRIDE * crow, axis=1), grad2)

    def share(v):
        return lax.dynamic_slice_in_dim(v, zh * STRIDE * prow, STRIDE * prow, axis=1)

    point = [mm_tn(share(b16), act0), mm_tn(share(back2), act1), mm_tn(share(cot), act2)]
    tile = jnp.concatenate(
        [conv1.reshape(STRIDE, crow, mid), conv2.reshape(STRIDE, crow, mid)]
        + [v.reshape(STRIDE, prow, mid) for v in point],
        axis=1,
    )
    trow = 2 * crow + 3 * prow
    half = STRIDE // 2
    tile = tile.reshape(half, 2, trow, mid)

    swap = [(s, s ^ 1) for s in range(n)]
    mine = lax.dynamic_index_in_dim(tile, core, axis=1, keepdims=False)
    other = lax.dynamic_index_in_dim(tile, 1 - core, axis=1, keepdims=False)
    mine = mine + lax.ppermute(other.astype(BF16), "seq", swap).astype(F32)
    small = small + lax.ppermute(small.astype(BF16), "seq", swap).astype(F32)

    drow = trow // dp
    mine = mine.reshape(half, dp, drow, mid)
    small16 = small.astype(BF16)
    total = lax.dynamic_slice(mine, (m, x, 0, 0), (1, 1, drow, mid))[0, 0]
    for mask in range(half * dp - 1, 0, -1):
        mm_, mx = mask // dp, mask % dp
        piece = lax.dynamic_slice(mine, (m ^ mm_, x ^ mx, 0, 0), (1, 1, drow, mid))[0, 0]
        message = jnp.concatenate([piece.astype(BF16), small16])
        route = [
            (s * dp + d, (s ^ (2 * mm_)) * dp + (d ^ mx)) for s in range(n) for d in range(dp)
        ]
        got = lax.ppermute(message, ("seq", "dp"), route).astype(F32)
        total = total + got[:drow]
        small = small + got[drow:]

    total16 = total.astype(BF16)
    pieces = [total16] + [
        lax.ppermute(total16, "dp", [(d, d ^ i) for d in range(dp)]) for i in range(1, dp)
    ]
    full = jnp.concatenate(
        [
            sum(jnp.where((x ^ i) == d, pieces[i].astype(F32), 0.0) for i in range(dp))
            for d in range(dp)
        ]
    )

    g, bt = small[:12], small[12:].reshape(4, width)
    ng0 = sum(
        mm_nt(g[4 * j : 4 * j + 4].astype(BF16), conv_weight[0, j * width : (j + 1) * width])
        for j in range(3)
    )
    inner = jnp.mean(ng0 * stream_e, axis=-1, keepdims=True)
    embed_grad = bt + scale_e * (ng0 - stream_e * scale_e * scale_e * inner)
    embed_grad = lax.dynamic_slice_in_dim(embed_grad, k * prow, prow, axis=1)
    spread = jnp.concatenate(
        [
            jnp.pad(normed_e, ((4 * j, 8 - 4 * j), (0, 0))) for j in range(3)
        ],
        axis=1,
    )
    spread = lax.dynamic_slice_in_dim(spread, k * crow, crow, axis=1)
    conv0 = mm_tn(spread, g.astype(BF16))
    conv_grad = jnp.stack([conv0, full[:crow], full[crow : 2 * crow]])
    point_grad = full[2 * crow :].reshape(3, prow, mid).transpose(0, 2, 1)
    return features[None], conv_grad, point_grad, embed_grad


def normal(v):
    return (v * norm_scale(v)).astype(BF16)


def table_kernel(embed_ref, w0_ref, w1_ref, p0_ref, sel_ref, act0_ref, slope0_ref, stab_ref, sparts_ref, ntab_ref, u_ref):
    width = embed_ref.shape[1]
    normed_e = normal(embed_ref[...].astype(F32))
    pre = None
    for j in range(3):
        taps = mm(sel_ref[j], normed_e).astype(BF16)
        term = mm(taps, w0_ref[j * width : (j + 1) * width, :])
        pre = term if pre is None else pre + term
    act0, slope0 = gelu_pair(pre)
    act0 = act0.astype(BF16)
    act0_ref[...] = act0
    slope0_ref[...] = slope0
    stab = mm(sel_ref[1], embed_ref[...]) + mm(act0, p0_ref[...])
    stab_ref[...] = stab
    high = stab.astype(BF16)
    sparts_ref[:CLASSES, :] = high
    sparts_ref[CLASSES:, :] = (stab - high.astype(F32)).astype(BF16)
    ntab = normal(stab)
    ntab_ref[...] = ntab
    for j in range(3):
        u = mm(ntab, w1_ref[j * width : (j + 1) * width, :])
        high = u.astype(BF16)
        u_ref[j * CLASSES : (j + 1) * CLASSES, :] = high
        u_ref[(3 + j) * CLASSES : (4 + j) * CLASSES, :] = (u - high.astype(F32)).astype(BF16)


def main_kernel(
    crow, prow,
    rowidx_ref, colidx_ref, cot_ref, w1_ref, w2_ref, p0_ref, p1_ref, p2_ref,
    act0_ref, slope0_ref, stab_ref, sparts_ref, ntab_ref, u_ref, selt_ref,
    features_ref, mine_ref, other_ref,
    stream_ref, normed_ref, act1_ref, act2_ref, slope1_ref, slope2_ref, grad_ref, back_ref,
    conv_ref, point_ref, bt_ref,
):
    rows, width = cot_ref.shape
    mid = p0_ref.shape[0]
    rb = rows // 2
    k = lax.axis_index("seq")
    zh, core = k // STRIDE, k % 2
    half = width // 2
    lanes = lax.broadcasted_iota(jnp.int32, (rows, CLASSES), 1)
    hot = [(lanes == colidx_ref[:, j : j + 1]).astype(F32).astype(BF16) for j in range(3)]
    spread = jnp.concatenate(hot + hot, axis=1)
    act1, slope1 = gelu_pair(mm(spread, u_ref[...]))
    act1 = act1.astype(BF16)
    act1_ref[...] = act1
    slope1_ref[...] = slope1
    stream = mm(jnp.concatenate([hot[1], hot[1]], axis=1), sparts_ref[...]) + mm(act1, p1_ref[...])
    stream_ref[...] = stream
    normed = normal(stream)
    normed_ref[...] = normed
    sides = jnp.concatenate(
        [mm(normed[rb:], w2_ref[2 * width :, :]), mm(normed[:rb], w2_ref[:width, :])]
    )
    act2, slope2 = gelu_pair(mm(normed, w2_ref[width : 2 * width, :]) + sides)
    act2_ref[...] = act2.astype(BF16)
    place = pl.ds(pl.multiple_of(zh * rb, 16), rb)
    features_ref[...] = stream_ref[place, :] + mm(act2_ref[place, :], p2_ref[...])

    grad2 = (mm_nt(cot_ref[...], p2_ref[...]) * slope2).astype(BF16)
    grad_ref[...] = grad2
    sides = jnp.concatenate(
        [mm_nt(grad2[rb:], w2_ref[:width, :]), mm_nt(grad2[:rb], w2_ref[2 * width :, :])]
    )
    ng = mm_nt(grad2, w2_ref[width : 2 * width, :]) + sides
    stream = stream_ref[...]
    scale = norm_scale(stream)
    inner = jnp.mean(ng * stream, axis=-1, keepdims=True)
    back = cot_ref[...].astype(F32) + scale * (ng - stream * (scale * scale * inner))
    back = back.astype(BF16)
    back_ref[...] = back
    grad1 = (mm_nt(back, p1_ref[...]) * slope1_ref[...]).astype(BF16)

    ids = lax.broadcasted_iota(jnp.int32, (CLASSES, rows), 0)
    hott = [(ids == rowidx_ref[j : j + 1, :]).astype(F32).astype(BF16) for j in range(3)]
    h = [mm(v, grad1).astype(BF16) for v in hott]
    ng = None
    for j in range(3):
        term = mm_nt(h[j], w1_ref[j * width : (j + 1) * width, :])
        ng = term if ng is None else ng + term
    stab = stab_ref[...]
    scale = norm_scale(stab)
    inner = jnp.mean(ng * stab, axis=-1, keepdims=True)
    b = mm(hott[1], back) + scale * (ng - stab * (scale * scale * inner))
    s = (mm_nt(b.astype(BF16), p0_ref[...]) * slope0_ref[...]).astype(BF16)
    g = mm(selt_ref[...], s)
    bt_ref[...] = jnp.transpose(b)

    columns = pl.ds(pl.multiple_of(zh * half, 128), half)
    side_at = pl.ds(pl.multiple_of(zh * half, 16), width)
    center_at = pl.ds(pl.multiple_of((1 - zh) * width, 16), half)
    far = pl.ds(pl.multiple_of((1 - zh) * rb, 16), rb)
    conv_ref[0, side_at, :] = mm_tn(ntab_ref[...], jnp.where(zh == 0, h[0], h[2]))
    conv_ref[0, center_at, :] = mm_tn(ntab_ref[:, columns], h[1])
    conv_ref[1, side_at, :] = mm_tn(normed_ref[place, :], grad_ref[far, :])
    conv_ref[1, center_at, :] = mm_tn(normed_ref[:, columns], grad_ref[...])
    point_ref[0] = mm_tn(back_ref[:, columns], act1_ref[...])
    point_ref[1] = mm_tn(cot_ref[:, columns], act2_ref[...])
    part = crow + prow
    step = 2 * part + 16
    for target, side in ((mine_ref, core), (other_ref, 1 - core)):
        for m in range(STRIDE // 2):
            tile = 2 * m + side
            crows = pl.ds(pl.multiple_of(tile * crow, 16), crow)
            prows = pl.ds(pl.multiple_of(tile * prow, 16), prow)
            for layer in range(2):
                at = m * step + layer * part
                target[at : at + crow, :] = conv_ref[layer, crows, :].astype(target.dtype)
                target[at + crow : at + part, :] = point_ref[layer, prows, :].astype(target.dtype)
            at = m * step + 2 * part
            for q in range(3):
                place = pl.ds(pl.multiple_of(zh * half + tile * prow + 16 * q, 16), 16)
                target[at : at + 16, q * CLASSES : (q + 1) * CLASSES] = bt_ref[place, :].astype(target.dtype)
        at = STRIDE // 2 * step
        target[at : at + 16, :] = g.astype(target.dtype)


def message_kernel(part, mine_ref, other_ref, *out_refs):
    k, x = lax.axis_index("seq"), lax.axis_index("dp")
    m = (k % STRIDE) // 2
    step = 2 * part + 16
    end = STRIDE // 2 * step
    small = mine_ref[end : end + 16, :] + other_ref[end : end + 16, :].astype(F32)
    for mask, out_ref in enumerate(out_refs):
        target, layer = m ^ (mask // 2), x ^ (mask % 2)
        at = pl.ds(pl.multiple_of(target * step + layer * part, 16), part)
        out_ref[:part, :] = (mine_ref[at, :] + other_ref[at, :].astype(F32)).astype(out_ref.dtype)
        at = pl.ds(pl.multiple_of(target * step + 2 * part, 16), 16)
        out_ref[part : part + 16, :] = (mine_ref[at, :] + other_ref[at, :].astype(F32)).astype(out_ref.dtype)
        out_ref[part + 16 :, :] = small.astype(out_ref.dtype)


def sum_kernel(own_ref, *refs):
    got, (total_ref, send_ref, rest_ref) = refs[:-3], refs[-3:]
    part = total_ref.shape[0]
    total = own_ref[...]
    for ref in got:
        total = total + ref[...].astype(F32)
    total_ref[...] = total[:part]
    send_ref[...] = total[:part].astype(BF16)
    rest_ref[...] = total[part:]


def small_kernel(rest_ref, embed_ref, w0_ref, act0_ref, msel_ref, spread_ref, conv0_ref, point0_ref, embed_out_ref, bt_ref):
    width = embed_ref.shape[1]
    g = rest_ref[16:, :]
    bt = jnp.concatenate([rest_ref[:16, q * CLASSES : (q + 1) * CLASSES] for q in range(3)])
    bt = bt.astype(BF16)
    stream = embed_ref[...].astype(F32)
    scale = norm_scale(stream)
    g16 = g.astype(BF16)
    ng = None
    for j in range(3):
        term = mm_nt(g16, w0_ref[j * width : (j + 1) * width, :])[4 * j : 4 * j + 4]
        ng = term if ng is None else ng + term
    inner = jnp.mean(ng * stream, axis=-1, keepdims=True)
    embed_out_ref[...] = scale * (ng - stream * (scale * scale * inner))
    bt_ref[...] = mm_nt(msel_ref[...], bt)
    conv0_ref[...] = mm(spread_ref[...], g16)
    point0_ref[...] = jnp.transpose(mm(bt, act0_ref[...]))


def finish_kernel(total_ref, got_ref, conv0_ref, point0_ref, conv_ref, point_ref):
    crow = conv_ref.shape[1]
    x = lax.axis_index("dp")
    conv_ref[0] = conv0_ref[...]
    point_ref[0] = point0_ref[...]
    own = total_ref[...]
    got = got_ref[...].astype(F32)
    first = jnp.where(x == 0, own, got)
    second = jnp.where(x == 0, got, own)
    conv_ref[1] = first[:crow]
    conv_ref[2] = second[:crow]
    point_ref[1] = jnp.transpose(first[crow:])
    point_ref[2] = jnp.transpose(second[crow:])


def call(kernel, outs, *args, scratch=(), limit=32, flops=0, name=None):
    moved = sum(v.size * v.dtype.itemsize for v in list(args) + list(outs))
    return pl.pallas_call(
        kernel,
        out_shape=outs,
        in_specs=[pl.BlockSpec(memory_space=pltpu.VMEM)] * len(args),
        out_specs=[pl.BlockSpec(memory_space=pltpu.VMEM)] * len(outs),
        scratch_shapes=list(scratch),
        compiler_params=pltpu.CompilerParams(vmem_limit_bytes=limit * 1024 * 1024),
        cost_estimate=pl.CostEstimate(flops=flops, bytes_accessed=moved, transcendentals=0),
        name=name,
    )(*args)


def on_device(bases, embed, conv_weight, point_weight, cotangent):
    n, dp = lax.axis_size("seq"), lax.axis_size("dp")
    rb, width, mid = bases.shape[1], embed.shape[1], conv_weight.shape[2]
    if n != 2 * STRIDE or dp != 2:
        return general(bases, embed, conv_weight, point_weight, cotangent)
    k = lax.axis_index("seq")
    zh, r = k // STRIDE, k % STRIDE
    rows = 2 * rb
    crow, prow = 3 * width // n, width // n
    part = crow + prow
    w = [conv_weight[i] for i in range(3)]
    p = [point_weight[i] for i in range(3)]
    shape = jax.ShapeDtypeStruct

    gathered = lax.all_to_all(jnp.broadcast_to(bases, (n, rb)), "seq", 0, 0, tiled=True)
    own = cotangent[0]
    far = lax.ppermute(own, "seq", [(s, (s + STRIDE) % n) for s in range(n)])
    cot = jnp.where(zh == 0, jnp.concatenate([own, far]), jnp.concatenate([far, own]))

    sel = selectors()
    act0, slope0, stab, sparts, ntab, u = call(
        table_kernel,
        [
            shape((CLASSES, mid), BF16),
            shape((CLASSES, mid), F32),
            shape((CLASSES, width), F32),
            shape((2 * CLASSES, width), BF16),
            shape((CLASSES, width), BF16),
            shape((6 * CLASSES, mid), BF16),
        ],
        embed, w[0], w[1], p[0], jnp.asarray(np.stack(sel), BF16),
        flops=4 * CLASSES * 3 * width * mid,
        name="tables",
    )

    cls = classes(gathered, rb // 8)
    rowidx = jnp.concatenate(
        [
            jnp.concatenate(
                [lax.dynamic_slice(cls, (a * STRIDE + r + 2 * j, 0), (1, rb)) for a in range(2)],
                axis=1,
            )
            for j in range(3)
        ]
    )
    selt = np.concatenate([v.T for v in sel] + [np.zeros((4, CLASSES))])
    total_rows = STRIDE // 2 * (2 * part + 16) + 16
    features, mine, other = call(
        lambda *refs: main_kernel(crow, prow, *refs),
        [shape((rb, width), F32), shape((total_rows, mid), F32), shape((total_rows, mid), BF16)],
        rowidx, rowidx.T, cot, w[1], w[2], p[0], p[1], p[2],
        act0, slope0, stab, sparts, ntab, u, jnp.asarray(selt, BF16),
        scratch=[
            pltpu.VMEM((rows, width), F32),
            pltpu.VMEM((rows, width), BF16),
            pltpu.VMEM((rows, mid), BF16),
            pltpu.VMEM((rows, mid), BF16),
            pltpu.VMEM((rows, mid), F32),
            pltpu.VMEM((rows, mid), F32),
            pltpu.VMEM((rows, mid), BF16),
            pltpu.VMEM((rows, width), BF16),
            pltpu.VMEM((2, STRIDE * crow, mid), F32),
            pltpu.VMEM((2, STRIDE * prow, mid), F32),
            pltpu.VMEM((width, CLASSES), F32),
        ],
        flops=8 * rows * 3 * width * mid,
        name="tower",
    )

    got = lax.ppermute(other, "seq", [(s, s ^ 1) for s in range(n)])
    peers = STRIDE // 2 * dp
    pieces = call(
        lambda *refs: message_kernel(part, *refs),
        [shape((part + 32, mid), F32 if i == 0 else BF16) for i in range(peers)],
        mine, got,
        name="messages",
    )
    arrived = []
    for mask in range(peers - 1, 0, -1):
        route = [
            (s * dp + d, (s ^ (2 * (mask // dp))) * dp + (d ^ (mask % dp)))
            for s in range(n)
            for d in range(dp)
        ]
        arrived.append(lax.ppermute(pieces[mask], ("seq", "dp"), route))
    total, send, rest = call(
        sum_kernel,
        [shape((part, mid), F32), shape((part, mid), BF16), shape((32, mid), F32)],
        pieces[0], *arrived,
        name="sums",
    )
    swapped = lax.ppermute(send, "dp", [(d, d ^ 1) for d in range(dp)])

    stream_e = embed.astype(F32)
    normed_e = (stream_e * norm_scale(stream_e)).astype(BF16)
    spread = jnp.concatenate(
        [jnp.pad(normed_e, ((4 * j, 12 - 4 * j), (0, 0))) for j in range(3)], axis=1
    )
    spread = lax.dynamic_slice_in_dim(spread, k * crow, crow, axis=1).T
    conv0, point0, embed_full, bt = call(
        small_kernel,
        [
            shape((crow, mid), F32),
            shape((mid, prow), F32),
            shape((4, width), F32),
            shape((4, prow), F32),
        ],
        rest, embed, w[0], act0, jnp.asarray(sel[1].T, BF16), spread,
        name="layer0",
    )
    embed_grad = bt + lax.dynamic_slice_in_dim(embed_full, k * prow, prow, axis=1)
    conv_grad, point_grad = call(
        finish_kernel,
        [shape((3, crow, mid), F32), shape((3, mid, prow), F32)],
        total, swapped, conv0, point0,
        name="finish",
    )
    return features[None], conv_grad, point_grad, embed_grad


def solution(mesh):
    in_specs = (P("dp", "seq"), P(), P(), P(), P("dp", "seq", None))
    out_specs = (P("dp", "seq", None), P(None, "seq", None), P(None, None, "seq"), P(None, "seq"))
    return jax.shard_map(
        on_device, mesh=mesh, in_specs=in_specs, out_specs=out_specs, check_vma=False
    )
```

```python
import math

import jax
import jax.numpy as jnp
import numpy as np
from jax import lax
from jax.experimental import pallas as pl
from jax.experimental.pallas import tpu as pltpu
from jax.sharding import PartitionSpec as P

BF16 = jnp.bfloat16
F32 = jnp.float32
CLASSES = 128
STRIDE = 8
LIMIT = 52


def gelu_pair(v):
    coef = math.sqrt(2.0 / math.pi)
    inner = coef * (v + 0.044715 * v * v * v)
    t = jnp.tanh(inner)
    slope = 0.5 * (1.0 + t) + 0.5 * v * (1.0 - t * t) * coef * (1.0 + 3.0 * 0.044715 * v * v)
    return 0.5 * v * (1.0 + t), slope


def mm(a, b):
    return jnp.dot(a, b, preferred_element_type=F32)


def mm_tn(a, b):
    return lax.dot_general(a, b, (((0,), (0,)), ((), ())), preferred_element_type=F32)


def mm_nt(a, b):
    return lax.dot_general(a, b, (((1,), (1,)), ((), ())), preferred_element_type=F32)


def halves(v):
    high = lax.reduce_precision(v, 8, 7)
    return high.astype(BF16), (v - high).astype(BF16)


def selectors():
    c = np.arange(CLASSES)
    digits = (c // 20, (c // 5) % 4, c % 5)
    valid = (c < 100)[:, None]
    return [((d[:, None] == np.arange(4)[None, :]) & valid).astype(np.float32) for d in digits]


def norm_scale(v):
    return lax.rsqrt(jnp.mean(v * v, axis=-1, keepdims=True) + 1e-06)


def tables(embed, conv_weight, point_weight):
    sel = [jnp.asarray(s, BF16) for s in selectors()]
    stream = embed.astype(F32)
    scale_e = norm_scale(stream)
    normed_e = (stream * scale_e).astype(BF16)
    taps = jnp.concatenate([mm(s, normed_e).astype(BF16) for s in sel], axis=1)
    act0, slope0 = gelu_pair(mm(taps, conv_weight[0]))
    act0 = act0.astype(BF16)
    stab = mm(sel[1], embed) + mm(act0, point_weight[0])
    scale1 = norm_scale(stab)
    ntab = (stab * scale1).astype(BF16)
    width = embed.shape[1]
    u = jnp.concatenate([mm(ntab, conv_weight[1, j * width : (j + 1) * width]) for j in range(3)])
    return stream, scale_e, normed_e, act0, slope0, stab, scale1, ntab, u


def classes(gathered, dil):
    n, rb = gathered.shape
    edge = jnp.full((1, dil), 4, jnp.int32)
    left = jnp.concatenate(
        [jnp.concatenate([edge, gathered[:-1, rb - dil :]]), gathered[:, : rb - dil]], axis=1
    )
    right = jnp.concatenate(
        [gathered[:, dil:], jnp.concatenate([gathered[1:, :dil], edge])], axis=1
    )
    cls = left * 20 + gathered * 5 + right
    none = jnp.full((2, rb), -1, jnp.int32)
    return jnp.concatenate([none, cls, none])


def general(bases, embed, conv_weight, point_weight, cotangent):
    n, dp = lax.axis_size("seq"), lax.axis_size("dp")
    rb, width, mid = bases.shape[1], embed.shape[1], conv_weight.shape[2]
    group = n // STRIDE
    k, x = lax.axis_index("seq"), lax.axis_index("dp")
    zh, r = k // STRIDE, k % STRIDE
    m, core = r // 2, r % 2
    rows = group * rb
    w1, w2 = conv_weight[1], conv_weight[2]
    p0, p1, p2 = point_weight[0], point_weight[1], point_weight[2]

    gathered = lax.all_to_all(jnp.broadcast_to(bases, (n, rb)), "seq", 0, 0, tiled=True)
    own = cotangent[0]
    parts = [own]
    for i in range(1, group):
        parts.append(lax.ppermute(own, "seq", [(s, (s - STRIDE * i) % n) for s in range(n)]))
    cot = lax.dynamic_slice_in_dim(
        jnp.concatenate(parts + parts), ((group - zh) % group) * rb, rows
    )

    stream_e, scale_e, normed_e, act0, slope0, stab, scale1, ntab, u = tables(
        embed, conv_weight, point_weight
    )
    u_high, u_low = halves(u)
    s_high, s_low = halves(stab)

    cls = classes(gathered, rb // 8)
    hots = []
    for j in range(3):
        index = jnp.concatenate(
            [lax.dynamic_slice(cls, (a * STRIDE + r + 2 * j, 0), (1, rb)) for a in range(group)],
            axis=1,
        )
        hots.append((jnp.arange(CLASSES, dtype=jnp.int32)[:, None] == index).astype(BF16))
    hot = jnp.concatenate(hots)

    pre1 = mm_tn(hot, u_high) + mm_tn(hot, u_low)
    act1, slope1 = gelu_pair(pre1)
    act1 = act1.astype(BF16)
    stream2 = mm_tn(hots[1], s_high) + mm_tn(hots[1], s_low) + mm(act1, p1)
    scale2 = norm_scale(stream2)
    normed2 = (stream2 * scale2).astype(BF16)
    nothing = jnp.zeros((rb, width), BF16)
    taps2 = jnp.concatenate(
        [
            jnp.concatenate([nothing, normed2[: rows - rb]]),
            normed2,
            jnp.concatenate([normed2[rb:], nothing]),
        ],
        axis=1,
    )
    pre2 = mm(taps2, w2)
    act2, slope2 = gelu_pair(pre2)
    act2 = act2.astype(BF16)
    features = lax.dynamic_slice_in_dim(stream2, zh * rb, rb) + mm(
        lax.dynamic_slice_in_dim(act2, zh * rb, rb), p2
    )

    grad2 = (mm_nt(cot, p2) * slope2).astype(BF16)
    nothing = jnp.zeros((rb, mid), BF16)
    above = jnp.concatenate([grad2[rb:], nothing])
    below = jnp.concatenate([nothing, grad2[: rows - rb]])
    ng2 = (
        mm_nt(above, w2[:width]) + mm_nt(grad2, w2[width : 2 * width]) + mm_nt(below, w2[2 * width :])
    )
    inner = jnp.mean(ng2 * stream2, axis=-1, keepdims=True)
    back2 = cot.astype(F32) + scale2 * (ng2 - stream2 * scale2 * scale2 * inner)
    back2 = back2.astype(BF16)
    grad1 = (mm_nt(back2, p1) * slope1).astype(BF16)

    h = mm(hot, grad1).astype(BF16)
    ng1 = sum(
        mm_nt(h[j * CLASSES : (j + 1) * CLASSES], w1[j * width : (j + 1) * width]) for j in range(3)
    )
    inner = jnp.mean(ng1 * stab, axis=-1, keepdims=True)
    b = mm(hots[1], back2) + scale1 * (ng1 - stab * scale1 * scale1 * inner)
    b16 = b.astype(BF16)
    s = (mm_nt(b16, p0) * slope0).astype(BF16)
    sel = selectors()
    g = mm(jnp.asarray(np.concatenate([v.T for v in sel]), BF16), s)
    bt = mm(jnp.asarray(sel[1].T, BF16), b16)
    small = jnp.concatenate([g, bt.reshape(2 * 4, mid)])

    crow, prow = 3 * width // n, width // n
    conv1 = jnp.concatenate(
        [mm_tn(ntab, h[j * CLASSES : (j + 1) * CLASSES]) for j in range(3)]
    )
    conv1 = lax.dynamic_slice_in_dim(conv1, zh * STRIDE * crow, STRIDE * crow)
    conv2 = mm_tn(lax.dynamic_slice_in_dim(taps2, zh * STRIDE * crow, STRIDE * crow, axis=1), grad2)

    def share(v):
        return lax.dynamic_slice_in_dim(v, zh * STRIDE * prow, STRIDE * prow, axis=1)

    point = [mm_tn(share(b16), act0), mm_tn(share(back2), act1), mm_tn(share(cot), act2)]
    tile = jnp.concatenate(
        [conv1.reshape(STRIDE, crow, mid), conv2.reshape(STRIDE, crow, mid)]
        + [v.reshape(STRIDE, prow, mid) for v in point],
        axis=1,
    )
    trow = 2 * crow + 3 * prow
    half = STRIDE // 2
    tile = tile.reshape(half, 2, trow, mid)

    swap = [(s, s ^ 1) for s in range(n)]
    mine = lax.dynamic_index_in_dim(tile, core, axis=1, keepdims=False)
    other = lax.dynamic_index_in_dim(tile, 1 - core, axis=1, keepdims=False)
    mine = mine + lax.ppermute(other.astype(BF16), "seq", swap).astype(F32)
    small = small + lax.ppermute(small.astype(BF16), "seq", swap).astype(F32)

    drow = trow // dp
    mine = mine.reshape(half, dp, drow, mid)
    small16 = small.astype(BF16)
    total = lax.dynamic_slice(mine, (m, x, 0, 0), (1, 1, drow, mid))[0, 0]
    for mask in range(half * dp - 1, 0, -1):
        mm_, mx = mask // dp, mask % dp
        piece = lax.dynamic_slice(mine, (m ^ mm_, x ^ mx, 0, 0), (1, 1, drow, mid))[0, 0]
        message = jnp.concatenate([piece.astype(BF16), small16])
        route = [
            (s * dp + d, (s ^ (2 * mm_)) * dp + (d ^ mx)) for s in range(n) for d in range(dp)
        ]
        got = lax.ppermute(message, ("seq", "dp"), route).astype(F32)
        total = total + got[:drow]
        small = small + got[drow:]

    total16 = total.astype(BF16)
    pieces = [total16] + [
        lax.ppermute(total16, "dp", [(d, d ^ i) for d in range(dp)]) for i in range(1, dp)
    ]
    full = jnp.concatenate(
        [
            sum(jnp.where((x ^ i) == d, pieces[i].astype(F32), 0.0) for i in range(dp))
            for d in range(dp)
        ]
    )

    g, bt = small[:12], small[12:].reshape(4, width)
    ng0 = sum(
        mm_nt(g[4 * j : 4 * j + 4].astype(BF16), conv_weight[0, j * width : (j + 1) * width])
        for j in range(3)
    )
    inner = jnp.mean(ng0 * stream_e, axis=-1, keepdims=True)
    embed_grad = bt + scale_e * (ng0 - stream_e * scale_e * scale_e * inner)
    embed_grad = lax.dynamic_slice_in_dim(embed_grad, k * prow, prow, axis=1)
    spread = jnp.concatenate(
        [
            jnp.pad(normed_e, ((4 * j, 8 - 4 * j), (0, 0))) for j in range(3)
        ],
        axis=1,
    )
    spread = lax.dynamic_slice_in_dim(spread, k * crow, crow, axis=1)
    conv0 = mm_tn(spread, g.astype(BF16))
    conv_grad = jnp.stack([conv0, full[:crow], full[crow : 2 * crow]])
    point_grad = full[2 * crow :].reshape(3, prow, mid).transpose(0, 2, 1)
    return features[None], conv_grad, point_grad, embed_grad


def normal(v):
    return (v * norm_scale(v)).astype(BF16)


def spread_kernel(bases_ref, out_ref):
    for i in range(out_ref.shape[0]):
        out_ref[i] = bases_ref[...]


def fetch(source, target, sem):
    copy = pltpu.make_async_copy(source, target, sem)
    copy.start()
    return copy


def fetch_taps(w_ref, layer, held_ref, sems, first, order=(0, 1, 2)):
    width = held_ref.shape[0] // 3
    copies = {}
    for j in order:
        at = pl.ds(j * width, width)
        copies[j] = fetch(w_ref.at[layer, at, :], held_ref.at[at, :], sems.at[first + j])
    return copies


def digits(shape, axis):
    c = lax.broadcasted_iota(jnp.int32, shape, axis).astype(F32)
    left, both = jnp.floor((c + 0.5) / 20.0), jnp.floor((c + 0.5) / 5.0)
    return c < 100.0, (left, both - 4.0 * left, c - 5.0 * both)


def digit_columns():
    valid, values = digits((CLASSES, 4), 0)
    base = lax.broadcasted_iota(jnp.int32, (CLASSES, 4), 1).astype(F32)
    return [jnp.where(valid & (v == base), 1.0, 0.0).astype(BF16) for v in values]


def digit_rows():
    valid, values = digits((16, CLASSES), 1)
    row = lax.broadcasted_iota(jnp.int32, (16, CLASSES), 0).astype(F32)
    hit = (values[0] == row) & (row < 4.0)
    hit |= (values[1] + 4.0 == row) & (row >= 4.0) & (row < 8.0)
    hit |= (values[2] + 8.0 == row) & (row >= 8.0) & (row < 12.0)
    return jnp.where(valid & hit, 1.0, 0.0).astype(BF16)


def table_kernel(embed_ref, w_ref, p_ref, act0_ref, table_ref, w0_ref, w1_ref, p0_ref, sems):
    width, mid = embed_ref.shape[1], act0_ref.shape[1]
    copy_w0 = fetch_taps(w_ref, 0, w0_ref, sems, 0)
    copy_p0 = fetch(p_ref.at[0], p0_ref, sems.at[6])
    copy_w1 = fetch_taps(w_ref, 1, w1_ref, sems, 3)
    normed_e = normal(embed_ref[...].astype(F32))
    sel = digit_columns()
    pre = None
    for j in range(3):
        taps = mm(sel[j], normed_e).astype(BF16)
        copy_w0[j].wait()
        term = mm(taps, w0_ref[j * width : (j + 1) * width, :])
        pre = term if pre is None else pre + term
    act0, slope0 = gelu_pair(pre)
    act0 = act0.astype(BF16)
    act0_ref[...] = act0
    copy_p0.wait()
    stab = mm(sel[1], embed_ref[...]) + mm(act0, p0_ref[...])
    table_ref[:, :width] = stab
    table_ref[:, width : width + mid] = slope0
    ntab = normal(stab)
    for j in range(3):
        copy_w1[j].wait()
        at = width + (j + 1) * mid
        table_ref[:, at : at + mid] = mm(ntab, w1_ref[j * width : (j + 1) * width, :])


def main_kernel(
    crow, prow, bases_ref, own_ref, far_ref, w_ref, p_ref, table_ref,
    features_ref, mine_ref, other_ref,
    hot_ref, stream_ref, normed_ref, act1_ref, act2_ref, slope1_ref, slope2_ref,
    cot_ref, grad_ref, back_ref, conv_ref, point_ref, bt_ref, ntab_ref, w1_ref, w2_ref, pt_ref, sems,
):
    n, _, rb = bases_ref.shape
    rows, width = stream_ref.shape
    mid = act1_ref.shape[1]
    dil, half = rb // 8, width // 2
    k = lax.axis_index("seq")
    zh, r, core = k // STRIDE, k % STRIDE, k % 2
    place = pl.ds(pl.multiple_of(zh * rb, 16), rb)
    far = pl.ds(pl.multiple_of((1 - zh) * rb, 16), rb)
    copy_p1 = fetch(p_ref.at[1], pt_ref.at[1], sems.at[7])
    copy_w2 = fetch_taps(w_ref, 2, w2_ref, sems, 3, (2, 0, 1))
    copy_p2 = fetch(p_ref.at[2], pt_ref.at[2], sems.at[8])
    copy_w1 = fetch_taps(w_ref, 1, w1_ref, sems, 0)
    copy_p0 = fetch(p_ref.at[0], pt_ref.at[0], sems.at[6])
    held = jnp.concatenate([bases_ref[i] for i in range(n)])
    held = (held - 4).astype(F32)
    edge = jnp.zeros((1, rb), F32)
    held = jnp.concatenate(
        [
            jnp.concatenate([edge, held[:-1]]).astype(BF16),
            held.astype(BF16),
            jnp.concatenate([held[1:], edge]).astype(BF16),
        ]
    )
    ahead = lax.broadcasted_iota(jnp.int32, (rb, rb), 0) - lax.broadcasted_iota(jnp.int32, (rb, rb), 1)

    def weight(gap):
        value = jnp.where(gap == -dil, 20.0, jnp.where(gap == 0, 5.0, jnp.where(gap == dil, 1.0, 0.0)))
        return value.astype(BF16)

    cls = (
        mm(held[:n], weight(ahead - rb)) + mm(held[n : 2 * n], weight(ahead)) + mm(held[2 * n :], weight(ahead + rb))
        + 105.0
    ).astype(BF16)
    block = lax.broadcasted_iota(jnp.int32, (n, CLASSES), 0)
    slot = lax.broadcasted_iota(jnp.int32, (n, CLASSES), 1)
    wanted = (slot // 3) * STRIDE + r + 2 * (slot % 3) - 2
    pick = jnp.where((block == wanted) & (slot < 6), 1.0, 0.0).astype(BF16)
    column = mm_tn(cls, pick)
    lanes = (lax.broadcasted_iota(jnp.int32, (rb, CLASSES), 1) + 1).astype(F32)
    for a in range(2):
        for j in range(3):
            i = 3 * a + j
            hot_ref[a * rb : (a + 1) * rb, j * CLASSES : (j + 1) * CLASSES] = jnp.where(
                lanes == column[:, i : i + 1], 1.0, 0.0
            ).astype(BF16)

    hot = hot_ref[...]
    mid_hot = hot[:, CLASSES : 2 * CLASSES]
    u = jnp.concatenate(
        [table_ref[:, width + (j + 1) * mid : width + (j + 2) * mid] for j in range(3)]
    )
    u_high = u.astype(BF16)
    act1, slope1 = gelu_pair(mm(hot, u_high) + mm(hot, (u - u_high.astype(F32)).astype(BF16)))
    act1 = act1.astype(BF16)
    act1_ref[...] = act1
    slope1_ref[...] = slope1
    stab = table_ref[:, :width]
    s_high = stab.astype(BF16)
    stream = mm(mid_hot, s_high) + mm(mid_hot, (stab - s_high.astype(F32)).astype(BF16))
    copy_p1.wait()
    stream = stream + mm(act1, pt_ref[1])
    stream_ref[...] = stream
    normed = normal(stream)
    normed_ref[...] = normed
    copy_w2[2].wait()
    copy_w2[0].wait()
    sides = jnp.concatenate(
        [mm(normed[rb:], w2_ref[2 * width :, :]), mm(normed[:rb], w2_ref[:width, :])]
    )
    copy_w2[1].wait()
    act2, slope2 = gelu_pair(mm(normed, w2_ref[width : 2 * width, :]) + sides)
    act2_ref[...] = act2.astype(BF16)
    slope2_ref[...] = slope2
    copy_p2.wait()
    features_ref[...] = stream_ref[place, :] + mm(act2_ref[place, :], pt_ref[2])

    cot_ref[place, :] = own_ref[...]
    cot_ref[far, :] = far_ref[...]
    grad2 = (mm_nt(cot_ref[...], pt_ref[2]) * slope2_ref[...]).astype(BF16)
    grad_ref[...] = grad2
    sides = jnp.concatenate(
        [mm_nt(grad2[rb:], w2_ref[:width, :]), mm_nt(grad2[:rb], w2_ref[2 * width :, :])]
    )
    ng = mm_nt(grad2, w2_ref[width : 2 * width, :]) + sides
    stream = stream_ref[...]
    scale = norm_scale(stream)
    inner = jnp.mean(ng * stream, axis=-1, keepdims=True)
    back = cot_ref[...].astype(F32) + scale * (ng - stream * (scale * scale * inner))
    back = back.astype(BF16)
    back_ref[...] = back
    grad1 = (mm_nt(back, pt_ref[1]) * slope1_ref[...]).astype(BF16)

    h = mm_tn(hot_ref[...], grad1).astype(BF16)
    h = [h[j * CLASSES : (j + 1) * CLASSES] for j in range(3)]
    ng = None
    for j in range(3):
        copy_w1[j].wait()
        term = mm_nt(h[j], w1_ref[j * width : (j + 1) * width, :])
        ng = term if ng is None else ng + term
    stab = table_ref[:, :width]
    scale = norm_scale(stab)
    ntab_ref[...] = (stab * scale).astype(BF16)
    inner = jnp.mean(ng * stab, axis=-1, keepdims=True)
    b = mm_tn(hot_ref[:, CLASSES : 2 * CLASSES], back) + scale * (ng - stab * (scale * scale * inner))
    copy_p0.wait()
    s = (mm_nt(b.astype(BF16), pt_ref[0]) * table_ref[:, width : width + mid]).astype(BF16)
    g = mm(digit_rows(), s)
    bt_ref[...] = jnp.transpose(b)

    columns = pl.ds(pl.multiple_of(zh * half, 128), half)
    side_at = pl.ds(pl.multiple_of(zh * half, 16), width)
    center_at = pl.ds(pl.multiple_of((1 - zh) * width, 16), half)
    conv_ref[0, side_at, :] = mm_tn(ntab_ref[...], jnp.where(zh == 0, h[0], h[2]))
    conv_ref[0, center_at, :] = mm_tn(ntab_ref[:, columns], h[1])
    conv_ref[1, side_at, :] = mm_tn(normed_ref[place, :], grad_ref[far, :])
    conv_ref[1, center_at, :] = mm_tn(normed_ref[:, columns], grad_ref[...])
    point_ref[0] = mm_tn(back_ref[:, columns], act1_ref[...])
    point_ref[1] = mm_tn(cot_ref[:, columns], act2_ref[...])
    part = crow + prow
    step = 2 * part + 16
    for target, side in ((mine_ref, core), (other_ref, 1 - core)):
        for m in range(STRIDE // 2):
            tile = 2 * m + side
            crows = pl.ds(pl.multiple_of(tile * crow, 16), crow)
            prows = pl.ds(pl.multiple_of(tile * prow, 16), prow)
            for layer in range(2):
                at = m * step + layer * part
                target[at : at + crow, :] = conv_ref[layer, crows, :].astype(target.dtype)
                target[at + crow : at + part, :] = point_ref[layer, prows, :].astype(target.dtype)
            at = m * step + 2 * part
            for q in range(3):
                brows = pl.ds(pl.multiple_of(zh * half + tile * prow + 16 * q, 16), 16)
                target[at : at + 16, q * CLASSES : (q + 1) * CLASSES] = bt_ref[brows, :].astype(target.dtype)
        at = STRIDE // 2 * step
        target[at : at + 16, :] = g.astype(target.dtype)


def message_kernel(part, mine_ref, other_ref, *out_refs):
    k, x = lax.axis_index("seq"), lax.axis_index("dp")
    m = (k % STRIDE) // 2
    step = 2 * part + 16
    end = STRIDE // 2 * step
    small = mine_ref[end : end + 16, :] + other_ref[end : end + 16, :].astype(F32)
    for mask, out_ref in enumerate(out_refs):
        target, layer = m ^ (mask // 2), x ^ (mask % 2)
        at = pl.ds(pl.multiple_of(target * step + layer * part, 16), part)
        out_ref[:part, :] = (mine_ref[at, :] + other_ref[at, :].astype(F32)).astype(out_ref.dtype)
        at = pl.ds(pl.multiple_of(target * step + 2 * part, 16), 16)
        out_ref[part : part + 16, :] = (mine_ref[at, :] + other_ref[at, :].astype(F32)).astype(out_ref.dtype)
        out_ref[part + 16 :, :] = small.astype(out_ref.dtype)


def sum_kernel(own_ref, *refs):
    got, (total_ref, send_ref, rest_ref) = refs[:-3], refs[-3:]
    part = total_ref.shape[0]
    total = own_ref[...]
    for ref in got:
        total = total + ref[...].astype(F32)
    total_ref[...] = total[:part]
    send_ref[...] = total[:part].astype(BF16)
    rest_ref[...] = total[part:]


def small_kernel(rest_ref, embed_ref, w_ref, act0_ref, spread_ref, conv0_ref, point0_ref, embed_out_ref, bt_ref, w0_ref, sems):
    copy_w0 = fetch_taps(w_ref, 0, w0_ref, sems, 0)
    width = embed_ref.shape[1]
    g = rest_ref[16:, :]
    bt = jnp.concatenate([rest_ref[:16, q * CLASSES : (q + 1) * CLASSES] for q in range(3)])
    bt = bt.astype(BF16)
    stream = embed_ref[...].astype(F32)
    scale = norm_scale(stream)
    g16 = g.astype(BF16)
    ng = None
    for j in range(3):
        copy_w0[j].wait()
        term = mm_nt(g16, w0_ref[j * width : (j + 1) * width, :])[4 * j : 4 * j + 4]
        ng = term if ng is None else ng + term
    inner = jnp.mean(ng * stream, axis=-1, keepdims=True)
    embed_out_ref[...] = scale * (ng - stream * (scale * scale * inner))
    bt_ref[...] = mm_nt(digit_rows(), bt)[4:8]
    conv0_ref[...] = mm(spread_ref[...], g16)
    point0_ref[...] = mm(bt, act0_ref[...])


def finish_kernel(total_ref, got_ref, conv0_ref, point0_ref, conv_ref, point_ref):
    crow = conv_ref.shape[1]
    x = lax.axis_index("dp")
    conv_ref[0] = conv0_ref[...]
    point_ref[0] = point0_ref[...]
    own = total_ref[...]
    got = got_ref[...].astype(F32)
    first = jnp.where(x == 0, own, got)
    second = jnp.where(x == 0, got, own)
    conv_ref[1] = first[:crow]
    conv_ref[2] = second[:crow]
    point_ref[1] = first[crow:]
    point_ref[2] = second[crow:]


def call(kernel, outs, *args, far=(), scratch=(), flops=0, name=None):
    moved = sum(v.size * v.dtype.itemsize for v in list(args) + list(outs))
    return pl.pallas_call(
        kernel,
        out_shape=outs,
        in_specs=[
            pl.BlockSpec(memory_space=pl.ANY if i in far else pltpu.VMEM) for i in range(len(args))
        ],
        out_specs=[pl.BlockSpec(memory_space=pltpu.VMEM)] * len(outs),
        scratch_shapes=list(scratch),
        compiler_params=pltpu.CompilerParams(vmem_limit_bytes=(LIMIT if far else 24) * 1024 * 1024),
        cost_estimate=pl.CostEstimate(flops=flops, bytes_accessed=moved, transcendentals=0),
        name=name,
    )(*args)


def on_device(bases, embed, conv_weight, point_weight, cotangent):
    n, dp = lax.axis_size("seq"), lax.axis_size("dp")
    rb, width, mid = bases.shape[1], embed.shape[1], conv_weight.shape[2]
    if n != 2 * STRIDE or dp != 2:
        return general(bases, embed, conv_weight, point_weight, cotangent)
    k = lax.axis_index("seq")
    zh, r = k // STRIDE, k % STRIDE
    rows = 2 * rb
    crow, prow = 3 * width // n, width // n
    part = crow + prow
    shape = jax.ShapeDtypeStruct

    own = cotangent[0]
    far = lax.ppermute(own, "seq", [(s, (s + STRIDE) % n) for s in range(n)])
    (copies,) = call(spread_kernel, [shape((n, 1, rb), jnp.int32)], bases, name="spread")
    gathered = lax.all_to_all(copies, "seq", 0, 0, tiled=True)

    taps = pltpu.VMEM((3 * width, mid), BF16)
    act0, table = call(
        table_kernel,
        [shape((CLASSES, mid), BF16), shape((CLASSES, width + 4 * mid), F32)],
        embed, conv_weight, point_weight,
        far=(1, 2),
        scratch=[taps, taps, pltpu.VMEM((mid, width), BF16), pltpu.SemaphoreType.DMA((7,))],
        flops=4 * CLASSES * 3 * width * mid,
        name="tables",
    )
    total_rows = STRIDE // 2 * (2 * part + 16) + 16
    features, mine, other = call(
        lambda *refs: main_kernel(crow, prow, *refs),
        [shape((rb, width), F32), shape((total_rows, mid), F32), shape((total_rows, mid), BF16)],
        gathered, own, far, conv_weight, point_weight, table,
        far=(3, 4),
        scratch=[
            pltpu.VMEM((rows, 3 * CLASSES), BF16),
            pltpu.VMEM((rows, width), F32),
            pltpu.VMEM((rows, width), BF16),
            pltpu.VMEM((rows, mid), BF16),
            pltpu.VMEM((rows, mid), BF16),
            pltpu.VMEM((rows, mid), F32),
            pltpu.VMEM((rows, mid), F32),
            pltpu.VMEM((rows, width), BF16),
            pltpu.VMEM((rows, mid), BF16),
            pltpu.VMEM((rows, width), BF16),
            pltpu.VMEM((2, STRIDE * crow, mid), F32),
            pltpu.VMEM((2, STRIDE * prow, mid), F32),
            pltpu.VMEM((width, CLASSES), F32),
            pltpu.VMEM((CLASSES, width), BF16),
            taps,
            taps,
            pltpu.VMEM((3, mid, width), BF16),
            pltpu.SemaphoreType.DMA((9,)),
        ],
        flops=9 * rows * 3 * width * mid,
        name="tower",
    )

    got = lax.ppermute(other, "seq", [(s, s ^ 1) for s in range(n)])
    peers = STRIDE // 2 * dp
    pieces = call(
        lambda *refs: message_kernel(part, *refs),
        [shape((part + 32, mid), F32 if i == 0 else BF16) for i in range(peers)],
        mine, got,
        name="messages",
    )
    arrived = []
    for mask in range(peers - 1, 0, -1):
        route = [
            (s * dp + d, (s ^ (2 * (mask // dp))) * dp + (d ^ (mask % dp)))
            for s in range(n)
            for d in range(dp)
        ]
        arrived.append(lax.ppermute(pieces[mask], ("seq", "dp"), route))
    total, send, rest = call(
        sum_kernel,
        [shape((part, mid), F32), shape((part, mid), BF16), shape((32, mid), F32)],
        pieces[0], *arrived,
        name="sums",
    )
    swapped = lax.ppermute(send, "dp", [(d, d ^ 1) for d in range(dp)])

    stream_e = embed.astype(F32)
    normed_e = (stream_e * norm_scale(stream_e)).astype(BF16)
    spread = jnp.concatenate(
        [jnp.pad(normed_e, ((4 * j, 12 - 4 * j), (0, 0))) for j in range(3)], axis=1
    )
    spread = lax.dynamic_slice_in_dim(spread, k * crow, crow, axis=1).T
    conv0, point0, embed_full, bt = call(
        small_kernel,
        [
            shape((crow, mid), F32),
            shape((prow, mid), F32),
            shape((4, width), F32),
            shape((4, prow), F32),
        ],
        rest, embed, conv_weight, act0, spread,
        far=(2,),
        scratch=[taps, pltpu.SemaphoreType.DMA((3,))],
        name="layer0",
    )
    embed_grad = bt + lax.dynamic_slice_in_dim(embed_full, k * prow, prow, axis=1)
    conv_grad, point_grad = call(
        finish_kernel,
        [shape((3, crow, mid), F32), shape((3, prow, mid), F32)],
        total, swapped, conv0, point0,
        name="finish",
    )
    return features[None], conv_grad, point_grad.transpose(0, 2, 1), embed_grad


def solution(mesh):
    in_specs = (P("dp", "seq"), P(), P(), P(), P("dp", "seq", None))
    out_specs = (P("dp", "seq", None), P(None, "seq", None), P(None, None, "seq"), P(None, "seq"))
    return jax.shard_map(
        on_device, mesh=mesh, in_specs=in_specs, out_specs=out_specs, check_vma=False
    )
```

```python
import math

import jax
import jax.numpy as jnp
import numpy as np
from jax import lax
from jax.experimental import pallas as pl
from jax.experimental.pallas import tpu as pltpu
from jax.sharding import PartitionSpec as P

BF16 = jnp.bfloat16
F32 = jnp.float32
CLASSES = 128
STRIDE = 8


def gelu_pair(v):
    coef = math.sqrt(2.0 / math.pi)
    inner = coef * (v + 0.044715 * v * v * v)
    t = jnp.tanh(inner)
    slope = 0.5 * (1.0 + t) + 0.5 * v * (1.0 - t * t) * coef * (1.0 + 3.0 * 0.044715 * v * v)
    return 0.5 * v * (1.0 + t), slope


def mm(a, b):
    return jnp.dot(a, b, preferred_element_type=F32)


def mm_tn(a, b):
    return lax.dot_general(a, b, (((0,), (0,)), ((), ())), preferred_element_type=F32)


def mm_nt(a, b):
    return lax.dot_general(a, b, (((1,), (1,)), ((), ())), preferred_element_type=F32)


def halves(v):
    high = lax.reduce_precision(v, 8, 7)
    return high.astype(BF16), (v - high).astype(BF16)


def selectors():
    c = np.arange(CLASSES)
    digits = (c // 20, (c // 5) % 4, c % 5)
    valid = (c < 100)[:, None]
    return [((d[:, None] == np.arange(4)[None, :]) & valid).astype(np.float32) for d in digits]


def norm_scale(v):
    return lax.rsqrt(jnp.mean(v * v, axis=-1, keepdims=True) + 1e-06)


def tables(embed, conv_weight, point_weight):
    sel = [jnp.asarray(s, BF16) for s in selectors()]
    stream = embed.astype(F32)
    scale_e = norm_scale(stream)
    normed_e = (stream * scale_e).astype(BF16)
    taps = jnp.concatenate([mm(s, normed_e).astype(BF16) for s in sel], axis=1)
    act0, slope0 = gelu_pair(mm(taps, conv_weight[0]))
    act0 = act0.astype(BF16)
    stab = mm(sel[1], embed) + mm(act0, point_weight[0])
    scale1 = norm_scale(stab)
    ntab = (stab * scale1).astype(BF16)
    width = embed.shape[1]
    u = jnp.concatenate([mm(ntab, conv_weight[1, j * width : (j + 1) * width]) for j in range(3)])
    return stream, scale_e, normed_e, act0, slope0, stab, scale1, ntab, u


def classes(gathered, dil):
    n, rb = gathered.shape
    edge = jnp.full((1, dil), 4, jnp.int32)
    left = jnp.concatenate(
        [jnp.concatenate([edge, gathered[:-1, rb - dil :]]), gathered[:, : rb - dil]], axis=1
    )
    right = jnp.concatenate(
        [gathered[:, dil:], jnp.concatenate([gathered[1:, :dil], edge])], axis=1
    )
    cls = left * 20 + gathered * 5 + right
    none = jnp.full((2, rb), -1, jnp.int32)
    return jnp.concatenate([none, cls, none])


def general(bases, embed, conv_weight, point_weight, cotangent):
    n, dp = lax.axis_size("seq"), lax.axis_size("dp")
    rb, width, mid = bases.shape[1], embed.shape[1], conv_weight.shape[2]
    group = n // STRIDE
    k, x = lax.axis_index("seq"), lax.axis_index("dp")
    zh, r = k // STRIDE, k % STRIDE
    m, core = r // 2, r % 2
    rows = group * rb
    w1, w2 = conv_weight[1], conv_weight[2]
    p0, p1, p2 = point_weight[0], point_weight[1], point_weight[2]

    gathered = lax.all_to_all(jnp.broadcast_to(bases, (n, rb)), "seq", 0, 0, tiled=True)
    own = cotangent[0]
    parts = [own]
    for i in range(1, group):
        parts.append(lax.ppermute(own, "seq", [(s, (s - STRIDE * i) % n) for s in range(n)]))
    cot = lax.dynamic_slice_in_dim(
        jnp.concatenate(parts + parts), ((group - zh) % group) * rb, rows
    )

    stream_e, scale_e, normed_e, act0, slope0, stab, scale1, ntab, u = tables(
        embed, conv_weight, point_weight
    )
    u_high, u_low = halves(u)
    s_high, s_low = halves(stab)

    cls = classes(gathered, rb // 8)
    hots = []
    for j in range(3):
        index = jnp.concatenate(
            [lax.dynamic_slice(cls, (a * STRIDE + r + 2 * j, 0), (1, rb)) for a in range(group)],
            axis=1,
        )
        hots.append((jnp.arange(CLASSES, dtype=jnp.int32)[:, None] == index).astype(BF16))
    hot = jnp.concatenate(hots)

    pre1 = mm_tn(hot, u_high) + mm_tn(hot, u_low)
    act1, slope1 = gelu_pair(pre1)
    act1 = act1.astype(BF16)
    stream2 = mm_tn(hots[1], s_high) + mm_tn(hots[1], s_low) + mm(act1, p1)
    scale2 = norm_scale(stream2)
    normed2 = (stream2 * scale2).astype(BF16)
    nothing = jnp.zeros((rb, width), BF16)
    taps2 = jnp.concatenate(
        [
            jnp.concatenate([nothing, normed2[: rows - rb]]),
            normed2,
            jnp.concatenate([normed2[rb:], nothing]),
        ],
        axis=1,
    )
    pre2 = mm(taps2, w2)
    act2, slope2 = gelu_pair(pre2)
    act2 = act2.astype(BF16)
    features = lax.dynamic_slice_in_dim(stream2, zh * rb, rb) + mm(
        lax.dynamic_slice_in_dim(act2, zh * rb, rb), p2
    )

    grad2 = (mm_nt(cot, p2) * slope2).astype(BF16)
    nothing = jnp.zeros((rb, mid), BF16)
    above = jnp.concatenate([grad2[rb:], nothing])
    below = jnp.concatenate([nothing, grad2[: rows - rb]])
    ng2 = (
        mm_nt(above, w2[:width]) + mm_nt(grad2, w2[width : 2 * width]) + mm_nt(below, w2[2 * width :])
    )
    inner = jnp.mean(ng2 * stream2, axis=-1, keepdims=True)
    back2 = cot.astype(F32) + scale2 * (ng2 - stream2 * scale2 * scale2 * inner)
    back2 = back2.astype(BF16)
    grad1 = (mm_nt(back2, p1) * slope1).astype(BF16)

    h = mm(hot, grad1).astype(BF16)
    ng1 = sum(
        mm_nt(h[j * CLASSES : (j + 1) * CLASSES], w1[j * width : (j + 1) * width]) for j in range(3)
    )
    inner = jnp.mean(ng1 * stab, axis=-1, keepdims=True)
    b = mm(hots[1], back2) + scale1 * (ng1 - stab * scale1 * scale1 * inner)
    b16 = b.astype(BF16)
    s = (mm_nt(b16, p0) * slope0).astype(BF16)
    sel = selectors()
    g = mm(jnp.asarray(np.concatenate([v.T for v in sel]), BF16), s)
    bt = mm(jnp.asarray(sel[1].T, BF16), b16)
    small = jnp.concatenate([g, bt.reshape(2 * 4, mid)])

    crow, prow = 3 * width // n, width // n
    conv1 = jnp.concatenate(
        [mm_tn(ntab, h[j * CLASSES : (j + 1) * CLASSES]) for j in range(3)]
    )
    conv1 = lax.dynamic_slice_in_dim(conv1, zh * STRIDE * crow, STRIDE * crow)
    conv2 = mm_tn(lax.dynamic_slice_in_dim(taps2, zh * STRIDE * crow, STRIDE * crow, axis=1), grad2)

    def share(v):
        return lax.dynamic_slice_in_dim(v, zh * STRIDE * prow, STRIDE * prow, axis=1)

    point = [mm_tn(share(b16), act0), mm_tn(share(back2), act1), mm_tn(share(cot), act2)]
    tile = jnp.concatenate(
        [conv1.reshape(STRIDE, crow, mid), conv2.reshape(STRIDE, crow, mid)]
        + [v.reshape(STRIDE, prow, mid) for v in point],
        axis=1,
    )
    trow = 2 * crow + 3 * prow
    half = STRIDE // 2
    tile = tile.reshape(half, 2, trow, mid)

    swap = [(s, s ^ 1) for s in range(n)]
    mine = lax.dynamic_index_in_dim(tile, core, axis=1, keepdims=False)
    other = lax.dynamic_index_in_dim(tile, 1 - core, axis=1, keepdims=False)
    mine = mine + lax.ppermute(other.astype(BF16), "seq", swap).astype(F32)
    small = small + lax.ppermute(small.astype(BF16), "seq", swap).astype(F32)

    drow = trow // dp
    mine = mine.reshape(half, dp, drow, mid)
    small16 = small.astype(BF16)
    total = lax.dynamic_slice(mine, (m, x, 0, 0), (1, 1, drow, mid))[0, 0]
    for mask in range(half * dp - 1, 0, -1):
        mm_, mx = mask // dp, mask % dp
        piece = lax.dynamic_slice(mine, (m ^ mm_, x ^ mx, 0, 0), (1, 1, drow, mid))[0, 0]
        message = jnp.concatenate([piece.astype(BF16), small16])
        route = [
            (s * dp + d, (s ^ (2 * mm_)) * dp + (d ^ mx)) for s in range(n) for d in range(dp)
        ]
        got = lax.ppermute(message, ("seq", "dp"), route).astype(F32)
        total = total + got[:drow]
        small = small + got[drow:]

    total16 = total.astype(BF16)
    pieces = [total16] + [
        lax.ppermute(total16, "dp", [(d, d ^ i) for d in range(dp)]) for i in range(1, dp)
    ]
    full = jnp.concatenate(
        [
            sum(jnp.where((x ^ i) == d, pieces[i].astype(F32), 0.0) for i in range(dp))
            for d in range(dp)
        ]
    )

    g, bt = small[:12], small[12:].reshape(4, width)
    ng0 = sum(
        mm_nt(g[4 * j : 4 * j + 4].astype(BF16), conv_weight[0, j * width : (j + 1) * width])
        for j in range(3)
    )
    inner = jnp.mean(ng0 * stream_e, axis=-1, keepdims=True)
    embed_grad = bt + scale_e * (ng0 - stream_e * scale_e * scale_e * inner)
    embed_grad = lax.dynamic_slice_in_dim(embed_grad, k * prow, prow, axis=1)
    spread = jnp.concatenate(
        [
            jnp.pad(normed_e, ((4 * j, 8 - 4 * j), (0, 0))) for j in range(3)
        ],
        axis=1,
    )
    spread = lax.dynamic_slice_in_dim(spread, k * crow, crow, axis=1)
    conv0 = mm_tn(spread, g.astype(BF16))
    conv_grad = jnp.stack([conv0, full[:crow], full[crow : 2 * crow]])
    point_grad = full[2 * crow :].reshape(3, prow, mid).transpose(0, 2, 1)
    return features[None], conv_grad, point_grad, embed_grad


def normal(v):
    return (v * norm_scale(v)).astype(BF16)


def spread_kernel(bases_ref, out_ref):
    for i in range(out_ref.shape[0]):
        out_ref[i] = bases_ref[...]


def fetch(source, target, sem):
    copy = pltpu.make_async_copy(source, target, sem)
    copy.start()
    return copy


def fetch_taps(w_ref, layer, held_ref, sems, first, order=(0, 1, 2)):
    width = held_ref.shape[0] // 3
    copies = {}
    for j in order:
        at = pl.ds(j * width, width)
        copies[j] = fetch(w_ref.at[layer, at, :], held_ref.at[at, :], sems.at[first + j])
    return copies


def digits(shape, axis):
    c = lax.broadcasted_iota(jnp.int32, shape, axis).astype(F32)
    left, both = jnp.floor((c + 0.5) / 20.0), jnp.floor((c + 0.5) / 5.0)
    return c < 100.0, (left, both - 4.0 * left, c - 5.0 * both)


def digit_columns():
    valid, values = digits((CLASSES, 4), 0)
    base = lax.broadcasted_iota(jnp.int32, (CLASSES, 4), 1).astype(F32)
    return [jnp.where(valid & (v == base), 1.0, 0.0).astype(BF16) for v in values]


def digit_rows():
    valid, values = digits((16, CLASSES), 1)
    row = lax.broadcasted_iota(jnp.int32, (16, CLASSES), 0).astype(F32)
    hit = (values[0] == row) & (row < 4.0)
    hit |= (values[1] + 4.0 == row) & (row >= 4.0) & (row < 8.0)
    hit |= (values[2] + 8.0 == row) & (row >= 8.0) & (row < 12.0)
    return jnp.where(valid & hit, 1.0, 0.0).astype(BF16)


def table_kernel(embed_ref, w_ref, p_ref, act0_ref, table_ref, w0_ref, w1_ref, p0_ref, sems):
    width, mid = embed_ref.shape[1], act0_ref.shape[1]
    copy_w0 = fetch_taps(w_ref, 0, w0_ref, sems, 0)
    copy_p0 = fetch(p_ref.at[0], p0_ref, sems.at[6])
    copy_w1 = fetch_taps(w_ref, 1, w1_ref, sems, 3)
    normed_e = normal(embed_ref[...].astype(F32))
    sel = digit_columns()
    pre = None
    for j in range(3):
        taps = mm(sel[j], normed_e).astype(BF16)
        copy_w0[j].wait()
        term = mm(taps, w0_ref[j * width : (j + 1) * width, :])
        pre = term if pre is None else pre + term
    act0, slope0 = gelu_pair(pre)
    act0 = act0.astype(BF16)
    act0_ref[...] = act0
    copy_p0.wait()
    stab = mm(sel[1], embed_ref[...]) + mm(act0, p0_ref[...])
    table_ref[:, :width] = stab
    table_ref[:, width : width + mid] = slope0
    ntab = normal(stab)
    for j in range(3):
        copy_w1[j].wait()
        at = width + (j + 1) * mid
        table_ref[:, at : at + mid] = mm(ntab, w1_ref[j * width : (j + 1) * width, :])


def main_kernel(
    crow, prow, bases_ref, own_ref, far_ref, w_ref, p_ref, table_ref,
    features_ref, mine_ref, other_ref,
    hot_ref, stream_ref, normed_ref, act1_ref, act2_ref, slope1_ref, slope2_ref,
    cot_ref, grad_ref, back_ref, conv_ref, point_ref, bt_ref, ntab_ref, w1_ref, w2_ref, pt_ref, sent_ref, sems,
):
    n, _, rb = bases_ref.shape
    rows, width = stream_ref.shape
    mid = act1_ref.shape[1]
    dil, half = rb // 8, width // 2
    k = lax.axis_index("seq")
    zh, r, core = k // STRIDE, k % STRIDE, k % 2
    place = pl.ds(pl.multiple_of(zh * rb, 16), rb)
    far = pl.ds(pl.multiple_of((1 - zh) * rb, 16), rb)
    copy_p1 = fetch(p_ref.at[1], pt_ref.at[1], sems.at[7])
    copy_w2 = fetch_taps(w_ref, 2, w2_ref, sems, 3, (2, 0, 1))
    copy_p2 = fetch(p_ref.at[2], pt_ref.at[2], sems.at[8])
    copy_w1 = fetch_taps(w_ref, 1, w1_ref, sems, 0)
    copy_p0 = fetch(p_ref.at[0], pt_ref.at[0], sems.at[6])
    held = jnp.concatenate([bases_ref[i] for i in range(n)])
    held = (held - 4).astype(F32)
    edge = jnp.zeros((1, rb), F32)
    held = jnp.concatenate(
        [
            jnp.concatenate([edge, held[:-1]]).astype(BF16),
            held.astype(BF16),
            jnp.concatenate([held[1:], edge]).astype(BF16),
        ]
    )
    ahead = lax.broadcasted_iota(jnp.int32, (rb, rb), 0) - lax.broadcasted_iota(jnp.int32, (rb, rb), 1)

    def weight(gap):
        value = jnp.where(gap == -dil, 20.0, jnp.where(gap == 0, 5.0, jnp.where(gap == dil, 1.0, 0.0)))
        return value.astype(BF16)

    cls = (
        mm(held[:n], weight(ahead - rb)) + mm(held[n : 2 * n], weight(ahead)) + mm(held[2 * n :], weight(ahead + rb))
        + 105.0
    ).astype(BF16)
    block = lax.broadcasted_iota(jnp.int32, (n, CLASSES), 0)
    slot = lax.broadcasted_iota(jnp.int32, (n, CLASSES), 1)
    wanted = (slot // 3) * STRIDE + r + 2 * (slot % 3) - 2
    pick = jnp.where((block == wanted) & (slot < 6), 1.0, 0.0).astype(BF16)
    column = mm_tn(cls, pick)
    lanes = (lax.broadcasted_iota(jnp.int32, (rb, CLASSES), 1) + 1).astype(F32)
    for a in range(2):
        for j in range(3):
            i = 3 * a + j
            hot_ref[a * rb : (a + 1) * rb, j * CLASSES : (j + 1) * CLASSES] = jnp.where(
                lanes == column[:, i : i + 1], 1.0, 0.0
            ).astype(BF16)

    hot = hot_ref[...]
    mid_hot = hot[:, CLASSES : 2 * CLASSES]
    u = jnp.concatenate(
        [table_ref[:, width + (j + 1) * mid : width + (j + 2) * mid] for j in range(3)]
    )
    u_high = u.astype(BF16)
    act1, slope1 = gelu_pair(mm(hot, u_high) + mm(hot, (u - u_high.astype(F32)).astype(BF16)))
    act1 = act1.astype(BF16)
    act1_ref[...] = act1
    slope1_ref[...] = slope1
    stab = table_ref[:, :width]
    s_high = stab.astype(BF16)
    stream = mm(mid_hot, s_high) + mm(mid_hot, (stab - s_high.astype(F32)).astype(BF16))
    copy_p1.wait()
    stream = stream + mm(act1, pt_ref[1])
    stream_ref[...] = stream
    normed = normal(stream)
    normed_ref[...] = normed
    copy_w2[2].wait()
    copy_w2[0].wait()
    sides = jnp.concatenate(
        [mm(normed[rb:], w2_ref[2 * width :, :]), mm(normed[:rb], w2_ref[:width, :])]
    )
    copy_w2[1].wait()
    act2, slope2 = gelu_pair(mm(normed, w2_ref[width : 2 * width, :]) + sides)
    act2_ref[...] = act2.astype(BF16)
    slope2_ref[...] = slope2
    copy_p2.wait()
    sent_ref[...] = stream_ref[place, :] + mm(act2_ref[place, :], pt_ref[2])
    copy_features = fetch(sent_ref, features_ref, sems.at[9])

    cot_ref[place, :] = own_ref[...]
    cot_ref[far, :] = far_ref[...]
    grad2 = (mm_nt(cot_ref[...], pt_ref[2]) * slope2_ref[...]).astype(BF16)
    grad_ref[...] = grad2
    sides = jnp.concatenate(
        [mm_nt(grad2[rb:], w2_ref[:width, :]), mm_nt(grad2[:rb], w2_ref[2 * width :, :])]
    )
    ng = mm_nt(grad2, w2_ref[width : 2 * width, :]) + sides
    stream = stream_ref[...]
    scale = norm_scale(stream)
    inner = jnp.mean(ng * stream, axis=-1, keepdims=True)
    back = cot_ref[...].astype(F32) + scale * (ng - stream * (scale * scale * inner))
    back = back.astype(BF16)
    back_ref[...] = back
    grad1 = (mm_nt(back, pt_ref[1]) * slope1_ref[...]).astype(BF16)

    h = mm_tn(hot_ref[...], grad1).astype(BF16)
    h = [h[j * CLASSES : (j + 1) * CLASSES] for j in range(3)]
    ng = None
    for j in range(3):
        copy_w1[j].wait()
        term = mm_nt(h[j], w1_ref[j * width : (j + 1) * width, :])
        ng = term if ng is None else ng + term
    stab = table_ref[:, :width]
    scale = norm_scale(stab)
    ntab_ref[...] = (stab * scale).astype(BF16)
    inner = jnp.mean(ng * stab, axis=-1, keepdims=True)
    b = mm_tn(hot_ref[:, CLASSES : 2 * CLASSES], back) + scale * (ng - stab * (scale * scale * inner))
    copy_p0.wait()
    s = (mm_nt(b.astype(BF16), pt_ref[0]) * table_ref[:, width : width + mid]).astype(BF16)
    g = mm(digit_rows(), s)
    bt_ref[...] = jnp.transpose(b)

    columns = pl.ds(pl.multiple_of(zh * half, 128), half)
    side_at = pl.ds(pl.multiple_of(zh * half, 16), width)
    center_at = pl.ds(pl.multiple_of((1 - zh) * width, 16), half)
    conv_ref[0, side_at, :] = mm_tn(ntab_ref[...], jnp.where(zh == 0, h[0], h[2]))
    conv_ref[0, center_at, :] = mm_tn(ntab_ref[:, columns], h[1])
    conv_ref[1, side_at, :] = mm_tn(normed_ref[place, :], grad_ref[far, :])
    conv_ref[1, center_at, :] = mm_tn(normed_ref[:, columns], grad_ref[...])
    point_ref[0] = mm_tn(back_ref[:, columns], act1_ref[...])
    point_ref[1] = mm_tn(cot_ref[:, columns], act2_ref[...])
    part = crow + prow
    step = 2 * part + 16
    for target, side in ((mine_ref, core), (other_ref, 1 - core)):
        for m in range(STRIDE // 2):
            tile = 2 * m + side
            crows = pl.ds(pl.multiple_of(tile * crow, 16), crow)
            prows = pl.ds(pl.multiple_of(tile * prow, 16), prow)
            for layer in range(2):
                at = m * step + layer * part
                target[at : at + crow, :] = conv_ref[layer, crows, :].astype(target.dtype)
                target[at + crow : at + part, :] = point_ref[layer, prows, :].astype(target.dtype)
            at = m * step + 2 * part
            for q in range(3):
                brows = pl.ds(pl.multiple_of(zh * half + tile * prow + 16 * q, 16), 16)
                target[at : at + 16, q * CLASSES : (q + 1) * CLASSES] = bt_ref[brows, :].astype(target.dtype)
        at = STRIDE // 2 * step
        target[at : at + 16, :] = g.astype(target.dtype)
    copy_features.wait()


def message_kernel(part, mine_ref, other_ref, *out_refs):
    k, x = lax.axis_index("seq"), lax.axis_index("dp")
    m = (k % STRIDE) // 2
    step = 2 * part + 16
    end = STRIDE // 2 * step
    small = mine_ref[end : end + 16, :] + other_ref[end : end + 16, :].astype(F32)
    for mask, out_ref in enumerate(out_refs):
        target, layer = m ^ (mask // 2), x ^ (mask % 2)
        at = pl.ds(pl.multiple_of(target * step + layer * part, 16), part)
        out_ref[:part, :] = (mine_ref[at, :] + other_ref[at, :].astype(F32)).astype(out_ref.dtype)
        at = pl.ds(pl.multiple_of(target * step + 2 * part, 16), 16)
        out_ref[part : part + 16, :] = (mine_ref[at, :] + other_ref[at, :].astype(F32)).astype(out_ref.dtype)
        out_ref[part + 16 :, :] = small.astype(out_ref.dtype)


def sum_kernel(own_ref, *refs):
    got, (total_ref, send_ref, rest_ref) = refs[:-3], refs[-3:]
    part = total_ref.shape[0]
    total = own_ref[...]
    for ref in got:
        total = total + ref[...].astype(F32)
    total_ref[...] = total[:part]
    send_ref[...] = total[:part].astype(BF16)
    rest_ref[...] = total[part:]


def small_kernel(rest_ref, embed_ref, w_ref, act0_ref, spread_ref, conv0_ref, point0_ref, embed_out_ref, bt_ref, w0_ref, sems):
    copy_w0 = fetch_taps(w_ref, 0, w0_ref, sems, 0)
    width = embed_ref.shape[1]
    g = rest_ref[16:, :]
    bt = jnp.concatenate([rest_ref[:16, q * CLASSES : (q + 1) * CLASSES] for q in range(3)])
    bt = bt.astype(BF16)
    stream = embed_ref[...].astype(F32)
    scale = norm_scale(stream)
    g16 = g.astype(BF16)
    ng = None
    for j in range(3):
        copy_w0[j].wait()
        term = mm_nt(g16, w0_ref[j * width : (j + 1) * width, :])[4 * j : 4 * j + 4]
        ng = term if ng is None else ng + term
    inner = jnp.mean(ng * stream, axis=-1, keepdims=True)
    embed_out_ref[...] = scale * (ng - stream * (scale * scale * inner))
    bt_ref[...] = mm_nt(digit_rows(), bt)[4:8]
    conv0_ref[...] = mm(spread_ref[...], g16)
    point0_ref[...] = mm(bt, act0_ref[...])


def finish_kernel(total_ref, got_ref, conv0_ref, point0_ref, conv_ref, point_ref):
    crow = conv_ref.shape[1]
    x = lax.axis_index("dp")
    conv_ref[0] = conv0_ref[...]
    point_ref[0] = point0_ref[...]
    own = total_ref[...]
    got = got_ref[...].astype(F32)
    first = jnp.where(x == 0, own, got)
    second = jnp.where(x == 0, got, own)
    conv_ref[1] = first[:crow]
    conv_ref[2] = second[:crow]
    point_ref[1] = first[crow:]
    point_ref[2] = second[crow:]


def call(kernel, outs, *args, far=(), away=(), scratch=(), limit=24, flops=0, name=None):
    moved = sum(v.size * v.dtype.itemsize for v in list(args) + list(outs))
    return pl.pallas_call(
        kernel,
        out_shape=outs,
        in_specs=[
            pl.BlockSpec(memory_space=pl.ANY if i in far else pltpu.VMEM) for i in range(len(args))
        ],
        out_specs=[
            pl.BlockSpec(memory_space=pl.ANY if i in away else pltpu.VMEM) for i in range(len(outs))
        ],
        scratch_shapes=list(scratch),
        compiler_params=pltpu.CompilerParams(vmem_limit_bytes=limit * 1024 * 1024),
        cost_estimate=pl.CostEstimate(flops=flops, bytes_accessed=moved, transcendentals=0),
        name=name,
    )(*args)


def on_device(bases, embed, conv_weight, point_weight, cotangent):
    n, dp = lax.axis_size("seq"), lax.axis_size("dp")
    rb, width, mid = bases.shape[1], embed.shape[1], conv_weight.shape[2]
    if n != 2 * STRIDE or dp != 2:
        return general(bases, embed, conv_weight, point_weight, cotangent)
    k = lax.axis_index("seq")
    zh, r = k // STRIDE, k % STRIDE
    rows = 2 * rb
    crow, prow = 3 * width // n, width // n
    part = crow + prow
    shape = jax.ShapeDtypeStruct

    own = cotangent[0]
    far = lax.ppermute(own, "seq", [(s, (s + STRIDE) % n) for s in range(n)])
    (copies,) = call(spread_kernel, [shape((n, 1, rb), jnp.int32)], bases, name="spread")
    gathered = lax.all_to_all(copies, "seq", 0, 0, tiled=True)

    taps = pltpu.VMEM((3 * width, mid), BF16)
    act0, table = call(
        table_kernel,
        [shape((CLASSES, mid), BF16), shape((CLASSES, width + 4 * mid), F32)],
        embed, conv_weight, point_weight,
        far=(1, 2),
        scratch=[taps, taps, pltpu.VMEM((mid, width), BF16), pltpu.SemaphoreType.DMA((7,))],
        limit=52,
        flops=4 * CLASSES * 3 * width * mid,
        name="tables",
    )
    total_rows = STRIDE // 2 * (2 * part + 16) + 16
    features, mine, other = call(
        lambda *refs: main_kernel(crow, prow, *refs),
        [shape((rb, width), F32), shape((total_rows, mid), F32), shape((total_rows, mid), BF16)],
        gathered, own, far, conv_weight, point_weight, table,
        far=(3, 4),
        scratch=[
            pltpu.VMEM((rows, 3 * CLASSES), BF16),
            pltpu.VMEM((rows, width), F32),
            pltpu.VMEM((rows, width), BF16),
            pltpu.VMEM((rows, mid), BF16),
            pltpu.VMEM((rows, mid), BF16),
            pltpu.VMEM((rows, mid), F32),
            pltpu.VMEM((rows, mid), F32),
            pltpu.VMEM((rows, width), BF16),
            pltpu.VMEM((rows, mid), BF16),
            pltpu.VMEM((rows, width), BF16),
            pltpu.VMEM((2, STRIDE * crow, mid), F32),
            pltpu.VMEM((2, STRIDE * prow, mid), F32),
            pltpu.VMEM((width, CLASSES), F32),
            pltpu.VMEM((CLASSES, width), BF16),
            taps,
            taps,
            pltpu.VMEM((3, mid, width), BF16),
            pltpu.VMEM((rb, width), F32),
            pltpu.SemaphoreType.DMA((10,)),
        ],
        away=(0,),
        limit=46,
        flops=9 * rows * 3 * width * mid,
        name="tower",
    )

    got = lax.ppermute(other, "seq", [(s, s ^ 1) for s in range(n)])
    peers = STRIDE // 2 * dp
    pieces = call(
        lambda *refs: message_kernel(part, *refs),
        [shape((part + 32, mid), F32 if i == 0 else BF16) for i in range(peers)],
        mine, got,
        name="messages",
    )
    arrived = []
    for mask in range(peers - 1, 0, -1):
        route = [
            (s * dp + d, (s ^ (2 * (mask // dp))) * dp + (d ^ (mask % dp)))
            for s in range(n)
            for d in range(dp)
        ]
        arrived.append(lax.ppermute(pieces[mask], ("seq", "dp"), route))
    total, send, rest = call(
        sum_kernel,
        [shape((part, mid), F32), shape((part, mid), BF16), shape((32, mid), F32)],
        pieces[0], *arrived,
        name="sums",
    )
    swapped = lax.ppermute(send, "dp", [(d, d ^ 1) for d in range(dp)])

    stream_e = embed.astype(F32)
    normed_e = (stream_e * norm_scale(stream_e)).astype(BF16)
    spread = jnp.concatenate(
        [jnp.pad(normed_e, ((4 * j, 12 - 4 * j), (0, 0))) for j in range(3)], axis=1
    )
    spread = lax.dynamic_slice_in_dim(spread, k * crow, crow, axis=1).T
    conv0, point0, embed_full, bt = call(
        small_kernel,
        [
            shape((crow, mid), F32),
            shape((prow, mid), F32),
            shape((4, width), F32),
            shape((4, prow), F32),
        ],
        rest, embed, conv_weight, act0, spread,
        far=(2,),
        scratch=[taps, pltpu.SemaphoreType.DMA((3,))],
        limit=52,
        name="layer0",
    )
    embed_grad = bt + lax.dynamic_slice_in_dim(embed_full, k * prow, prow, axis=1)
    conv_grad, point_grad = call(
        finish_kernel,
        [shape((3, crow, mid), F32), shape((3, prow, mid), F32)],
        total, swapped, conv0, point0,
        name="finish",
    )
    return features[None], conv_grad, point_grad.transpose(0, 2, 1), embed_grad


def solution(mesh):
    in_specs = (P("dp", "seq"), P(), P(), P(), P("dp", "seq", None))
    out_specs = (P("dp", "seq", None), P(None, "seq", None), P(None, None, "seq"), P(None, "seq"))
    return jax.shard_map(
        on_device, mesh=mesh, in_specs=in_specs, out_specs=out_specs, check_vma=False
    )
```

```python
import math

import jax
import jax.numpy as jnp
import numpy as np
from jax import lax
from jax.experimental import pallas as pl
from jax.experimental.pallas import tpu as pltpu
from jax.sharding import PartitionSpec as P

BF16 = jnp.bfloat16
F32 = jnp.float32
CLASSES = 128
STRIDE = 8
ORDER = (7, 6, 1, 5, 2, 3, 4)


def gelu_pair(v):
    coef = math.sqrt(2.0 / math.pi)
    inner = coef * (v + 0.044715 * v * v * v)
    t = jnp.tanh(inner)
    slope = 0.5 * (1.0 + t) + 0.5 * v * (1.0 - t * t) * coef * (1.0 + 3.0 * 0.044715 * v * v)
    return 0.5 * v * (1.0 + t), slope


def mm(a, b):
    return jnp.dot(a, b, preferred_element_type=F32)


def mm_tn(a, b):
    return lax.dot_general(a, b, (((0,), (0,)), ((), ())), preferred_element_type=F32)


def mm_nt(a, b):
    return lax.dot_general(a, b, (((1,), (1,)), ((), ())), preferred_element_type=F32)


def halves(v):
    high = lax.reduce_precision(v, 8, 7)
    return high.astype(BF16), (v - high).astype(BF16)


def selectors():
    c = np.arange(CLASSES)
    digits = (c // 20, (c // 5) % 4, c % 5)
    valid = (c < 100)[:, None]
    return [((d[:, None] == np.arange(4)[None, :]) & valid).astype(np.float32) for d in digits]


def norm_scale(v):
    return lax.rsqrt(jnp.mean(v * v, axis=-1, keepdims=True) + 1e-06)


def tables(embed, conv_weight, point_weight):
    sel = [jnp.asarray(s, BF16) for s in selectors()]
    stream = embed.astype(F32)
    scale_e = norm_scale(stream)
    normed_e = (stream * scale_e).astype(BF16)
    taps = jnp.concatenate([mm(s, normed_e).astype(BF16) for s in sel], axis=1)
    act0, slope0 = gelu_pair(mm(taps, conv_weight[0]))
    act0 = act0.astype(BF16)
    stab = mm(sel[1], embed) + mm(act0, point_weight[0])
    scale1 = norm_scale(stab)
    ntab = (stab * scale1).astype(BF16)
    width = embed.shape[1]
    u = jnp.concatenate([mm(ntab, conv_weight[1, j * width : (j + 1) * width]) for j in range(3)])
    return stream, scale_e, normed_e, act0, slope0, stab, scale1, ntab, u


def classes(gathered, dil):
    n, rb = gathered.shape
    edge = jnp.full((1, dil), 4, jnp.int32)
    left = jnp.concatenate(
        [jnp.concatenate([edge, gathered[:-1, rb - dil :]]), gathered[:, : rb - dil]], axis=1
    )
    right = jnp.concatenate(
        [gathered[:, dil:], jnp.concatenate([gathered[1:, :dil], edge])], axis=1
    )
    cls = left * 20 + gathered * 5 + right
    none = jnp.full((2, rb), -1, jnp.int32)
    return jnp.concatenate([none, cls, none])


def general(bases, embed, conv_weight, point_weight, cotangent):
    n, dp = lax.axis_size("seq"), lax.axis_size("dp")
    rb, width, mid = bases.shape[1], embed.shape[1], conv_weight.shape[2]
    group = n // STRIDE
    k, x = lax.axis_index("seq"), lax.axis_index("dp")
    zh, r = k // STRIDE, k % STRIDE
    m, core = r // 2, r % 2
    rows = group * rb
    w1, w2 = conv_weight[1], conv_weight[2]
    p0, p1, p2 = point_weight[0], point_weight[1], point_weight[2]

    gathered = lax.all_to_all(jnp.broadcast_to(bases, (n, rb)), "seq", 0, 0, tiled=True)
    own = cotangent[0]
    parts = [own]
    for i in range(1, group):
        parts.append(lax.ppermute(own, "seq", [(s, (s - STRIDE * i) % n) for s in range(n)]))
    cot = lax.dynamic_slice_in_dim(
        jnp.concatenate(parts + parts), ((group - zh) % group) * rb, rows
    )

    stream_e, scale_e, normed_e, act0, slope0, stab, scale1, ntab, u = tables(
        embed, conv_weight, point_weight
    )
    u_high, u_low = halves(u)
    s_high, s_low = halves(stab)

    cls = classes(gathered, rb // 8)
    hots = []
    for j in range(3):
        index = jnp.concatenate(
            [lax.dynamic_slice(cls, (a * STRIDE + r + 2 * j, 0), (1, rb)) for a in range(group)],
            axis=1,
        )
        hots.append((jnp.arange(CLASSES, dtype=jnp.int32)[:, None] == index).astype(BF16))
    hot = jnp.concatenate(hots)

    pre1 = mm_tn(hot, u_high) + mm_tn(hot, u_low)
    act1, slope1 = gelu_pair(pre1)
    act1 = act1.astype(BF16)
    stream2 = mm_tn(hots[1], s_high) + mm_tn(hots[1], s_low) + mm(act1, p1)
    scale2 = norm_scale(stream2)
    normed2 = (stream2 * scale2).astype(BF16)
    nothing = jnp.zeros((rb, width), BF16)
    taps2 = jnp.concatenate(
        [
            jnp.concatenate([nothing, normed2[: rows - rb]]),
            normed2,
            jnp.concatenate([normed2[rb:], nothing]),
        ],
        axis=1,
    )
    pre2 = mm(taps2, w2)
    act2, slope2 = gelu_pair(pre2)
    act2 = act2.astype(BF16)
    features = lax.dynamic_slice_in_dim(stream2, zh * rb, rb) + mm(
        lax.dynamic_slice_in_dim(act2, zh * rb, rb), p2
    )

    grad2 = (mm_nt(cot, p2) * slope2).astype(BF16)
    nothing = jnp.zeros((rb, mid), BF16)
    above = jnp.concatenate([grad2[rb:], nothing])
    below = jnp.concatenate([nothing, grad2[: rows - rb]])
    ng2 = (
        mm_nt(above, w2[:width]) + mm_nt(grad2, w2[width : 2 * width]) + mm_nt(below, w2[2 * width :])
    )
    inner = jnp.mean(ng2 * stream2, axis=-1, keepdims=True)
    back2 = cot.astype(F32) + scale2 * (ng2 - stream2 * scale2 * scale2 * inner)
    back2 = back2.astype(BF16)
    grad1 = (mm_nt(back2, p1) * slope1).astype(BF16)

    h = mm(hot, grad1).astype(BF16)
    ng1 = sum(
        mm_nt(h[j * CLASSES : (j + 1) * CLASSES], w1[j * width : (j + 1) * width]) for j in range(3)
    )
    inner = jnp.mean(ng1 * stab, axis=-1, keepdims=True)
    b = mm(hots[1], back2) + scale1 * (ng1 - stab * scale1 * scale1 * inner)
    b16 = b.astype(BF16)
    s = (mm_nt(b16, p0) * slope0).astype(BF16)
    sel = selectors()
    g = mm(jnp.asarray(np.concatenate([v.T for v in sel]), BF16), s)
    bt = mm(jnp.asarray(sel[1].T, BF16), b16)
    small = jnp.concatenate([g, bt.reshape(2 * 4, mid)])

    crow, prow = 3 * width // n, width // n
    conv1 = jnp.concatenate(
        [mm_tn(ntab, h[j * CLASSES : (j + 1) * CLASSES]) for j in range(3)]
    )
    conv1 = lax.dynamic_slice_in_dim(conv1, zh * STRIDE * crow, STRIDE * crow)
    conv2 = mm_tn(lax.dynamic_slice_in_dim(taps2, zh * STRIDE * crow, STRIDE * crow, axis=1), grad2)

    def share(v):
        return lax.dynamic_slice_in_dim(v, zh * STRIDE * prow, STRIDE * prow, axis=1)

    point = [mm_tn(share(b16), act0), mm_tn(share(back2), act1), mm_tn(share(cot), act2)]
    tile = jnp.concatenate(
        [conv1.reshape(STRIDE, crow, mid), conv2.reshape(STRIDE, crow, mid)]
        + [v.reshape(STRIDE, prow, mid) for v in point],
        axis=1,
    )
    trow = 2 * crow + 3 * prow
    half = STRIDE // 2
    tile = tile.reshape(half, 2, trow, mid)

    swap = [(s, s ^ 1) for s in range(n)]
    mine = lax.dynamic_index_in_dim(tile, core, axis=1, keepdims=False)
    other = lax.dynamic_index_in_dim(tile, 1 - core, axis=1, keepdims=False)
    mine = mine + lax.ppermute(other.astype(BF16), "seq", swap).astype(F32)
    small = small + lax.ppermute(small.astype(BF16), "seq", swap).astype(F32)

    drow = trow // dp
    mine = mine.reshape(half, dp, drow, mid)
    small16 = small.astype(BF16)
    total = lax.dynamic_slice(mine, (m, x, 0, 0), (1, 1, drow, mid))[0, 0]
    for mask in range(half * dp - 1, 0, -1):
        mm_, mx = mask // dp, mask % dp
        piece = lax.dynamic_slice(mine, (m ^ mm_, x ^ mx, 0, 0), (1, 1, drow, mid))[0, 0]
        message = jnp.concatenate([piece.astype(BF16), small16])
        route = [
            (s * dp + d, (s ^ (2 * mm_)) * dp + (d ^ mx)) for s in range(n) for d in range(dp)
        ]
        got = lax.ppermute(message, ("seq", "dp"), route).astype(F32)
        total = total + got[:drow]
        small = small + got[drow:]

    total16 = total.astype(BF16)
    pieces = [total16] + [
        lax.ppermute(total16, "dp", [(d, d ^ i) for d in range(dp)]) for i in range(1, dp)
    ]
    full = jnp.concatenate(
        [
            sum(jnp.where((x ^ i) == d, pieces[i].astype(F32), 0.0) for i in range(dp))
            for d in range(dp)
        ]
    )

    g, bt = small[:12], small[12:].reshape(4, width)
    ng0 = sum(
        mm_nt(g[4 * j : 4 * j + 4].astype(BF16), conv_weight[0, j * width : (j + 1) * width])
        for j in range(3)
    )
    inner = jnp.mean(ng0 * stream_e, axis=-1, keepdims=True)
    embed_grad = bt + scale_e * (ng0 - stream_e * scale_e * scale_e * inner)
    embed_grad = lax.dynamic_slice_in_dim(embed_grad, k * prow, prow, axis=1)
    spread = jnp.concatenate(
        [
            jnp.pad(normed_e, ((4 * j, 8 - 4 * j), (0, 0))) for j in range(3)
        ],
        axis=1,
    )
    spread = lax.dynamic_slice_in_dim(spread, k * crow, crow, axis=1)
    conv0 = mm_tn(spread, g.astype(BF16))
    conv_grad = jnp.stack([conv0, full[:crow], full[crow : 2 * crow]])
    point_grad = full[2 * crow :].reshape(3, prow, mid).transpose(0, 2, 1)
    return features[None], conv_grad, point_grad, embed_grad


def normal(v):
    return (v * norm_scale(v)).astype(BF16)


def spread_kernel(bases_ref, out_ref):
    for i in range(out_ref.shape[0]):
        out_ref[i] = bases_ref[...]


def fetch(source, target, sem):
    copy = pltpu.make_async_copy(source, target, sem)
    copy.start()
    return copy


def fetch_taps(w_ref, layer, held_ref, sems, first, order=(0, 1, 2)):
    width = held_ref.shape[0] // 3
    copies = {}
    for j in order:
        at = pl.ds(j * width, width)
        copies[j] = fetch(w_ref.at[layer, at, :], held_ref.at[at, :], sems.at[first + j])
    return copies


def digits(shape, axis):
    c = lax.broadcasted_iota(jnp.int32, shape, axis).astype(F32)
    left, both = jnp.floor((c + 0.5) / 20.0), jnp.floor((c + 0.5) / 5.0)
    return c < 100.0, (left, both - 4.0 * left, c - 5.0 * both)


def digit_columns():
    valid, values = digits((CLASSES, 4), 0)
    base = lax.broadcasted_iota(jnp.int32, (CLASSES, 4), 1).astype(F32)
    return [jnp.where(valid & (v == base), 1.0, 0.0).astype(BF16) for v in values]


def digit_rows():
    valid, values = digits((16, CLASSES), 1)
    row = lax.broadcasted_iota(jnp.int32, (16, CLASSES), 0).astype(F32)
    hit = (values[0] == row) & (row < 4.0)
    hit |= (values[1] + 4.0 == row) & (row >= 4.0) & (row < 8.0)
    hit |= (values[2] + 8.0 == row) & (row >= 8.0) & (row < 12.0)
    return jnp.where(valid & hit, 1.0, 0.0).astype(BF16)


def table_kernel(embed_ref, w_ref, p_ref, act0_ref, table_ref, w2_ref, w0_ref, w1_ref, p0_ref, sems):
    width, mid = embed_ref.shape[1], act0_ref.shape[1]
    copy_w0 = fetch_taps(w_ref, 0, w0_ref, sems, 0)
    copy_p0 = fetch(p_ref.at[0], p0_ref, sems.at[6])
    copy_w1 = fetch_taps(w_ref, 1, w1_ref, sems, 3)
    copy_w2 = fetch(w_ref.at[2], w2_ref, sems.at[7])
    normed_e = normal(embed_ref[...].astype(F32))
    sel = digit_columns()
    pre = None
    for j in range(3):
        taps = mm(sel[j], normed_e).astype(BF16)
        copy_w0[j].wait()
        term = mm(taps, w0_ref[j * width : (j + 1) * width, :])
        pre = term if pre is None else pre + term
    act0, slope0 = gelu_pair(pre)
    act0 = act0.astype(BF16)
    act0_ref[...] = act0
    copy_p0.wait()
    stab = mm(sel[1], embed_ref[...]) + mm(act0, p0_ref[...])
    table_ref[:, :width] = stab
    table_ref[:, width : width + mid] = slope0
    ntab = normal(stab)
    for j in range(3):
        copy_w1[j].wait()
        at = width + (j + 1) * mid
        table_ref[:, at : at + mid] = mm(ntab, w1_ref[j * width : (j + 1) * width, :])
    copy_w2.wait()


def main_kernel(
    crow, prow, bases_ref, own_ref, far_ref, w_ref, p_ref, w2_ref, table_ref,
    features_ref, mine_ref, other_ref,
    hot_ref, stream_ref, normed_ref, act1_ref, act2_ref, slope1_ref, slope2_ref,
    cot_ref, grad_ref, back_ref, conv_ref, point_ref, bt_ref, ntab_ref, w1_ref, pt_ref, sent_ref, sems,
):
    n, _, rb = bases_ref.shape
    rows, width = stream_ref.shape
    mid = act1_ref.shape[1]
    dil, half = rb // 8, width // 2
    k = lax.axis_index("seq")
    zh, r, core = k // STRIDE, k % STRIDE, k % 2
    place = pl.ds(pl.multiple_of(zh * rb, 16), rb)
    far = pl.ds(pl.multiple_of((1 - zh) * rb, 16), rb)
    copy_p1 = fetch(p_ref.at[1], pt_ref.at[1], sems.at[7])
    copy_p2 = fetch(p_ref.at[2], pt_ref.at[2], sems.at[8])
    copy_w1 = fetch_taps(w_ref, 1, w1_ref, sems, 0)
    copy_p0 = fetch(p_ref.at[0], pt_ref.at[0], sems.at[6])
    held = jnp.concatenate([bases_ref[i] for i in range(n)])
    held = (held - 4).astype(F32)
    edge = jnp.zeros((1, rb), F32)
    held = jnp.concatenate(
        [
            jnp.concatenate([edge, held[:-1]]).astype(BF16),
            held.astype(BF16),
            jnp.concatenate([held[1:], edge]).astype(BF16),
        ]
    )
    ahead = lax.broadcasted_iota(jnp.int32, (rb, rb), 0) - lax.broadcasted_iota(jnp.int32, (rb, rb), 1)

    def weight(gap):
        value = jnp.where(gap == -dil, 20.0, jnp.where(gap == 0, 5.0, jnp.where(gap == dil, 1.0, 0.0)))
        return value.astype(BF16)

    cls = (
        mm(held[:n], weight(ahead - rb)) + mm(held[n : 2 * n], weight(ahead)) + mm(held[2 * n :], weight(ahead + rb))
        + 105.0
    ).astype(BF16)
    block = lax.broadcasted_iota(jnp.int32, (n, CLASSES), 0)
    slot = lax.broadcasted_iota(jnp.int32, (n, CLASSES), 1)
    wanted = (slot // 3) * STRIDE + r + 2 * (slot % 3) - 2
    pick = jnp.where((block == wanted) & (slot < 6), 1.0, 0.0).astype(BF16)
    column = mm_tn(cls, pick)
    lanes = (lax.broadcasted_iota(jnp.int32, (rb, CLASSES), 1) + 1).astype(F32)
    for a in range(2):
        for j in range(3):
            i = 3 * a + j
            hot_ref[a * rb : (a + 1) * rb, j * CLASSES : (j + 1) * CLASSES] = jnp.where(
                lanes == column[:, i : i + 1], 1.0, 0.0
            ).astype(BF16)

    hot = hot_ref[...]
    mid_hot = hot[:, CLASSES : 2 * CLASSES]
    u = jnp.concatenate(
        [table_ref[:, width + (j + 1) * mid : width + (j + 2) * mid] for j in range(3)]
    )
    u_high = u.astype(BF16)
    act1, slope1 = gelu_pair(mm(hot, u_high) + mm(hot, (u - u_high.astype(F32)).astype(BF16)))
    act1 = act1.astype(BF16)
    act1_ref[...] = act1
    slope1_ref[...] = slope1
    stab = table_ref[:, :width]
    s_high = stab.astype(BF16)
    stream = mm(mid_hot, s_high) + mm(mid_hot, (stab - s_high.astype(F32)).astype(BF16))
    copy_p1.wait()
    stream = stream + mm(act1, pt_ref[1])
    stream_ref[...] = stream
    normed = normal(stream)
    normed_ref[...] = normed
    sides = jnp.concatenate(
        [mm(normed[rb:], w2_ref[2 * width :, :]), mm(normed[:rb], w2_ref[:width, :])]
    )
    act2, slope2 = gelu_pair(mm(normed, w2_ref[width : 2 * width, :]) + sides)
    act2_ref[...] = act2.astype(BF16)
    slope2_ref[...] = slope2
    copy_p2.wait()
    sent_ref[...] = stream_ref[place, :] + mm(act2_ref[place, :], pt_ref[2])
    copy_features = fetch(sent_ref, features_ref, sems.at[9])

    cot_ref[place, :] = own_ref[...]
    cot_ref[far, :] = far_ref[...]
    grad2 = (mm_nt(cot_ref[...], pt_ref[2]) * slope2_ref[...]).astype(BF16)
    grad_ref[...] = grad2
    sides = jnp.concatenate(
        [mm_nt(grad2[rb:], w2_ref[:width, :]), mm_nt(grad2[:rb], w2_ref[2 * width :, :])]
    )
    ng = mm_nt(grad2, w2_ref[width : 2 * width, :]) + sides
    stream = stream_ref[...]
    scale = norm_scale(stream)
    inner = jnp.mean(ng * stream, axis=-1, keepdims=True)
    back = cot_ref[...].astype(F32) + scale * (ng - stream * (scale * scale * inner))
    back = back.astype(BF16)
    back_ref[...] = back
    grad1 = (mm_nt(back, pt_ref[1]) * slope1_ref[...]).astype(BF16)

    h = mm_tn(hot_ref[...], grad1).astype(BF16)
    h = [h[j * CLASSES : (j + 1) * CLASSES] for j in range(3)]
    ng = None
    for j in range(3):
        copy_w1[j].wait()
        term = mm_nt(h[j], w1_ref[j * width : (j + 1) * width, :])
        ng = term if ng is None else ng + term
    stab = table_ref[:, :width]
    scale = norm_scale(stab)
    ntab_ref[...] = (stab * scale).astype(BF16)
    inner = jnp.mean(ng * stab, axis=-1, keepdims=True)
    b = mm_tn(hot_ref[:, CLASSES : 2 * CLASSES], back) + scale * (ng - stab * (scale * scale * inner))
    copy_p0.wait()
    s = (mm_nt(b.astype(BF16), pt_ref[0]) * table_ref[:, width : width + mid]).astype(BF16)
    g = mm(digit_rows(), s)
    bt_ref[...] = jnp.transpose(b)

    columns = pl.ds(pl.multiple_of(zh * half, 128), half)
    side_at = pl.ds(pl.multiple_of(zh * half, 16), width)
    center_at = pl.ds(pl.multiple_of((1 - zh) * width, 16), half)
    conv_ref[0, side_at, :] = mm_tn(ntab_ref[...], jnp.where(zh == 0, h[0], h[2]))
    conv_ref[0, center_at, :] = mm_tn(ntab_ref[:, columns], h[1])
    conv_ref[1, side_at, :] = mm_tn(normed_ref[place, :], grad_ref[far, :])
    conv_ref[1, center_at, :] = mm_tn(normed_ref[:, columns], grad_ref[...])
    point_ref[0] = mm_tn(back_ref[:, columns], act1_ref[...])
    point_ref[1] = mm_tn(cot_ref[:, columns], act2_ref[...])
    part = crow + prow
    step = 2 * part + 16
    for target, side in ((mine_ref, core), (other_ref, 1 - core)):
        for m in range(STRIDE // 2):
            tile = 2 * m + side
            crows = pl.ds(pl.multiple_of(tile * crow, 16), crow)
            prows = pl.ds(pl.multiple_of(tile * prow, 16), prow)
            for layer in range(2):
                at = m * step + layer * part
                target[at : at + crow, :] = conv_ref[layer, crows, :].astype(target.dtype)
                target[at + crow : at + part, :] = point_ref[layer, prows, :].astype(target.dtype)
            at = m * step + 2 * part
            for q in range(3):
                brows = pl.ds(pl.multiple_of(zh * half + tile * prow + 16 * q, 16), 16)
                target[at : at + 16, q * CLASSES : (q + 1) * CLASSES] = bt_ref[brows, :].astype(target.dtype)
        at = STRIDE // 2 * step
        target[at : at + 16, :] = g.astype(target.dtype)
    copy_features.wait()


def message_kernel(part, mine_ref, other_ref, *out_refs):
    k, x = lax.axis_index("seq"), lax.axis_index("dp")
    m = (k % STRIDE) // 2
    step = 2 * part + 16
    end = STRIDE // 2 * step
    small = mine_ref[end : end + 16, :] + other_ref[end : end + 16, :].astype(F32)
    for mask, out_ref in enumerate(out_refs):
        target, layer = m ^ (mask // 2), x ^ (mask % 2)
        at = pl.ds(pl.multiple_of(target * step + layer * part, 16), part)
        out_ref[:part, :] = (mine_ref[at, :] + other_ref[at, :].astype(F32)).astype(out_ref.dtype)
        at = pl.ds(pl.multiple_of(target * step + 2 * part, 16), 16)
        out_ref[part : part + 16, :] = (mine_ref[at, :] + other_ref[at, :].astype(F32)).astype(out_ref.dtype)
        out_ref[part + 16 :, :] = small.astype(out_ref.dtype)


def sum_kernel(own_ref, *refs):
    got, (total_ref, send_ref, rest_ref) = refs[:-3], refs[-3:]
    part = total_ref.shape[0]
    total = own_ref[...]
    for ref in got:
        total = total + ref[...].astype(F32)
    total_ref[...] = total[:part]
    send_ref[...] = total[:part].astype(BF16)
    rest_ref[...] = total[part:]


def small_kernel(rest_ref, embed_ref, w_ref, act0_ref, spread_ref, conv0_ref, point0_ref, embed_out_ref, bt_ref, w0_ref, sems):
    copy_w0 = fetch_taps(w_ref, 0, w0_ref, sems, 0)
    width = embed_ref.shape[1]
    g = rest_ref[16:, :]
    bt = jnp.concatenate([rest_ref[:16, q * CLASSES : (q + 1) * CLASSES] for q in range(3)])
    bt = bt.astype(BF16)
    stream = embed_ref[...].astype(F32)
    scale = norm_scale(stream)
    g16 = g.astype(BF16)
    ng = None
    for j in range(3):
        copy_w0[j].wait()
        term = mm_nt(g16, w0_ref[j * width : (j + 1) * width, :])[4 * j : 4 * j + 4]
        ng = term if ng is None else ng + term
    inner = jnp.mean(ng * stream, axis=-1, keepdims=True)
    embed_out_ref[...] = scale * (ng - stream * (scale * scale * inner))
    bt_ref[...] = mm_nt(digit_rows(), bt)[4:8]
    conv0_ref[...] = mm(spread_ref[...], g16)
    point0_ref[...] = mm(bt, act0_ref[...])


def finish_kernel(total_ref, got_ref, conv0_ref, point0_ref, conv_ref, point_ref):
    crow = conv_ref.shape[1]
    x = lax.axis_index("dp")
    conv_ref[0] = conv0_ref[...]
    point_ref[0] = point0_ref[...]
    own = total_ref[...]
    got = got_ref[...].astype(F32)
    first = jnp.where(x == 0, own, got)
    second = jnp.where(x == 0, got, own)
    conv_ref[1] = first[:crow]
    conv_ref[2] = second[:crow]
    point_ref[1] = first[crow:]
    point_ref[2] = second[crow:]


def call(kernel, outs, *args, far=(), whole=(), away=(), scratch=(), limit=24, flops=0, name=None):
    args = [pltpu.with_memory_space_constraint(v, pltpu.HBM) if i in far else v for i, v in enumerate(args)]
    moved = sum(math.prod(v.shape) * jnp.dtype(v.dtype).itemsize for v in list(args) + list(outs))
    return pl.pallas_call(
        kernel,
        out_shape=outs,
        in_specs=[
            pl.BlockSpec(memory_space=pl.ANY if i in far and i not in whole else pltpu.VMEM)
            for i in range(len(args))
        ],
        out_specs=[
            pl.BlockSpec(memory_space=pl.ANY if i in away else pltpu.VMEM) for i in range(len(outs))
        ],
        scratch_shapes=list(scratch),
        compiler_params=pltpu.CompilerParams(vmem_limit_bytes=limit * 1024 * 1024),
        cost_estimate=pl.CostEstimate(flops=flops, bytes_accessed=moved, transcendentals=0),
        name=name,
    )(*args)


def on_device(bases, embed, conv_weight, point_weight, cotangent):
    n, dp = lax.axis_size("seq"), lax.axis_size("dp")
    rb, width, mid = bases.shape[1], embed.shape[1], conv_weight.shape[2]
    if n != 2 * STRIDE or dp != 2:
        return general(bases, embed, conv_weight, point_weight, cotangent)
    k = lax.axis_index("seq")
    zh, r = k // STRIDE, k % STRIDE
    rows = 2 * rb
    crow, prow = 3 * width // n, width // n
    part = crow + prow
    shape = jax.ShapeDtypeStruct

    own = cotangent[0]
    far = lax.ppermute(own, "seq", [(s, (s + STRIDE) % n) for s in range(n)])
    (copies,) = call(spread_kernel, [shape((n, 1, rb), jnp.int32)], bases, far=(0,), whole=(0,), name="spread")
    gathered = lax.all_to_all(copies, "seq", 0, 0, tiled=True)

    taps = pltpu.VMEM((3 * width, mid), BF16)
    act0, table, w2 = call(
        table_kernel,
        [
            shape((CLASSES, mid), BF16),
            pltpu.VMEM((CLASSES, width + 4 * mid), F32),
            pltpu.VMEM((3 * width, mid), BF16),
        ],
        embed, conv_weight, point_weight,
        far=(0, 1, 2),
        whole=(0,),
        scratch=[taps, taps, pltpu.VMEM((mid, width), BF16), pltpu.SemaphoreType.DMA((8,))],
        limit=20,
        flops=4 * CLASSES * 3 * width * mid,
        name="tables",
    )
    total_rows = STRIDE // 2 * (2 * part + 16) + 16
    features, mine, other = call(
        lambda *refs: main_kernel(crow, prow, *refs),
        [shape((rb, width), F32), shape((total_rows, mid), F32), shape((total_rows, mid), BF16)],
        gathered, own, far, conv_weight, point_weight, w2, table,
        far=(3, 4),
        scratch=[
            pltpu.VMEM((rows, 3 * CLASSES), BF16),
            pltpu.VMEM((rows, width), F32),
            pltpu.VMEM((rows, width), BF16),
            pltpu.VMEM((rows, mid), BF16),
            pltpu.VMEM((rows, mid), BF16),
            pltpu.VMEM((rows, mid), F32),
            pltpu.VMEM((rows, mid), F32),
            pltpu.VMEM((rows, width), BF16),
            pltpu.VMEM((rows, mid), BF16),
            pltpu.VMEM((rows, width), BF16),
            pltpu.VMEM((2, STRIDE * crow, mid), F32),
            pltpu.VMEM((2, STRIDE * prow, mid), F32),
            pltpu.VMEM((width, CLASSES), F32),
            pltpu.VMEM((CLASSES, width), BF16),
            taps,
            pltpu.VMEM((3, mid, width), BF16),
            pltpu.VMEM((rb, width), F32),
            pltpu.SemaphoreType.DMA((10,)),
        ],
        away=(0,),
        limit=24,
        flops=9 * rows * 3 * width * mid,
        name="tower",
    )

    got = lax.ppermute(other, "seq", [(s, s ^ 1) for s in range(n)])
    peers = STRIDE // 2 * dp
    pieces = call(
        lambda *refs: message_kernel(part, *refs),
        [shape((part + 32, mid), F32 if i == 0 else BF16) for i in range(peers)],
        mine, got,
        name="messages",
    )
    arrived = []
    for mask in ORDER:
        route = [
            (s * dp + d, (s ^ (2 * (mask // dp))) * dp + (d ^ (mask % dp)))
            for s in range(n)
            for d in range(dp)
        ]
        arrived.append(lax.ppermute(pieces[mask], ("seq", "dp"), route))
    total, send, rest = call(
        sum_kernel,
        [shape((part, mid), F32), shape((part, mid), BF16), shape((32, mid), F32)],
        pieces[0], *arrived,
        name="sums",
    )
    swapped = lax.ppermute(send, "dp", [(d, d ^ 1) for d in range(dp)])

    stream_e = embed.astype(F32)
    normed_e = (stream_e * norm_scale(stream_e)).astype(BF16)
    spread = jnp.concatenate(
        [jnp.pad(normed_e, ((4 * j, 12 - 4 * j), (0, 0))) for j in range(3)], axis=1
    )
    spread = lax.dynamic_slice_in_dim(spread, k * crow, crow, axis=1).T
    conv0, point0, embed_full, bt = call(
        small_kernel,
        [
            shape((crow, mid), F32),
            shape((prow, mid), F32),
            shape((4, width), F32),
            shape((4, prow), F32),
        ],
        rest, embed, conv_weight, act0, spread,
        far=(2,),
        scratch=[taps, pltpu.SemaphoreType.DMA((3,))],
        limit=24,
        name="layer0",
    )
    embed_grad = bt + lax.dynamic_slice_in_dim(embed_full, k * prow, prow, axis=1)
    conv_grad, point_grad = call(
        finish_kernel,
        [shape((3, crow, mid), F32), shape((3, prow, mid), F32)],
        total, swapped, conv0, point0,
        name="finish",
    )
    return features[None], conv_grad, point_grad.transpose(0, 2, 1), embed_grad


def solution(mesh):
    in_specs = (P("dp", "seq"), P(), P(), P(), P("dp", "seq", None))
    out_specs = (P("dp", "seq", None), P(None, "seq", None), P(None, None, "seq"), P(None, "seq"))
    return jax.shard_map(
        on_device, mesh=mesh, in_specs=in_specs, out_specs=out_specs, check_vma=False
    )
```

```python
import math

import jax
import jax.numpy as jnp
import numpy as np
from jax import lax
from jax.experimental import pallas as pl
from jax.experimental.pallas import tpu as pltpu
from jax.sharding import PartitionSpec as P

BF16 = jnp.bfloat16
F32 = jnp.float32
CLASSES = 128
STRIDE = 8
ORDER = (7, 6, 1, 5, 2, 3, 4)


def gelu_pair(v):
    coef = math.sqrt(2.0 / math.pi)
    inner = coef * (v + 0.044715 * v * v * v)
    t = jnp.tanh(inner)
    slope = 0.5 * (1.0 + t) + 0.5 * v * (1.0 - t * t) * coef * (1.0 + 3.0 * 0.044715 * v * v)
    return 0.5 * v * (1.0 + t), slope


def mm(a, b):
    return jnp.dot(a, b, preferred_element_type=F32)


def mm_tn(a, b):
    return lax.dot_general(a, b, (((0,), (0,)), ((), ())), preferred_element_type=F32)


def mm_nt(a, b):
    return lax.dot_general(a, b, (((1,), (1,)), ((), ())), preferred_element_type=F32)


def halves(v):
    high = lax.reduce_precision(v, 8, 7)
    return high.astype(BF16), (v - high).astype(BF16)


def selectors():
    c = np.arange(CLASSES)
    digits = (c // 20, (c // 5) % 4, c % 5)
    valid = (c < 100)[:, None]
    return [((d[:, None] == np.arange(4)[None, :]) & valid).astype(np.float32) for d in digits]


def norm_scale(v):
    return lax.rsqrt(jnp.mean(v * v, axis=-1, keepdims=True) + 1e-06)


def tables(embed, conv_weight, point_weight):
    sel = [jnp.asarray(s, BF16) for s in selectors()]
    stream = embed.astype(F32)
    scale_e = norm_scale(stream)
    normed_e = (stream * scale_e).astype(BF16)
    taps = jnp.concatenate([mm(s, normed_e).astype(BF16) for s in sel], axis=1)
    act0, slope0 = gelu_pair(mm(taps, conv_weight[0]))
    act0 = act0.astype(BF16)
    stab = mm(sel[1], embed) + mm(act0, point_weight[0])
    scale1 = norm_scale(stab)
    ntab = (stab * scale1).astype(BF16)
    width = embed.shape[1]
    u = jnp.concatenate([mm(ntab, conv_weight[1, j * width : (j + 1) * width]) for j in range(3)])
    return stream, scale_e, normed_e, act0, slope0, stab, scale1, ntab, u


def classes(gathered, dil):
    n, rb = gathered.shape
    edge = jnp.full((1, dil), 4, jnp.int32)
    left = jnp.concatenate(
        [jnp.concatenate([edge, gathered[:-1, rb - dil :]]), gathered[:, : rb - dil]], axis=1
    )
    right = jnp.concatenate(
        [gathered[:, dil:], jnp.concatenate([gathered[1:, :dil], edge])], axis=1
    )
    cls = left * 20 + gathered * 5 + right
    none = jnp.full((2, rb), -1, jnp.int32)
    return jnp.concatenate([none, cls, none])


def general(bases, embed, conv_weight, point_weight, cotangent):
    n, dp = lax.axis_size("seq"), lax.axis_size("dp")
    rb, width, mid = bases.shape[1], embed.shape[1], conv_weight.shape[2]
    group = n // STRIDE
    k, x = lax.axis_index("seq"), lax.axis_index("dp")
    zh, r = k // STRIDE, k % STRIDE
    m, core = r // 2, r % 2
    rows = group * rb
    w1, w2 = conv_weight[1], conv_weight[2]
    p0, p1, p2 = point_weight[0], point_weight[1], point_weight[2]

    gathered = lax.all_to_all(jnp.broadcast_to(bases, (n, rb)), "seq", 0, 0, tiled=True)
    own = cotangent[0]
    parts = [own]
    for i in range(1, group):
        parts.append(lax.ppermute(own, "seq", [(s, (s - STRIDE * i) % n) for s in range(n)]))
    cot = lax.dynamic_slice_in_dim(
        jnp.concatenate(parts + parts), ((group - zh) % group) * rb, rows
    )

    stream_e, scale_e, normed_e, act0, slope0, stab, scale1, ntab, u = tables(
        embed, conv_weight, point_weight
    )
    u_high, u_low = halves(u)
    s_high, s_low = halves(stab)

    cls = classes(gathered, rb // 8)
    hots = []
    for j in range(3):
        index = jnp.concatenate(
            [lax.dynamic_slice(cls, (a * STRIDE + r + 2 * j, 0), (1, rb)) for a in range(group)],
            axis=1,
        )
        hots.append((jnp.arange(CLASSES, dtype=jnp.int32)[:, None] == index).astype(BF16))
    hot = jnp.concatenate(hots)

    pre1 = mm_tn(hot, u_high) + mm_tn(hot, u_low)
    act1, slope1 = gelu_pair(pre1)
    act1 = act1.astype(BF16)
    stream2 = mm_tn(hots[1], s_high) + mm_tn(hots[1], s_low) + mm(act1, p1)
    scale2 = norm_scale(stream2)
    normed2 = (stream2 * scale2).astype(BF16)
    nothing = jnp.zeros((rb, width), BF16)
    taps2 = jnp.concatenate(
        [
            jnp.concatenate([nothing, normed2[: rows - rb]]),
            normed2,
            jnp.concatenate([normed2[rb:], nothing]),
        ],
        axis=1,
    )
    pre2 = mm(taps2, w2)
    act2, slope2 = gelu_pair(pre2)
    act2 = act2.astype(BF16)
    features = lax.dynamic_slice_in_dim(stream2, zh * rb, rb) + mm(
        lax.dynamic_slice_in_dim(act2, zh * rb, rb), p2
    )

    grad2 = (mm_nt(cot, p2) * slope2).astype(BF16)
    nothing = jnp.zeros((rb, mid), BF16)
    above = jnp.concatenate([grad2[rb:], nothing])
    below = jnp.concatenate([nothing, grad2[: rows - rb]])
    ng2 = (
        mm_nt(above, w2[:width]) + mm_nt(grad2, w2[width : 2 * width]) + mm_nt(below, w2[2 * width :])
    )
    inner = jnp.mean(ng2 * stream2, axis=-1, keepdims=True)
    back2 = cot.astype(F32) + scale2 * (ng2 - stream2 * scale2 * scale2 * inner)
    back2 = back2.astype(BF16)
    grad1 = (mm_nt(back2, p1) * slope1).astype(BF16)

    h = mm(hot, grad1).astype(BF16)
    ng1 = sum(
        mm_nt(h[j * CLASSES : (j + 1) * CLASSES], w1[j * width : (j + 1) * width]) for j in range(3)
    )
    inner = jnp.mean(ng1 * stab, axis=-1, keepdims=True)
    b = mm(hots[1], back2) + scale1 * (ng1 - stab * scale1 * scale1 * inner)
    b16 = b.astype(BF16)
    s = (mm_nt(b16, p0) * slope0).astype(BF16)
    sel = selectors()
    g = mm(jnp.asarray(np.concatenate([v.T for v in sel]), BF16), s)
    bt = mm(jnp.asarray(sel[1].T, BF16), b16)
    small = jnp.concatenate([g, bt.reshape(2 * 4, mid)])

    crow, prow = 3 * width // n, width // n
    conv1 = jnp.concatenate(
        [mm_tn(ntab, h[j * CLASSES : (j + 1) * CLASSES]) for j in range(3)]
    )
    conv1 = lax.dynamic_slice_in_dim(conv1, zh * STRIDE * crow, STRIDE * crow)
    conv2 = mm_tn(lax.dynamic_slice_in_dim(taps2, zh * STRIDE * crow, STRIDE * crow, axis=1), grad2)

    def share(v):
        return lax.dynamic_slice_in_dim(v, zh * STRIDE * prow, STRIDE * prow, axis=1)

    point = [mm_tn(share(b16), act0), mm_tn(share(back2), act1), mm_tn(share(cot), act2)]
    tile = jnp.concatenate(
        [conv1.reshape(STRIDE, crow, mid), conv2.reshape(STRIDE, crow, mid)]
        + [v.reshape(STRIDE, prow, mid) for v in point],
        axis=1,
    )
    trow = 2 * crow + 3 * prow
    half = STRIDE // 2
    tile = tile.reshape(half, 2, trow, mid)

    swap = [(s, s ^ 1) for s in range(n)]
    mine = lax.dynamic_index_in_dim(tile, core, axis=1, keepdims=False)
    other = lax.dynamic_index_in_dim(tile, 1 - core, axis=1, keepdims=False)
    mine = mine + lax.ppermute(other.astype(BF16), "seq", swap).astype(F32)
    small = small + lax.ppermute(small.astype(BF16), "seq", swap).astype(F32)

    drow = trow // dp
    mine = mine.reshape(half, dp, drow, mid)
    small16 = small.astype(BF16)
    total = lax.dynamic_slice(mine, (m, x, 0, 0), (1, 1, drow, mid))[0, 0]
    for mask in range(half * dp - 1, 0, -1):
        mm_, mx = mask // dp, mask % dp
        piece = lax.dynamic_slice(mine, (m ^ mm_, x ^ mx, 0, 0), (1, 1, drow, mid))[0, 0]
        message = jnp.concatenate([piece.astype(BF16), small16])
        route = [
            (s * dp + d, (s ^ (2 * mm_)) * dp + (d ^ mx)) for s in range(n) for d in range(dp)
        ]
        got = lax.ppermute(message, ("seq", "dp"), route).astype(F32)
        total = total + got[:drow]
        small = small + got[drow:]

    total16 = total.astype(BF16)
    pieces = [total16] + [
        lax.ppermute(total16, "dp", [(d, d ^ i) for d in range(dp)]) for i in range(1, dp)
    ]
    full = jnp.concatenate(
        [
            sum(jnp.where((x ^ i) == d, pieces[i].astype(F32), 0.0) for i in range(dp))
            for d in range(dp)
        ]
    )

    g, bt = small[:12], small[12:].reshape(4, width)
    ng0 = sum(
        mm_nt(g[4 * j : 4 * j + 4].astype(BF16), conv_weight[0, j * width : (j + 1) * width])
        for j in range(3)
    )
    inner = jnp.mean(ng0 * stream_e, axis=-1, keepdims=True)
    embed_grad = bt + scale_e * (ng0 - stream_e * scale_e * scale_e * inner)
    embed_grad = lax.dynamic_slice_in_dim(embed_grad, k * prow, prow, axis=1)
    spread = jnp.concatenate(
        [
            jnp.pad(normed_e, ((4 * j, 8 - 4 * j), (0, 0))) for j in range(3)
        ],
        axis=1,
    )
    spread = lax.dynamic_slice_in_dim(spread, k * crow, crow, axis=1)
    conv0 = mm_tn(spread, g.astype(BF16))
    conv_grad = jnp.stack([conv0, full[:crow], full[crow : 2 * crow]])
    point_grad = full[2 * crow :].reshape(3, prow, mid).transpose(0, 2, 1)
    return features[None], conv_grad, point_grad, embed_grad


def normal(v):
    return (v * norm_scale(v)).astype(BF16)


def spread_kernel(bases_ref, out_ref):
    for i in range(out_ref.shape[0]):
        out_ref[i] = bases_ref[...]


def fetch(source, target, sem):
    copy = pltpu.make_async_copy(source, target, sem)
    copy.start()
    return copy


def fetch_taps(w_ref, layer, held_ref, sems, first, order=(0, 1, 2)):
    width = held_ref.shape[0] // 3
    copies = {}
    for j in order:
        at = pl.ds(j * width, width)
        copies[j] = fetch(w_ref.at[layer, at, :], held_ref.at[at, :], sems.at[first + j])
    return copies


def digits(shape, axis):
    c = lax.broadcasted_iota(jnp.int32, shape, axis).astype(F32)
    left, both = jnp.floor((c + 0.5) / 20.0), jnp.floor((c + 0.5) / 5.0)
    return c < 100.0, (left, both - 4.0 * left, c - 5.0 * both)


def digit_columns():
    valid, values = digits((CLASSES, 4), 0)
    base = lax.broadcasted_iota(jnp.int32, (CLASSES, 4), 1).astype(F32)
    return [jnp.where(valid & (v == base), 1.0, 0.0).astype(BF16) for v in values]


def digit_rows():
    valid, values = digits((16, CLASSES), 1)
    row = lax.broadcasted_iota(jnp.int32, (16, CLASSES), 0).astype(F32)
    hit = (values[0] == row) & (row < 4.0)
    hit |= (values[1] + 4.0 == row) & (row >= 4.0) & (row < 8.0)
    hit |= (values[2] + 8.0 == row) & (row >= 8.0) & (row < 12.0)
    return jnp.where(valid & hit, 1.0, 0.0).astype(BF16)


def table_kernel(embed_ref, w_ref, p_ref, act0_ref, table_ref, w2_ref, w0_ref, w1_ref, p0_ref, sems):
    width, mid = embed_ref.shape[1], act0_ref.shape[1]
    copy_w0 = fetch_taps(w_ref, 0, w0_ref, sems, 0)
    copy_p0 = fetch(p_ref.at[0], p0_ref, sems.at[6])
    copy_w1 = fetch_taps(w_ref, 1, w1_ref, sems, 3)
    copy_w2 = fetch(w_ref.at[2], w2_ref, sems.at[7])
    normed_e = normal(embed_ref[...].astype(F32))
    sel = digit_columns()
    pre = None
    for j in range(3):
        taps = mm(sel[j], normed_e).astype(BF16)
        copy_w0[j].wait()
        term = mm(taps, w0_ref[j * width : (j + 1) * width, :])
        pre = term if pre is None else pre + term
    act0, slope0 = gelu_pair(pre)
    act0 = act0.astype(BF16)
    act0_ref[...] = act0
    copy_p0.wait()
    stab = mm(sel[1], embed_ref[...]) + mm(act0, p0_ref[...])
    table_ref[:, :width] = stab
    table_ref[:, width : width + mid] = slope0
    ntab = normal(stab)
    for j in range(3):
        copy_w1[j].wait()
        at = width + (j + 1) * mid
        table_ref[:, at : at + mid] = mm(ntab, w1_ref[j * width : (j + 1) * width, :])
    copy_w2.wait()


def main_kernel(
    crow, prow, bases_ref, own_ref, far_ref, w_ref, p_ref, w2_ref, table_ref,
    features_ref, mine_ref, other_ref, h_ref, c_ref, w1_ref, p0_ref,
    hot_ref, stream_ref, normed_ref, act1_ref, act2_ref, slope1_ref, slope2_ref,
    cot_ref, grad_ref, back_ref, conv_ref, point_ref, ntab_ref, pt_ref, sent_ref, sems,
):
    n, _, rb = bases_ref.shape
    rows, width = stream_ref.shape
    mid = act1_ref.shape[1]
    dil, half = rb // 8, width // 2
    k = lax.axis_index("seq")
    zh, r, core = k // STRIDE, k % STRIDE, k % 2
    place = pl.ds(pl.multiple_of(zh * rb, 16), rb)
    far = pl.ds(pl.multiple_of((1 - zh) * rb, 16), rb)
    copy_p1 = fetch(p_ref.at[1], pt_ref.at[0], sems.at[0])
    copy_p2 = fetch(p_ref.at[2], pt_ref.at[1], sems.at[1])
    copy_w1 = fetch(w_ref.at[1], w1_ref, sems.at[2])
    copy_p0 = fetch(p_ref.at[0], p0_ref, sems.at[3])
    held = jnp.concatenate([bases_ref[i] for i in range(n)])
    held = (held - 4).astype(F32)
    edge = jnp.zeros((1, rb), F32)
    held = jnp.concatenate(
        [
            jnp.concatenate([edge, held[:-1]]).astype(BF16),
            held.astype(BF16),
            jnp.concatenate([held[1:], edge]).astype(BF16),
        ]
    )
    ahead = lax.broadcasted_iota(jnp.int32, (rb, rb), 0) - lax.broadcasted_iota(jnp.int32, (rb, rb), 1)

    def weight(gap):
        value = jnp.where(gap == -dil, 20.0, jnp.where(gap == 0, 5.0, jnp.where(gap == dil, 1.0, 0.0)))
        return value.astype(BF16)

    cls = (
        mm(held[:n], weight(ahead - rb)) + mm(held[n : 2 * n], weight(ahead)) + mm(held[2 * n :], weight(ahead + rb))
        + 105.0
    ).astype(BF16)
    block = lax.broadcasted_iota(jnp.int32, (n, CLASSES), 0)
    slot = lax.broadcasted_iota(jnp.int32, (n, CLASSES), 1)
    wanted = (slot // 3) * STRIDE + r + 2 * (slot % 3) - 2
    pick = jnp.where((block == wanted) & (slot < 6), 1.0, 0.0).astype(BF16)
    column = mm_tn(cls, pick)
    lanes = (lax.broadcasted_iota(jnp.int32, (rb, CLASSES), 1) + 1).astype(F32)
    for a in range(2):
        for j in range(3):
            i = 3 * a + j
            hot_ref[a * rb : (a + 1) * rb, j * CLASSES : (j + 1) * CLASSES] = jnp.where(
                lanes == column[:, i : i + 1], 1.0, 0.0
            ).astype(BF16)

    hot = hot_ref[...]
    mid_hot = hot[:, CLASSES : 2 * CLASSES]
    u = jnp.concatenate(
        [table_ref[:, width + (j + 1) * mid : width + (j + 2) * mid] for j in range(3)]
    )
    u_high = u.astype(BF16)
    act1, slope1 = gelu_pair(mm(hot, u_high) + mm(hot, (u - u_high.astype(F32)).astype(BF16)))
    act1 = act1.astype(BF16)
    act1_ref[...] = act1
    slope1_ref[...] = slope1
    stab = table_ref[:, :width]
    s_high = stab.astype(BF16)
    stream = mm(mid_hot, s_high) + mm(mid_hot, (stab - s_high.astype(F32)).astype(BF16))
    copy_p1.wait()
    stream = stream + mm(act1, pt_ref[0])
    stream_ref[...] = stream
    normed = normal(stream)
    normed_ref[...] = normed
    sides = jnp.concatenate(
        [mm(normed[rb:], w2_ref[2 * width :, :]), mm(normed[:rb], w2_ref[:width, :])]
    )
    act2, slope2 = gelu_pair(mm(normed, w2_ref[width : 2 * width, :]) + sides)
    act2_ref[...] = act2.astype(BF16)
    slope2_ref[...] = slope2
    copy_p2.wait()
    sent_ref[...] = stream_ref[place, :] + mm(act2_ref[place, :], pt_ref[1])
    copy_features = fetch(sent_ref, features_ref, sems.at[4])

    cot_ref[place, :] = own_ref[...]
    cot_ref[far, :] = far_ref[...]
    grad2 = (mm_nt(cot_ref[...], pt_ref[1]) * slope2_ref[...]).astype(BF16)
    grad_ref[...] = grad2
    sides = jnp.concatenate(
        [mm_nt(grad2[rb:], w2_ref[:width, :]), mm_nt(grad2[:rb], w2_ref[2 * width :, :])]
    )
    ng = mm_nt(grad2, w2_ref[width : 2 * width, :]) + sides
    stream = stream_ref[...]
    scale = norm_scale(stream)
    inner = jnp.mean(ng * stream, axis=-1, keepdims=True)
    back = cot_ref[...].astype(F32) + scale * (ng - stream * (scale * scale * inner))
    back = back.astype(BF16)
    back_ref[...] = back
    grad1 = (mm_nt(back, pt_ref[0]) * slope1_ref[...]).astype(BF16)

    h = mm_tn(hot_ref[...], grad1).astype(BF16)
    h_ref[...] = h
    h = [h[j * CLASSES : (j + 1) * CLASSES] for j in range(3)]
    c_ref[...] = mm_tn(hot_ref[:, CLASSES : 2 * CLASSES], back)
    ntab_ref[...] = normal(table_ref[:, :width])

    columns = pl.ds(pl.multiple_of(zh * half, 128), half)
    side_at = pl.ds(pl.multiple_of(zh * half, 16), width)
    center_at = pl.ds(pl.multiple_of((1 - zh) * width, 16), half)
    conv_ref[0, side_at, :] = mm_tn(ntab_ref[...], jnp.where(zh == 0, h[0], h[2]))
    conv_ref[0, center_at, :] = mm_tn(ntab_ref[:, columns], h[1])
    conv_ref[1, side_at, :] = mm_tn(normed_ref[place, :], grad_ref[far, :])
    conv_ref[1, center_at, :] = mm_tn(normed_ref[:, columns], grad_ref[...])
    point_ref[0] = mm_tn(back_ref[:, columns], act1_ref[...])
    point_ref[1] = mm_tn(cot_ref[:, columns], act2_ref[...])
    part = crow + prow
    for target, side in ((mine_ref, core), (other_ref, 1 - core)):
        for m in range(STRIDE // 2):
            tile = 2 * m + side
            crows = pl.ds(pl.multiple_of(tile * crow, 16), crow)
            prows = pl.ds(pl.multiple_of(tile * prow, 16), prow)
            for layer in range(2):
                at = (2 * m + layer) * part
                target[at : at + crow, :] = conv_ref[layer, crows, :].astype(target.dtype)
                target[at + crow : at + part, :] = point_ref[layer, prows, :].astype(target.dtype)
    for copy in (copy_features, copy_w1, copy_p0):
        copy.wait()


def class_kernel(prow, h_ref, c_ref, table_ref, w1_ref, p0_ref, mine_ref, other_ref, bt_ref):
    width, mid = c_ref.shape[1], h_ref.shape[1]
    half = width // 2
    k = lax.axis_index("seq")
    zh, core = k // STRIDE, k % 2
    ng = None
    for j in range(3):
        term = mm_nt(
            h_ref[j * CLASSES : (j + 1) * CLASSES, :], w1_ref[j * width : (j + 1) * width, :]
        )
        ng = term if ng is None else ng + term
    stab = table_ref[:, :width]
    scale = norm_scale(stab)
    inner = jnp.mean(ng * stab, axis=-1, keepdims=True)
    b = c_ref[...] + scale * (ng - stab * (scale * scale * inner))
    s = (mm_nt(b.astype(BF16), p0_ref[...]) * table_ref[:, width : width + mid]).astype(BF16)
    g = mm(digit_rows(), s)
    bt_ref[...] = jnp.transpose(b)
    for target, side in ((mine_ref, core), (other_ref, 1 - core)):
        for m in range(STRIDE // 2):
            for q in range(3):
                at = pl.ds(pl.multiple_of(zh * half + (2 * m + side) * prow + 16 * q, 16), 16)
                target[16 * m : 16 * m + 16, q * CLASSES : (q + 1) * CLASSES] = bt_ref[at, :].astype(
                    target.dtype
                )
        target[8 * STRIDE : 8 * STRIDE + 16, :] = g.astype(target.dtype)


def message_kernel(part, mine_ref, other_ref, mine_small_ref, other_small_ref, *out_refs):
    k, x = lax.axis_index("seq"), lax.axis_index("dp")
    m = (k % STRIDE) // 2
    end = 8 * STRIDE
    g = mine_small_ref[end:, :] + other_small_ref[end:, :].astype(F32)
    for mask, out_ref in enumerate(out_refs):
        target, layer = m ^ (mask // 2), x ^ (mask % 2)
        at = pl.ds(pl.multiple_of((2 * target + layer) * part, 16), part)
        out_ref[:part, :] = (mine_ref[at, :] + other_ref[at, :].astype(F32)).astype(out_ref.dtype)
        at = pl.ds(pl.multiple_of(target * 16, 16), 16)
        small = mine_small_ref[at, :] + other_small_ref[at, :].astype(F32)
        out_ref[part : part + 16, :] = small.astype(out_ref.dtype)
        out_ref[part + 16 :, :] = g.astype(out_ref.dtype)


def sum_kernel(own_ref, *refs):
    got, (total_ref, send_ref, rest_ref) = refs[:-3], refs[-3:]
    part = total_ref.shape[0]
    total = own_ref[...]
    for ref in got:
        total = total + ref[...].astype(F32)
    total_ref[...] = total[:part]
    send_ref[...] = total[:part].astype(BF16)
    rest_ref[...] = total[part:]


def small_kernel(
    rest_ref, total_ref, embed_ref, w_ref, act0_ref, spread_ref,
    conv_ref, point_ref, embed_out_ref, bt_ref, w0_ref, conv0_ref, point0_ref, sems,
):
    copy_w0 = fetch_taps(w_ref, 0, w0_ref, sems, 0)
    width = embed_ref.shape[1]
    crow = conv_ref.shape[1]
    own = lax.axis_index("dp") + 1
    copies = [
        fetch(total_ref.at[pl.ds(0, crow), :], conv_ref.at[own], sems.at[3]),
        fetch(total_ref.at[pl.ds(crow, point_ref.shape[1]), :], point_ref.at[own], sems.at[4]),
    ]
    g = rest_ref[16:, :]
    bt = jnp.concatenate([rest_ref[:16, q * CLASSES : (q + 1) * CLASSES] for q in range(3)])
    bt = bt.astype(BF16)
    g16 = g.astype(BF16)
    conv0_ref[...] = mm(spread_ref[...], g16)
    copies.append(fetch(conv0_ref, conv_ref.at[0], sems.at[5]))
    point0_ref[...] = mm(bt, act0_ref[...])
    copies.append(fetch(point0_ref, point_ref.at[0], sems.at[6]))
    bt_ref[...] = mm_nt(digit_rows(), bt)[4:8]
    stream = embed_ref[...].astype(F32)
    scale = norm_scale(stream)
    ng = None
    for j in range(3):
        copy_w0[j].wait()
        term = mm_nt(g16, w0_ref[j * width : (j + 1) * width, :])[4 * j : 4 * j + 4]
        ng = term if ng is None else ng + term
    inner = jnp.mean(ng * stream, axis=-1, keepdims=True)
    embed_out_ref[...] = scale * (ng - stream * (scale * scale * inner))
    for copy in copies:
        copy.wait()


def finish_kernel(got_ref, _, __, conv_ref, point_ref, held_ref, sems):
    crow = conv_ref.shape[1]
    other = 2 - lax.axis_index("dp")
    held_ref[...] = got_ref[...].astype(F32)
    copies = [
        fetch(held_ref.at[pl.ds(0, crow), :], conv_ref.at[other], sems.at[0]),
        fetch(held_ref.at[pl.ds(crow, point_ref.shape[1]), :], point_ref.at[other], sems.at[1]),
    ]
    for copy in copies:
        copy.wait()


def call(kernel, outs, *args, far=(), whole=(), away=(), scratch=(), limit=24, aliases=None, flops=0, name=None):
    args = [pltpu.with_memory_space_constraint(v, pltpu.HBM) if i in far else v for i, v in enumerate(args)]
    moved = sum(math.prod(v.shape) * jnp.dtype(v.dtype).itemsize for v in list(args) + list(outs))
    return pl.pallas_call(
        kernel,
        out_shape=outs,
        in_specs=[
            pl.BlockSpec(memory_space=pltpu.HBM if i in far and i not in whole else pltpu.VMEM)
            for i in range(len(args))
        ],
        out_specs=[
            pl.BlockSpec(memory_space=pltpu.HBM if i in away else pltpu.VMEM) for i in range(len(outs))
        ],
        scratch_shapes=list(scratch),
        input_output_aliases=aliases or {},
        compiler_params=pltpu.CompilerParams(vmem_limit_bytes=limit * 1024 * 1024),
        cost_estimate=pl.CostEstimate(flops=flops, bytes_accessed=moved, transcendentals=0),
        name=name,
    )(*args)


def on_device(bases, embed, conv_weight, point_weight, cotangent):
    n, dp = lax.axis_size("seq"), lax.axis_size("dp")
    rb, width, mid = bases.shape[1], embed.shape[1], conv_weight.shape[2]
    if n != 2 * STRIDE or dp != 2:
        return general(bases, embed, conv_weight, point_weight, cotangent)
    k = lax.axis_index("seq")
    zh, r = k // STRIDE, k % STRIDE
    rows = 2 * rb
    crow, prow = 3 * width // n, width // n
    part = crow + prow
    shape, near = jax.ShapeDtypeStruct, pltpu.VMEM

    own = cotangent[0]
    far = lax.ppermute(own, "seq", [(s, (s + STRIDE) % n) for s in range(n)])
    (copies,) = call(spread_kernel, [near((n, 1, rb), jnp.int32)], bases, far=(0,), whole=(0,), name="spread")
    gathered = lax.all_to_all(copies, "seq", 0, 0, tiled=True)

    taps = pltpu.VMEM((3 * width, mid), BF16)
    act0, table, w2 = call(
        table_kernel,
        [
            shape((CLASSES, mid), BF16),
            pltpu.VMEM((CLASSES, width + 4 * mid), F32),
            pltpu.VMEM((3 * width, mid), BF16),
        ],
        embed, conv_weight, point_weight,
        far=(0, 1, 2),
        whole=(0,),
        scratch=[taps, taps, pltpu.VMEM((mid, width), BF16), pltpu.SemaphoreType.DMA((8,))],
        limit=20,
        flops=4 * CLASSES * 3 * width * mid,
        name="tables",
    )
    features, mine, other, h, c, w1, p0 = call(
        lambda *refs: main_kernel(crow, prow, *refs),
        [
            shape((rb, width), F32),
            near((STRIDE * part, mid), F32),
            near((STRIDE * part, mid), BF16),
            near((3 * CLASSES, mid), BF16),
            near((CLASSES, width), F32),
            near((3 * width, mid), BF16),
            near((mid, width), BF16),
        ],
        gathered, own, far, conv_weight, point_weight, w2, table,
        far=(3, 4),
        scratch=[
            pltpu.VMEM((rows, 3 * CLASSES), BF16),
            pltpu.VMEM((rows, width), F32),
            pltpu.VMEM((rows, width), BF16),
            pltpu.VMEM((rows, mid), BF16),
            pltpu.VMEM((rows, mid), BF16),
            pltpu.VMEM((rows, mid), F32),
            pltpu.VMEM((rows, mid), F32),
            pltpu.VMEM((rows, width), BF16),
            pltpu.VMEM((rows, mid), BF16),
            pltpu.VMEM((rows, width), BF16),
            pltpu.VMEM((2, STRIDE * crow, mid), F32),
            pltpu.VMEM((2, STRIDE * prow, mid), F32),
            pltpu.VMEM((CLASSES, width), BF16),
            pltpu.VMEM((2, mid, width), BF16),
            pltpu.VMEM((rb, width), F32),
            pltpu.SemaphoreType.DMA((5,)),
        ],
        away=(0,),
        flops=9 * rows * 3 * width * mid,
        name="tower",
    )

    swap = [(s, s ^ 1) for s in range(n)]
    got = lax.ppermute(other, "seq", swap)
    small_rows = 8 * STRIDE + 16
    mine_small, other_small = call(
        lambda *refs: class_kernel(prow, *refs),
        [near((small_rows, mid), F32), near((small_rows, mid), BF16)],
        h, c, table, w1, p0,
        scratch=[pltpu.VMEM((width, CLASSES), F32)],
        flops=4 * CLASSES * 3 * width * mid,
        name="classes",
    )
    got_small = lax.ppermute(other_small, "seq", swap)
    peers = STRIDE // 2 * dp
    pieces = call(
        lambda *refs: message_kernel(part, *refs),
        [shape((part + 32, mid), F32 if i == 0 else BF16) for i in range(peers)],
        mine, got, mine_small, got_small,
        name="messages",
    )
    arrived = []
    for mask in ORDER:
        route = [
            (s * dp + d, (s ^ (2 * (mask // dp))) * dp + (d ^ (mask % dp)))
            for s in range(n)
            for d in range(dp)
        ]
        arrived.append(lax.ppermute(pieces[mask], ("seq", "dp"), route))
    total, send, rest = call(
        sum_kernel,
        [shape((part, mid), F32), shape((part, mid), BF16), shape((32, mid), F32)],
        pieces[0], *arrived,
        name="sums",
    )
    swapped = lax.ppermute(send, "dp", [(d, d ^ 1) for d in range(dp)])

    stream_e = embed.astype(F32)
    normed_e = (stream_e * norm_scale(stream_e)).astype(BF16)
    spread = jnp.concatenate(
        [jnp.pad(normed_e, ((4 * j, 12 - 4 * j), (0, 0))) for j in range(3)], axis=1
    )
    spread = lax.dynamic_slice_in_dim(spread, k * crow, crow, axis=1).T
    conv_grad, point_grad, embed_full, bt = call(
        small_kernel,
        [
            shape((3, crow, mid), F32),
            shape((3, prow, mid), F32),
            shape((4, width), F32),
            shape((4, prow), F32),
        ],
        rest, total, embed, conv_weight, act0, spread,
        far=(3,),
        away=(0, 1),
        scratch=[
            pltpu.VMEM((3 * width, mid), BF16),
            pltpu.VMEM((crow, mid), F32),
            pltpu.VMEM((prow, mid), F32),
            pltpu.SemaphoreType.DMA((7,)),
        ],
        name="layer0",
    )
    embed_grad = bt + lax.dynamic_slice_in_dim(embed_full, k * prow, prow, axis=1)
    conv_grad, point_grad = call(
        finish_kernel,
        [shape((3, crow, mid), F32), shape((3, prow, mid), F32)],
        swapped, conv_grad, point_grad,
        far=(1, 2),
        away=(0, 1),
        aliases={1: 0, 2: 1},
        scratch=[pltpu.VMEM((part, mid), F32), pltpu.SemaphoreType.DMA((2,))],
        name="finish",
    )
    return features[None], conv_grad, point_grad.transpose(0, 2, 1), embed_grad


def solution(mesh):
    in_specs = (P("dp", "seq"), P(), P(), P(), P("dp", "seq", None))
    out_specs = (P("dp", "seq", None), P(None, "seq", None), P(None, None, "seq"), P(None, "seq"))
    return jax.shard_map(
        on_device, mesh=mesh, in_specs=in_specs, out_specs=out_specs, check_vma=False
    )
```

```python
import math

import jax
import jax.numpy as jnp
import numpy as np
from jax import lax
from jax.experimental import pallas as pl
from jax.experimental.pallas import tpu as pltpu
from jax.sharding import PartitionSpec as P

BF16 = jnp.bfloat16
F32 = jnp.float32
CLASSES = 128
STRIDE = 8
ORDER = (7, 6, 1, 5, 2, 3, 4)


def gelu_pair(v):
    coef = math.sqrt(2.0 / math.pi)
    inner = coef * (v + 0.044715 * v * v * v)
    t = jnp.tanh(inner)
    slope = 0.5 * (1.0 + t) + 0.5 * v * (1.0 - t * t) * coef * (1.0 + 3.0 * 0.044715 * v * v)
    return 0.5 * v * (1.0 + t), slope


def mm(a, b):
    return jnp.dot(a, b, preferred_element_type=F32)


def mm_tn(a, b):
    return lax.dot_general(a, b, (((0,), (0,)), ((), ())), preferred_element_type=F32)


def mm_nt(a, b):
    return lax.dot_general(a, b, (((1,), (1,)), ((), ())), preferred_element_type=F32)


def halves(v):
    high = lax.reduce_precision(v, 8, 7)
    return high.astype(BF16), (v - high).astype(BF16)


def selectors():
    c = np.arange(CLASSES)
    digits = (c // 20, (c // 5) % 4, c % 5)
    valid = (c < 100)[:, None]
    return [((d[:, None] == np.arange(4)[None, :]) & valid).astype(np.float32) for d in digits]


def norm_scale(v):
    return lax.rsqrt(jnp.mean(v * v, axis=-1, keepdims=True) + 1e-06)


def tables(embed, conv_weight, point_weight):
    sel = [jnp.asarray(s, BF16) for s in selectors()]
    stream = embed.astype(F32)
    scale_e = norm_scale(stream)
    normed_e = (stream * scale_e).astype(BF16)
    taps = jnp.concatenate([mm(s, normed_e).astype(BF16) for s in sel], axis=1)
    act0, slope0 = gelu_pair(mm(taps, conv_weight[0]))
    act0 = act0.astype(BF16)
    stab = mm(sel[1], embed) + mm(act0, point_weight[0])
    scale1 = norm_scale(stab)
    ntab = (stab * scale1).astype(BF16)
    width = embed.shape[1]
    u = jnp.concatenate([mm(ntab, conv_weight[1, j * width : (j + 1) * width]) for j in range(3)])
    return stream, scale_e, normed_e, act0, slope0, stab, scale1, ntab, u


def classes(gathered, dil):
    n, rb = gathered.shape
    edge = jnp.full((1, dil), 4, jnp.int32)
    left = jnp.concatenate(
        [jnp.concatenate([edge, gathered[:-1, rb - dil :]]), gathered[:, : rb - dil]], axis=1
    )
    right = jnp.concatenate(
        [gathered[:, dil:], jnp.concatenate([gathered[1:, :dil], edge])], axis=1
    )
    cls = left * 20 + gathered * 5 + right
    none = jnp.full((2, rb), -1, jnp.int32)
    return jnp.concatenate([none, cls, none])


def general(bases, embed, conv_weight, point_weight, cotangent):
    n, dp = lax.axis_size("seq"), lax.axis_size("dp")
    rb, width, mid = bases.shape[1], embed.shape[1], conv_weight.shape[2]
    group = n // STRIDE
    k, x = lax.axis_index("seq"), lax.axis_index("dp")
    zh, r = k // STRIDE, k % STRIDE
    m, core = r // 2, r % 2
    rows = group * rb
    w1, w2 = conv_weight[1], conv_weight[2]
    p0, p1, p2 = point_weight[0], point_weight[1], point_weight[2]

    gathered = lax.all_to_all(jnp.broadcast_to(bases, (n, rb)), "seq", 0, 0, tiled=True)
    own = cotangent[0]
    parts = [own]
    for i in range(1, group):
        parts.append(lax.ppermute(own, "seq", [(s, (s - STRIDE * i) % n) for s in range(n)]))
    cot = lax.dynamic_slice_in_dim(
        jnp.concatenate(parts + parts), ((group - zh) % group) * rb, rows
    )

    stream_e, scale_e, normed_e, act0, slope0, stab, scale1, ntab, u = tables(
        embed, conv_weight, point_weight
    )
    u_high, u_low = halves(u)
    s_high, s_low = halves(stab)

    cls = classes(gathered, rb // 8)
    hots = []
    for j in range(3):
        index = jnp.concatenate(
            [lax.dynamic_slice(cls, (a * STRIDE + r + 2 * j, 0), (1, rb)) for a in range(group)],
            axis=1,
        )
        hots.append((jnp.arange(CLASSES, dtype=jnp.int32)[:, None] == index).astype(BF16))
    hot = jnp.concatenate(hots)

    pre1 = mm_tn(hot, u_high) + mm_tn(hot, u_low)
    act1, slope1 = gelu_pair(pre1)
    act1 = act1.astype(BF16)
    stream2 = mm_tn(hots[1], s_high) + mm_tn(hots[1], s_low) + mm(act1, p1)
    scale2 = norm_scale(stream2)
    normed2 = (stream2 * scale2).astype(BF16)
    nothing = jnp.zeros((rb, width), BF16)
    taps2 = jnp.concatenate(
        [
            jnp.concatenate([nothing, normed2[: rows - rb]]),
            normed2,
            jnp.concatenate([normed2[rb:], nothing]),
        ],
        axis=1,
    )
    pre2 = mm(taps2, w2)
    act2, slope2 = gelu_pair(pre2)
    act2 = act2.astype(BF16)
    features = lax.dynamic_slice_in_dim(stream2, zh * rb, rb) + mm(
        lax.dynamic_slice_in_dim(act2, zh * rb, rb), p2
    )

    grad2 = (mm_nt(cot, p2) * slope2).astype(BF16)
    nothing = jnp.zeros((rb, mid), BF16)
    above = jnp.concatenate([grad2[rb:], nothing])
    below = jnp.concatenate([nothing, grad2[: rows - rb]])
    ng2 = (
        mm_nt(above, w2[:width]) + mm_nt(grad2, w2[width : 2 * width]) + mm_nt(below, w2[2 * width :])
    )
    inner = jnp.mean(ng2 * stream2, axis=-1, keepdims=True)
    back2 = cot.astype(F32) + scale2 * (ng2 - stream2 * scale2 * scale2 * inner)
    back2 = back2.astype(BF16)
    grad1 = (mm_nt(back2, p1) * slope1).astype(BF16)

    h = mm(hot, grad1).astype(BF16)
    ng1 = sum(
        mm_nt(h[j * CLASSES : (j + 1) * CLASSES], w1[j * width : (j + 1) * width]) for j in range(3)
    )
    inner = jnp.mean(ng1 * stab, axis=-1, keepdims=True)
    b = mm(hots[1], back2) + scale1 * (ng1 - stab * scale1 * scale1 * inner)
    b16 = b.astype(BF16)
    s = (mm_nt(b16, p0) * slope0).astype(BF16)
    sel = selectors()
    g = mm(jnp.asarray(np.concatenate([v.T for v in sel]), BF16), s)
    bt = mm(jnp.asarray(sel[1].T, BF16), b16)
    small = jnp.concatenate([g, bt.reshape(2 * 4, mid)])

    crow, prow = 3 * width // n, width // n
    conv1 = jnp.concatenate(
        [mm_tn(ntab, h[j * CLASSES : (j + 1) * CLASSES]) for j in range(3)]
    )
    conv1 = lax.dynamic_slice_in_dim(conv1, zh * STRIDE * crow, STRIDE * crow)
    conv2 = mm_tn(lax.dynamic_slice_in_dim(taps2, zh * STRIDE * crow, STRIDE * crow, axis=1), grad2)

    def share(v):
        return lax.dynamic_slice_in_dim(v, zh * STRIDE * prow, STRIDE * prow, axis=1)

    point = [mm_tn(share(b16), act0), mm_tn(share(back2), act1), mm_tn(share(cot), act2)]
    tile = jnp.concatenate(
        [conv1.reshape(STRIDE, crow, mid), conv2.reshape(STRIDE, crow, mid)]
        + [v.reshape(STRIDE, prow, mid) for v in point],
        axis=1,
    )
    trow = 2 * crow + 3 * prow
    half = STRIDE // 2
    tile = tile.reshape(half, 2, trow, mid)

    swap = [(s, s ^ 1) for s in range(n)]
    mine = lax.dynamic_index_in_dim(tile, core, axis=1, keepdims=False)
    other = lax.dynamic_index_in_dim(tile, 1 - core, axis=1, keepdims=False)
    mine = mine + lax.ppermute(other.astype(BF16), "seq", swap).astype(F32)
    small = small + lax.ppermute(small.astype(BF16), "seq", swap).astype(F32)

    drow = trow // dp
    mine = mine.reshape(half, dp, drow, mid)
    small16 = small.astype(BF16)
    total = lax.dynamic_slice(mine, (m, x, 0, 0), (1, 1, drow, mid))[0, 0]
    for mask in range(half * dp - 1, 0, -1):
        mm_, mx = mask // dp, mask % dp
        piece = lax.dynamic_slice(mine, (m ^ mm_, x ^ mx, 0, 0), (1, 1, drow, mid))[0, 0]
        message = jnp.concatenate([piece.astype(BF16), small16])
        route = [
            (s * dp + d, (s ^ (2 * mm_)) * dp + (d ^ mx)) for s in range(n) for d in range(dp)
        ]
        got = lax.ppermute(message, ("seq", "dp"), route).astype(F32)
        total = total + got[:drow]
        small = small + got[drow:]

    total16 = total.astype(BF16)
    pieces = [total16] + [
        lax.ppermute(total16, "dp", [(d, d ^ i) for d in range(dp)]) for i in range(1, dp)
    ]
    full = jnp.concatenate(
        [
            sum(jnp.where((x ^ i) == d, pieces[i].astype(F32), 0.0) for i in range(dp))
            for d in range(dp)
        ]
    )

    g, bt = small[:12], small[12:].reshape(4, width)
    ng0 = sum(
        mm_nt(g[4 * j : 4 * j + 4].astype(BF16), conv_weight[0, j * width : (j + 1) * width])
        for j in range(3)
    )
    inner = jnp.mean(ng0 * stream_e, axis=-1, keepdims=True)
    embed_grad = bt + scale_e * (ng0 - stream_e * scale_e * scale_e * inner)
    embed_grad = lax.dynamic_slice_in_dim(embed_grad, k * prow, prow, axis=1)
    spread = jnp.concatenate(
        [
            jnp.pad(normed_e, ((4 * j, 8 - 4 * j), (0, 0))) for j in range(3)
        ],
        axis=1,
    )
    spread = lax.dynamic_slice_in_dim(spread, k * crow, crow, axis=1)
    conv0 = mm_tn(spread, g.astype(BF16))
    conv_grad = jnp.stack([conv0, full[:crow], full[crow : 2 * crow]])
    point_grad = full[2 * crow :].reshape(3, prow, mid).transpose(0, 2, 1)
    return features[None], conv_grad, point_grad, embed_grad


def normal(v):
    return (v * norm_scale(v)).astype(BF16)


def spread_kernel(bases_ref, out_ref, sems):
    copies = [fetch(bases_ref, out_ref.at[i], sems.at[i]) for i in range(out_ref.shape[0])]
    for copy in copies:
        copy.wait()


def fetch(source, target, sem):
    copy = pltpu.make_async_copy(source, target, sem)
    copy.start()
    return copy


def fetch_taps(w_ref, layer, held_ref, sems, first, order=(0, 1, 2)):
    width = held_ref.shape[0] // 3
    copies = {}
    for j in order:
        at = pl.ds(j * width, width)
        copies[j] = fetch(w_ref.at[layer, at, :], held_ref.at[at, :], sems.at[first + j])
    return copies


def digits(shape, axis):
    c = lax.broadcasted_iota(jnp.int32, shape, axis).astype(F32)
    left, both = jnp.floor((c + 0.5) / 20.0), jnp.floor((c + 0.5) / 5.0)
    return c < 100.0, (left, both - 4.0 * left, c - 5.0 * both)


def digit_columns():
    valid, values = digits((CLASSES, 4), 0)
    base = lax.broadcasted_iota(jnp.int32, (CLASSES, 4), 1).astype(F32)
    return [jnp.where(valid & (v == base), 1.0, 0.0).astype(BF16) for v in values]


def digit_rows():
    valid, values = digits((16, CLASSES), 1)
    row = lax.broadcasted_iota(jnp.int32, (16, CLASSES), 0).astype(F32)
    hit = (values[0] == row) & (row < 4.0)
    hit |= (values[1] + 4.0 == row) & (row >= 4.0) & (row < 8.0)
    hit |= (values[2] + 8.0 == row) & (row >= 8.0) & (row < 12.0)
    return jnp.where(valid & hit, 1.0, 0.0).astype(BF16)


def table_kernel(embed_ref, w_ref, p_ref, act0_ref, table_ref, w2_ref, w0_ref, w1_ref, p0_ref, sems):
    width, mid = embed_ref.shape[1], act0_ref.shape[1]
    copy_w0 = fetch_taps(w_ref, 0, w0_ref, sems, 0)
    copy_p0 = fetch(p_ref.at[0], p0_ref, sems.at[6])
    copy_w1 = fetch_taps(w_ref, 1, w1_ref, sems, 3)
    copy_w2 = fetch(w_ref.at[2], w2_ref, sems.at[7])
    normed_e = normal(embed_ref[...].astype(F32))
    sel = digit_columns()
    pre = None
    for j in range(3):
        taps = mm(sel[j], normed_e).astype(BF16)
        copy_w0[j].wait()
        term = mm(taps, w0_ref[j * width : (j + 1) * width, :])
        pre = term if pre is None else pre + term
    act0, slope0 = gelu_pair(pre)
    act0 = act0.astype(BF16)
    act0_ref[...] = act0
    copy_p0.wait()
    stab = mm(sel[1], embed_ref[...]) + mm(act0, p0_ref[...])
    table_ref[:, :width] = stab
    table_ref[:, width : width + mid] = slope0
    ntab = normal(stab)
    for j in range(3):
        copy_w1[j].wait()
        at = width + (j + 1) * mid
        table_ref[:, at : at + mid] = mm(ntab, w1_ref[j * width : (j + 1) * width, :])
    copy_w2.wait()


def main_kernel(
    crow, prow, bases_ref, own_ref, far_ref, w_ref, p_ref, w2_ref, table_ref,
    features_ref, conv_ref, point_ref, other_ref, h_ref, c_ref, w1_ref, p0_ref,
    hot_ref, stream_ref, normed_ref, act1_ref, act2_ref, slope1_ref, slope2_ref,
    cot_ref, grad_ref, back_ref, ntab_ref, pt_ref, sent_ref, sems,
):
    n, _, rb = bases_ref.shape
    rows, width = stream_ref.shape
    mid = act1_ref.shape[1]
    dil, half = rb // 8, width // 2
    k = lax.axis_index("seq")
    zh, r, core = k // STRIDE, k % STRIDE, k % 2
    place = pl.ds(pl.multiple_of(zh * rb, 16), rb)
    far = pl.ds(pl.multiple_of((1 - zh) * rb, 16), rb)
    copy_p1 = fetch(p_ref.at[1], pt_ref.at[0], sems.at[0])
    copy_p2 = fetch(p_ref.at[2], pt_ref.at[1], sems.at[1])
    copy_w1 = fetch(w_ref.at[1], w1_ref, sems.at[2])
    copy_p0 = fetch(p_ref.at[0], p0_ref, sems.at[3])
    held = jnp.concatenate([bases_ref[i] for i in range(n)])
    held = (held - 4).astype(F32)
    edge = jnp.zeros((1, rb), F32)
    held = jnp.concatenate(
        [
            jnp.concatenate([edge, held[:-1]]).astype(BF16),
            held.astype(BF16),
            jnp.concatenate([held[1:], edge]).astype(BF16),
        ]
    )
    ahead = lax.broadcasted_iota(jnp.int32, (rb, rb), 0) - lax.broadcasted_iota(jnp.int32, (rb, rb), 1)

    def weight(gap):
        value = jnp.where(gap == -dil, 20.0, jnp.where(gap == 0, 5.0, jnp.where(gap == dil, 1.0, 0.0)))
        return value.astype(BF16)

    cls = (
        mm(held[:n], weight(ahead - rb)) + mm(held[n : 2 * n], weight(ahead)) + mm(held[2 * n :], weight(ahead + rb))
        + 105.0
    ).astype(BF16)
    block = lax.broadcasted_iota(jnp.int32, (n, CLASSES), 0)
    slot = lax.broadcasted_iota(jnp.int32, (n, CLASSES), 1)
    wanted = (slot // 3) * STRIDE + r + 2 * (slot % 3) - 2
    pick = jnp.where((block == wanted) & (slot < 6), 1.0, 0.0).astype(BF16)
    column = mm_tn(cls, pick)
    lanes = (lax.broadcasted_iota(jnp.int32, (rb, CLASSES), 1) + 1).astype(F32)
    for a in range(2):
        for j in range(3):
            i = 3 * a + j
            hot_ref[a * rb : (a + 1) * rb, j * CLASSES : (j + 1) * CLASSES] = jnp.where(
                lanes == column[:, i : i + 1], 1.0, 0.0
            ).astype(BF16)

    hot = hot_ref[...]
    mid_hot = hot[:, CLASSES : 2 * CLASSES]
    u = jnp.concatenate(
        [table_ref[:, width + (j + 1) * mid : width + (j + 2) * mid] for j in range(3)]
    )
    u_high = u.astype(BF16)
    act1, slope1 = gelu_pair(mm(hot, u_high) + mm(hot, (u - u_high.astype(F32)).astype(BF16)))
    act1 = act1.astype(BF16)
    act1_ref[...] = act1
    slope1_ref[...] = slope1
    stab = table_ref[:, :width]
    s_high = stab.astype(BF16)
    stream = mm(mid_hot, s_high) + mm(mid_hot, (stab - s_high.astype(F32)).astype(BF16))
    copy_p1.wait()
    stream = stream + mm(act1, pt_ref[0])
    stream_ref[...] = stream
    normed = normal(stream)
    normed_ref[...] = normed
    sides = jnp.concatenate(
        [mm(normed[rb:], w2_ref[2 * width :, :]), mm(normed[:rb], w2_ref[:width, :])]
    )
    act2, slope2 = gelu_pair(mm(normed, w2_ref[width : 2 * width, :]) + sides)
    act2_ref[...] = act2.astype(BF16)
    slope2_ref[...] = slope2
    copy_p2.wait()
    sent_ref[...] = stream_ref[place, :] + mm(act2_ref[place, :], pt_ref[1])
    copy_features = fetch(sent_ref, features_ref, sems.at[4])

    cot_ref[place, :] = own_ref[...]
    cot_ref[far, :] = far_ref[...]
    grad2 = (mm_nt(cot_ref[...], pt_ref[1]) * slope2_ref[...]).astype(BF16)
    grad_ref[...] = grad2
    sides = jnp.concatenate(
        [mm_nt(grad2[rb:], w2_ref[:width, :]), mm_nt(grad2[:rb], w2_ref[2 * width :, :])]
    )
    ng = mm_nt(grad2, w2_ref[width : 2 * width, :]) + sides
    stream = stream_ref[...]
    scale = norm_scale(stream)
    inner = jnp.mean(ng * stream, axis=-1, keepdims=True)
    back = cot_ref[...].astype(F32) + scale * (ng - stream * (scale * scale * inner))
    back = back.astype(BF16)
    back_ref[...] = back
    grad1 = (mm_nt(back, pt_ref[0]) * slope1_ref[...]).astype(BF16)

    h = mm_tn(hot_ref[...], grad1).astype(BF16)
    h_ref[...] = h
    h = [h[j * CLASSES : (j + 1) * CLASSES] for j in range(3)]
    c_ref[...] = mm_tn(hot_ref[:, CLASSES : 2 * CLASSES], back)
    ntab_ref[...] = normal(table_ref[:, :width])

    columns = pl.ds(pl.multiple_of(zh * half, 128), half)
    side_at = pl.ds(pl.multiple_of(zh * half, 16), width)
    center_at = pl.ds(pl.multiple_of((1 - zh) * width, 16), half)
    conv_ref[0, side_at, :] = mm_tn(ntab_ref[...], jnp.where(zh == 0, h[0], h[2]))
    conv_ref[0, center_at, :] = mm_tn(ntab_ref[:, columns], h[1])
    conv_ref[1, side_at, :] = mm_tn(normed_ref[place, :], grad_ref[far, :])
    conv_ref[1, center_at, :] = mm_tn(normed_ref[:, columns], grad_ref[...])
    point_ref[0] = mm_tn(back_ref[:, columns], act1_ref[...])
    point_ref[1] = mm_tn(cot_ref[:, columns], act2_ref[...])
    part = crow + prow
    for m in range(STRIDE // 2):
        tile = 2 * m + 1 - core
        crows = pl.ds(pl.multiple_of(tile * crow, 16), crow)
        prows = pl.ds(pl.multiple_of(tile * prow, 16), prow)
        for layer in range(2):
            at = (2 * m + layer) * part
            other_ref[at : at + crow, :] = conv_ref[layer, crows, :].astype(BF16)
            other_ref[at + crow : at + part, :] = point_ref[layer, prows, :].astype(BF16)
    for copy in (copy_features, copy_w1, copy_p0):
        copy.wait()


def class_kernel(prow, h_ref, c_ref, table_ref, w1_ref, p0_ref, mine_ref, other_ref, bt_ref):
    width, mid = c_ref.shape[1], h_ref.shape[1]
    half = width // 2
    k = lax.axis_index("seq")
    zh, core = k // STRIDE, k % 2
    ng = None
    for j in range(3):
        term = mm_nt(
            h_ref[j * CLASSES : (j + 1) * CLASSES, :], w1_ref[j * width : (j + 1) * width, :]
        )
        ng = term if ng is None else ng + term
    stab = table_ref[:, :width]
    scale = norm_scale(stab)
    inner = jnp.mean(ng * stab, axis=-1, keepdims=True)
    b = c_ref[...] + scale * (ng - stab * (scale * scale * inner))
    s = (mm_nt(b.astype(BF16), p0_ref[...]) * table_ref[:, width : width + mid]).astype(BF16)
    g = mm(digit_rows(), s)
    bt_ref[...] = jnp.transpose(b)
    for target, side in ((mine_ref, core), (other_ref, 1 - core)):
        for m in range(STRIDE // 2):
            for q in range(3):
                at = pl.ds(pl.multiple_of(zh * half + (2 * m + side) * prow + 16 * q, 16), 16)
                target[16 * m : 16 * m + 16, q * CLASSES : (q + 1) * CLASSES] = bt_ref[at, :].astype(
                    target.dtype
                )
        target[8 * STRIDE : 8 * STRIDE + 16, :] = g.astype(target.dtype)


def message_kernel(
    crow, prow, conv_ref, point_ref, other_ref, mine_small_ref, other_small_ref, *out_refs
):
    k, x = lax.axis_index("seq"), lax.axis_index("dp")
    m, core = (k % STRIDE) // 2, k % 2
    part, end = crow + prow, 8 * STRIDE
    g = mine_small_ref[end:, :] + other_small_ref[end:, :].astype(F32)
    for mask, out_ref in enumerate(out_refs):
        target, layer = m ^ (mask // 2), x ^ (mask % 2)
        tile = 2 * target + core
        at = (2 * target + layer) * part
        mine = conv_ref[layer, pl.ds(pl.multiple_of(tile * crow, 16), crow), :]
        got = other_ref[pl.ds(pl.multiple_of(at, 16), crow), :].astype(F32)
        out_ref[:crow, :] = (mine + got).astype(out_ref.dtype)
        mine = point_ref[layer, pl.ds(pl.multiple_of(tile * prow, 16), prow), :]
        got = other_ref[pl.ds(pl.multiple_of(at + crow, 16), prow), :].astype(F32)
        out_ref[crow:part, :] = (mine + got).astype(out_ref.dtype)
        at = pl.ds(pl.multiple_of(target * 16, 16), 16)
        small = mine_small_ref[at, :] + other_small_ref[at, :].astype(F32)
        out_ref[part : part + 16, :] = small.astype(out_ref.dtype)
        out_ref[part + 16 :, :] = g.astype(out_ref.dtype)


def sum_kernel(own_ref, *refs):
    got, (total_ref, send_ref, rest_ref) = refs[:-3], refs[-3:]
    part = total_ref.shape[0]
    total = own_ref[...]
    for ref in got:
        total = total + ref[...].astype(F32)
    total_ref[...] = total[:part]
    send_ref[...] = total[:part].astype(BF16)
    rest_ref[...] = total[part:]


def small_kernel(
    rest_ref, total_ref, embed_ref, w_ref, act0_ref, spread_ref,
    conv_ref, point_ref, embed_out_ref, bt_ref, w0_ref, conv0_ref, point0_ref, sems,
):
    copy_w0 = fetch_taps(w_ref, 0, w0_ref, sems, 0)
    width = embed_ref.shape[1]
    crow = conv_ref.shape[1]
    own = lax.axis_index("dp") + 1
    copies = [
        fetch(total_ref.at[pl.ds(0, crow), :], conv_ref.at[own], sems.at[3]),
        fetch(total_ref.at[pl.ds(crow, point_ref.shape[1]), :], point_ref.at[own], sems.at[4]),
    ]
    g = rest_ref[16:, :]
    bt = jnp.concatenate([rest_ref[:16, q * CLASSES : (q + 1) * CLASSES] for q in range(3)])
    bt = bt.astype(BF16)
    g16 = g.astype(BF16)
    conv0_ref[...] = mm(spread_ref[...], g16)
    copies.append(fetch(conv0_ref, conv_ref.at[0], sems.at[5]))
    point0_ref[...] = mm(bt, act0_ref[...])
    copies.append(fetch(point0_ref, point_ref.at[0], sems.at[6]))
    bt_ref[...] = mm_nt(digit_rows(), bt)[4:8]
    stream = embed_ref[...].astype(F32)
    scale = norm_scale(stream)
    ng = None
    for j in range(3):
        copy_w0[j].wait()
        term = mm_nt(g16, w0_ref[j * width : (j + 1) * width, :])[4 * j : 4 * j + 4]
        ng = term if ng is None else ng + term
    inner = jnp.mean(ng * stream, axis=-1, keepdims=True)
    embed_out_ref[...] = scale * (ng - stream * (scale * scale * inner))
    for copy in copies:
        copy.wait()


def finish_kernel(got_ref, _, __, conv_ref, point_ref, held_ref, sems):
    crow = conv_ref.shape[1]
    other = 2 - lax.axis_index("dp")
    held_ref[...] = got_ref[...].astype(F32)
    copies = [
        fetch(held_ref.at[pl.ds(0, crow), :], conv_ref.at[other], sems.at[0]),
        fetch(held_ref.at[pl.ds(crow, point_ref.shape[1]), :], point_ref.at[other], sems.at[1]),
    ]
    for copy in copies:
        copy.wait()


def call(kernel, outs, *args, far=(), whole=(), away=(), scratch=(), limit=24, aliases=None, flops=0, name=None):
    args = [pltpu.with_memory_space_constraint(v, pltpu.HBM) if i in far else v for i, v in enumerate(args)]
    moved = sum(math.prod(v.shape) * jnp.dtype(v.dtype).itemsize for v in list(args) + list(outs))
    return pl.pallas_call(
        kernel,
        out_shape=outs,
        in_specs=[
            pl.BlockSpec(memory_space=pltpu.HBM if i in far and i not in whole else pltpu.VMEM)
            for i in range(len(args))
        ],
        out_specs=[
            pl.BlockSpec(memory_space=pltpu.HBM if i in away else pltpu.VMEM) for i in range(len(outs))
        ],
        scratch_shapes=list(scratch),
        input_output_aliases=aliases or {},
        compiler_params=pltpu.CompilerParams(vmem_limit_bytes=limit * 1024 * 1024),
        cost_estimate=pl.CostEstimate(flops=flops, bytes_accessed=moved, transcendentals=0),
        name=name,
    )(*args)


def on_device(bases, embed, conv_weight, point_weight, cotangent):
    n, dp = lax.axis_size("seq"), lax.axis_size("dp")
    rb, width, mid = bases.shape[1], embed.shape[1], conv_weight.shape[2]
    if n != 2 * STRIDE or dp != 2:
        return general(bases, embed, conv_weight, point_weight, cotangent)
    k = lax.axis_index("seq")
    zh, r = k // STRIDE, k % STRIDE
    rows = 2 * rb
    crow, prow = 3 * width // n, width // n
    part = crow + prow
    shape, near = jax.ShapeDtypeStruct, pltpu.VMEM

    own = cotangent[0]
    far = lax.ppermute(own, "seq", [(s, (s + STRIDE) % n) for s in range(n)])
    (copies,) = call(
        spread_kernel,
        [shape((n, 1, rb), jnp.int32)],
        bases,
        far=(0,),
        away=(0,),
        scratch=[pltpu.SemaphoreType.DMA((n,))],
        name="spread",
    )
    gathered = lax.all_to_all(copies, "seq", 0, 0, tiled=True)

    taps = pltpu.VMEM((3 * width, mid), BF16)
    act0, table, w2 = call(
        table_kernel,
        [
            shape((CLASSES, mid), BF16),
            pltpu.VMEM((CLASSES, width + 4 * mid), F32),
            pltpu.VMEM((3 * width, mid), BF16),
        ],
        embed, conv_weight, point_weight,
        far=(0, 1, 2),
        whole=(0,),
        scratch=[taps, taps, pltpu.VMEM((mid, width), BF16), pltpu.SemaphoreType.DMA((8,))],
        limit=20,
        flops=4 * CLASSES * 3 * width * mid,
        name="tables",
    )
    features, conv, points, other, h, c, w1, p0 = call(
        lambda *refs: main_kernel(crow, prow, *refs),
        [
            shape((rb, width), F32),
            near((2, STRIDE * crow, mid), F32),
            near((2, STRIDE * prow, mid), F32),
            near((STRIDE * part, mid), BF16),
            near((3 * CLASSES, mid), BF16),
            near((CLASSES, width), F32),
            near((3 * width, mid), BF16),
            near((mid, width), BF16),
        ],
        gathered, own, far, conv_weight, point_weight, w2, table,
        far=(3, 4),
        scratch=[
            pltpu.VMEM((rows, 3 * CLASSES), BF16),
            pltpu.VMEM((rows, width), F32),
            pltpu.VMEM((rows, width), BF16),
            pltpu.VMEM((rows, mid), BF16),
            pltpu.VMEM((rows, mid), BF16),
            pltpu.VMEM((rows, mid), F32),
            pltpu.VMEM((rows, mid), F32),
            pltpu.VMEM((rows, width), BF16),
            pltpu.VMEM((rows, mid), BF16),
            pltpu.VMEM((rows, width), BF16),
            pltpu.VMEM((CLASSES, width), BF16),
            pltpu.VMEM((2, mid, width), BF16),
            pltpu.VMEM((rb, width), F32),
            pltpu.SemaphoreType.DMA((5,)),
        ],
        away=(0,),
        flops=9 * rows * 3 * width * mid,
        name="tower",
    )

    swap = [(s, s ^ 1) for s in range(n)]
    got = lax.ppermute(other, "seq", swap)
    small_rows = 8 * STRIDE + 16
    mine_small, other_small = call(
        lambda *refs: class_kernel(prow, *refs),
        [near((small_rows, mid), F32), near((small_rows, mid), BF16)],
        h, c, table, w1, p0,
        scratch=[pltpu.VMEM((width, CLASSES), F32)],
        flops=4 * CLASSES * 3 * width * mid,
        name="classes",
    )
    got_small = lax.ppermute(other_small, "seq", swap)
    peers = STRIDE // 2 * dp
    pieces = call(
        lambda *refs: message_kernel(crow, prow, *refs),
        [shape((part + 32, mid), F32 if i == 0 else BF16) for i in range(peers)],
        conv, points, got, mine_small, got_small,
        name="messages",
    )
    arrived = []
    for mask in ORDER:
        route = [
            (s * dp + d, (s ^ (2 * (mask // dp))) * dp + (d ^ (mask % dp)))
            for s in range(n)
            for d in range(dp)
        ]
        arrived.append(lax.ppermute(pieces[mask], ("seq", "dp"), route))
    total, send, rest = call(
        sum_kernel,
        [shape((part, mid), F32), shape((part, mid), BF16), shape((32, mid), F32)],
        pieces[0], *arrived,
        name="sums",
    )
    swapped = lax.ppermute(send, "dp", [(d, d ^ 1) for d in range(dp)])

    stream_e = embed.astype(F32)
    normed_e = (stream_e * norm_scale(stream_e)).astype(BF16)
    spread = jnp.concatenate(
        [jnp.pad(normed_e, ((4 * j, 12 - 4 * j), (0, 0))) for j in range(3)], axis=1
    )
    spread = lax.dynamic_slice_in_dim(spread, k * crow, crow, axis=1).T
    conv_grad, point_grad, embed_full, bt = call(
        small_kernel,
        [
            shape((3, crow, mid), F32),
            shape((3, prow, mid), F32),
            shape((4, width), F32),
            shape((4, prow), F32),
        ],
        rest, total, embed, conv_weight, act0, spread,
        far=(3,),
        away=(0, 1),
        scratch=[
            pltpu.VMEM((3 * width, mid), BF16),
            pltpu.VMEM((crow, mid), F32),
            pltpu.VMEM((prow, mid), F32),
            pltpu.SemaphoreType.DMA((7,)),
        ],
        name="layer0",
    )
    embed_grad = bt + lax.dynamic_slice_in_dim(embed_full, k * prow, prow, axis=1)
    conv_grad, point_grad = call(
        finish_kernel,
        [shape((3, crow, mid), F32), shape((3, prow, mid), F32)],
        swapped, conv_grad, point_grad,
        far=(1, 2),
        away=(0, 1),
        aliases={1: 0, 2: 1},
        scratch=[pltpu.VMEM((part, mid), F32), pltpu.SemaphoreType.DMA((2,))],
        name="finish",
    )
    return features[None], conv_grad, point_grad.transpose(0, 2, 1), embed_grad


def solution(mesh):
    in_specs = (P("dp", "seq"), P(), P(), P(), P("dp", "seq", None))
    out_specs = (P("dp", "seq", None), P(None, "seq", None), P(None, None, "seq"), P(None, "seq"))
    return jax.shard_map(
        on_device, mesh=mesh, in_specs=in_specs, out_specs=out_specs, check_vma=False
    )
```

```python
import math

import jax
import jax.numpy as jnp
import numpy as np
from jax import lax
from jax.experimental import pallas as pl
from jax.experimental.pallas import tpu as pltpu
from jax.sharding import PartitionSpec as P

BF16 = jnp.bfloat16
F32 = jnp.float32
CLASSES = 128
STRIDE = 8
ORDER = (3, 4, 5, 2, 1, 6, 7)


def gelu_pair(v):
    coef = math.sqrt(2.0 / math.pi)
    inner = coef * (v + 0.044715 * v * v * v)
    t = jnp.tanh(inner)
    slope = 0.5 * (1.0 + t) + 0.5 * v * (1.0 - t * t) * coef * (1.0 + 3.0 * 0.044715 * v * v)
    return 0.5 * v * (1.0 + t), slope


def mm(a, b):
    return jnp.dot(a, b, preferred_element_type=F32)


def mm_tn(a, b):
    return lax.dot_general(a, b, (((0,), (0,)), ((), ())), preferred_element_type=F32)


def mm_nt(a, b):
    return lax.dot_general(a, b, (((1,), (1,)), ((), ())), preferred_element_type=F32)


def halves(v):
    high = lax.reduce_precision(v, 8, 7)
    return high.astype(BF16), (v - high).astype(BF16)


def selectors():
    c = np.arange(CLASSES)
    digits = (c // 20, (c // 5) % 4, c % 5)
    valid = (c < 100)[:, None]
    return [((d[:, None] == np.arange(4)[None, :]) & valid).astype(np.float32) for d in digits]


def norm_scale(v):
    return lax.rsqrt(jnp.mean(v * v, axis=-1, keepdims=True) + 1e-06)


def tables(embed, conv_weight, point_weight):
    sel = [jnp.asarray(s, BF16) for s in selectors()]
    stream = embed.astype(F32)
    scale_e = norm_scale(stream)
    normed_e = (stream * scale_e).astype(BF16)
    taps = jnp.concatenate([mm(s, normed_e).astype(BF16) for s in sel], axis=1)
    act0, slope0 = gelu_pair(mm(taps, conv_weight[0]))
    act0 = act0.astype(BF16)
    stab = mm(sel[1], embed) + mm(act0, point_weight[0])
    scale1 = norm_scale(stab)
    ntab = (stab * scale1).astype(BF16)
    width = embed.shape[1]
    u = jnp.concatenate([mm(ntab, conv_weight[1, j * width : (j + 1) * width]) for j in range(3)])
    return stream, scale_e, normed_e, act0, slope0, stab, scale1, ntab, u


def classes(gathered, dil):
    n, rb = gathered.shape
    edge = jnp.full((1, dil), 4, jnp.int32)
    left = jnp.concatenate(
        [jnp.concatenate([edge, gathered[:-1, rb - dil :]]), gathered[:, : rb - dil]], axis=1
    )
    right = jnp.concatenate(
        [gathered[:, dil:], jnp.concatenate([gathered[1:, :dil], edge])], axis=1
    )
    cls = left * 20 + gathered * 5 + right
    none = jnp.full((2, rb), -1, jnp.int32)
    return jnp.concatenate([none, cls, none])


def general(bases, embed, conv_weight, point_weight, cotangent):
    n, dp = lax.axis_size("seq"), lax.axis_size("dp")
    rb, width, mid = bases.shape[1], embed.shape[1], conv_weight.shape[2]
    group = n // STRIDE
    k, x = lax.axis_index("seq"), lax.axis_index("dp")
    zh, r = k // STRIDE, k % STRIDE
    m, core = r // 2, r % 2
    rows = group * rb
    w1, w2 = conv_weight[1], conv_weight[2]
    p0, p1, p2 = point_weight[0], point_weight[1], point_weight[2]

    gathered = lax.all_to_all(jnp.broadcast_to(bases, (n, rb)), "seq", 0, 0, tiled=True)
    own = cotangent[0]
    parts = [own]
    for i in range(1, group):
        parts.append(lax.ppermute(own, "seq", [(s, (s - STRIDE * i) % n) for s in range(n)]))
    cot = lax.dynamic_slice_in_dim(
        jnp.concatenate(parts + parts), ((group - zh) % group) * rb, rows
    )

    stream_e, scale_e, normed_e, act0, slope0, stab, scale1, ntab, u = tables(
        embed, conv_weight, point_weight
    )
    u_high, u_low = halves(u)
    s_high, s_low = halves(stab)

    cls = classes(gathered, rb // 8)
    hots = []
    for j in range(3):
        index = jnp.concatenate(
            [lax.dynamic_slice(cls, (a * STRIDE + r + 2 * j, 0), (1, rb)) for a in range(group)],
            axis=1,
        )
        hots.append((jnp.arange(CLASSES, dtype=jnp.int32)[:, None] == index).astype(BF16))
    hot = jnp.concatenate(hots)

    pre1 = mm_tn(hot, u_high) + mm_tn(hot, u_low)
    act1, slope1 = gelu_pair(pre1)
    act1 = act1.astype(BF16)
    stream2 = mm_tn(hots[1], s_high) + mm_tn(hots[1], s_low) + mm(act1, p1)
    scale2 = norm_scale(stream2)
    normed2 = (stream2 * scale2).astype(BF16)
    nothing = jnp.zeros((rb, width), BF16)
    taps2 = jnp.concatenate(
        [
            jnp.concatenate([nothing, normed2[: rows - rb]]),
            normed2,
            jnp.concatenate([normed2[rb:], nothing]),
        ],
        axis=1,
    )
    pre2 = mm(taps2, w2)
    act2, slope2 = gelu_pair(pre2)
    act2 = act2.astype(BF16)
    features = lax.dynamic_slice_in_dim(stream2, zh * rb, rb) + mm(
        lax.dynamic_slice_in_dim(act2, zh * rb, rb), p2
    )

    grad2 = (mm_nt(cot, p2) * slope2).astype(BF16)
    nothing = jnp.zeros((rb, mid), BF16)
    above = jnp.concatenate([grad2[rb:], nothing])
    below = jnp.concatenate([nothing, grad2[: rows - rb]])
    ng2 = (
        mm_nt(above, w2[:width]) + mm_nt(grad2, w2[width : 2 * width]) + mm_nt(below, w2[2 * width :])
    )
    inner = jnp.mean(ng2 * stream2, axis=-1, keepdims=True)
    back2 = cot.astype(F32) + scale2 * (ng2 - stream2 * scale2 * scale2 * inner)
    back2 = back2.astype(BF16)
    grad1 = (mm_nt(back2, p1) * slope1).astype(BF16)

    h = mm(hot, grad1).astype(BF16)
    ng1 = sum(
        mm_nt(h[j * CLASSES : (j + 1) * CLASSES], w1[j * width : (j + 1) * width]) for j in range(3)
    )
    inner = jnp.mean(ng1 * stab, axis=-1, keepdims=True)
    b = mm(hots[1], back2) + scale1 * (ng1 - stab * scale1 * scale1 * inner)
    b16 = b.astype(BF16)
    s = (mm_nt(b16, p0) * slope0).astype(BF16)
    sel = selectors()
    g = mm(jnp.asarray(np.concatenate([v.T for v in sel]), BF16), s)
    bt = mm(jnp.asarray(sel[1].T, BF16), b16)
    small = jnp.concatenate([g, bt.reshape(2 * 4, mid)])

    crow, prow = 3 * width // n, width // n
    conv1 = jnp.concatenate(
        [mm_tn(ntab, h[j * CLASSES : (j + 1) * CLASSES]) for j in range(3)]
    )
    conv1 = lax.dynamic_slice_in_dim(conv1, zh * STRIDE * crow, STRIDE * crow)
    conv2 = mm_tn(lax.dynamic_slice_in_dim(taps2, zh * STRIDE * crow, STRIDE * crow, axis=1), grad2)

    def share(v):
        return lax.dynamic_slice_in_dim(v, zh * STRIDE * prow, STRIDE * prow, axis=1)

    point = [mm_tn(share(b16), act0), mm_tn(share(back2), act1), mm_tn(share(cot), act2)]
    tile = jnp.concatenate(
        [conv1.reshape(STRIDE, crow, mid), conv2.reshape(STRIDE, crow, mid)]
        + [v.reshape(STRIDE, prow, mid) for v in point],
        axis=1,
    )
    trow = 2 * crow + 3 * prow
    half = STRIDE // 2
    tile = tile.reshape(half, 2, trow, mid)

    swap = [(s, s ^ 1) for s in range(n)]
    mine = lax.dynamic_index_in_dim(tile, core, axis=1, keepdims=False)
    other = lax.dynamic_index_in_dim(tile, 1 - core, axis=1, keepdims=False)
    mine = mine + lax.ppermute(other.astype(BF16), "seq", swap).astype(F32)
    small = small + lax.ppermute(small.astype(BF16), "seq", swap).astype(F32)

    drow = trow // dp
    mine = mine.reshape(half, dp, drow, mid)
    small16 = small.astype(BF16)
    total = lax.dynamic_slice(mine, (m, x, 0, 0), (1, 1, drow, mid))[0, 0]
    for mask in range(half * dp - 1, 0, -1):
        mm_, mx = mask // dp, mask % dp
        piece = lax.dynamic_slice(mine, (m ^ mm_, x ^ mx, 0, 0), (1, 1, drow, mid))[0, 0]
        message = jnp.concatenate([piece.astype(BF16), small16])
        route = [
            (s * dp + d, (s ^ (2 * mm_)) * dp + (d ^ mx)) for s in range(n) for d in range(dp)
        ]
        got = lax.ppermute(message, ("seq", "dp"), route).astype(F32)
        total = total + got[:drow]
        small = small + got[drow:]

    total16 = total.astype(BF16)
    pieces = [total16] + [
        lax.ppermute(total16, "dp", [(d, d ^ i) for d in range(dp)]) for i in range(1, dp)
    ]
    full = jnp.concatenate(
        [
            sum(jnp.where((x ^ i) == d, pieces[i].astype(F32), 0.0) for i in range(dp))
            for d in range(dp)
        ]
    )

    g, bt = small[:12], small[12:].reshape(4, width)
    ng0 = sum(
        mm_nt(g[4 * j : 4 * j + 4].astype(BF16), conv_weight[0, j * width : (j + 1) * width])
        for j in range(3)
    )
    inner = jnp.mean(ng0 * stream_e, axis=-1, keepdims=True)
    embed_grad = bt + scale_e * (ng0 - stream_e * scale_e * scale_e * inner)
    embed_grad = lax.dynamic_slice_in_dim(embed_grad, k * prow, prow, axis=1)
    spread = jnp.concatenate(
        [
            jnp.pad(normed_e, ((4 * j, 8 - 4 * j), (0, 0))) for j in range(3)
        ],
        axis=1,
    )
    spread = lax.dynamic_slice_in_dim(spread, k * crow, crow, axis=1)
    conv0 = mm_tn(spread, g.astype(BF16))
    conv_grad = jnp.stack([conv0, full[:crow], full[crow : 2 * crow]])
    point_grad = full[2 * crow :].reshape(3, prow, mid).transpose(0, 2, 1)
    return features[None], conv_grad, point_grad, embed_grad


def normal(v):
    return (v * norm_scale(v)).astype(BF16)


def spread_kernel(bases_ref, out_ref):
    for i in range(out_ref.shape[0]):
        out_ref[i] = bases_ref[...]


def fetch(source, target, sem):
    copy = pltpu.make_async_copy(source, target, sem)
    copy.start()
    return copy


def fetch_taps(w_ref, layer, held_ref, sems, first, order=(0, 1, 2)):
    width = held_ref.shape[0] // 3
    copies = {}
    for j in order:
        at = pl.ds(j * width, width)
        copies[j] = fetch(w_ref.at[layer, at, :], held_ref.at[at, :], sems.at[first + j])
    return copies


def digits(shape, axis):
    c = lax.broadcasted_iota(jnp.int32, shape, axis).astype(F32)
    left, both = jnp.floor((c + 0.5) / 20.0), jnp.floor((c + 0.5) / 5.0)
    return c < 100.0, (left, both - 4.0 * left, c - 5.0 * both)


def digit_columns():
    valid, values = digits((CLASSES, 4), 0)
    base = lax.broadcasted_iota(jnp.int32, (CLASSES, 4), 1).astype(F32)
    return [jnp.where(valid & (v == base), 1.0, 0.0).astype(BF16) for v in values]


def digit_rows():
    valid, values = digits((16, CLASSES), 1)
    row = lax.broadcasted_iota(jnp.int32, (16, CLASSES), 0).astype(F32)
    hit = (values[0] == row) & (row < 4.0)
    hit |= (values[1] + 4.0 == row) & (row >= 4.0) & (row < 8.0)
    hit |= (values[2] + 8.0 == row) & (row >= 8.0) & (row < 12.0)
    return jnp.where(valid & hit, 1.0, 0.0).astype(BF16)


def table_kernel(embed_ref, w_ref, p_ref, act0_ref, table_ref, w2_ref, w0_ref, w1_ref, p0_ref, sems):
    width, mid = embed_ref.shape[1], act0_ref.shape[1]
    copy_w0 = fetch_taps(w_ref, 0, w0_ref, sems, 0)
    copy_p0 = fetch(p_ref.at[0], p0_ref, sems.at[6])
    copy_w1 = fetch_taps(w_ref, 1, w1_ref, sems, 3)
    copy_w2 = fetch(w_ref.at[2], w2_ref, sems.at[7])
    normed_e = normal(embed_ref[...].astype(F32))
    sel = digit_columns()
    pre = None
    for j in range(3):
        taps = mm(sel[j], normed_e).astype(BF16)
        copy_w0[j].wait()
        term = mm(taps, w0_ref[j * width : (j + 1) * width, :])
        pre = term if pre is None else pre + term
    act0, slope0 = gelu_pair(pre)
    act0 = act0.astype(BF16)
    act0_ref[...] = act0
    copy_p0.wait()
    stab = mm(sel[1], embed_ref[...]) + mm(act0, p0_ref[...])
    table_ref[:, :width] = stab
    table_ref[:, width : width + mid] = slope0
    ntab = normal(stab)
    for j in range(3):
        copy_w1[j].wait()
        at = width + (j + 1) * mid
        table_ref[:, at : at + mid] = mm(ntab, w1_ref[j * width : (j + 1) * width, :])
    copy_w2.wait()


def main_kernel(
    crow, prow, bases_ref, own_ref, far_ref, w_ref, p_ref, w2_ref, table_ref,
    features_ref, mine_ref, other_ref, h_ref, c_ref, w1_ref, p0_ref,
    hot_ref, stream_ref, normed_ref, act1_ref, act2_ref, slope1_ref, slope2_ref,
    cot_ref, grad_ref, back_ref, conv_ref, point_ref, ntab_ref, pt_ref, sent_ref, sems,
):
    n, _, rb = bases_ref.shape
    rows, width = stream_ref.shape
    mid = act1_ref.shape[1]
    dil, half = rb // 8, width // 2
    k = lax.axis_index("seq")
    zh, r, core = k // STRIDE, k % STRIDE, k % 2
    place = pl.ds(pl.multiple_of(zh * rb, 16), rb)
    far = pl.ds(pl.multiple_of((1 - zh) * rb, 16), rb)
    copy_p1 = fetch(p_ref.at[1], pt_ref.at[0], sems.at[0])
    copy_p2 = fetch(p_ref.at[2], pt_ref.at[1], sems.at[1])
    copy_w1 = fetch(w_ref.at[1], w1_ref, sems.at[2])
    copy_p0 = fetch(p_ref.at[0], p0_ref, sems.at[3])
    held = jnp.concatenate([bases_ref[i] for i in range(n)])
    held = (held - 4).astype(F32)
    edge = jnp.zeros((1, rb), F32)
    held = jnp.concatenate(
        [
            jnp.concatenate([edge, held[:-1]]).astype(BF16),
            held.astype(BF16),
            jnp.concatenate([held[1:], edge]).astype(BF16),
        ]
    )
    ahead = lax.broadcasted_iota(jnp.int32, (rb, rb), 0) - lax.broadcasted_iota(jnp.int32, (rb, rb), 1)

    def weight(gap):
        value = jnp.where(gap == -dil, 20.0, jnp.where(gap == 0, 5.0, jnp.where(gap == dil, 1.0, 0.0)))
        return value.astype(BF16)

    cls = (
        mm(held[:n], weight(ahead - rb)) + mm(held[n : 2 * n], weight(ahead)) + mm(held[2 * n :], weight(ahead + rb))
        + 105.0
    ).astype(BF16)
    block = lax.broadcasted_iota(jnp.int32, (n, CLASSES), 0)
    slot = lax.broadcasted_iota(jnp.int32, (n, CLASSES), 1)
    wanted = (slot // 3) * STRIDE + r + 2 * (slot % 3) - 2
    pick = jnp.where((block == wanted) & (slot < 6), 1.0, 0.0).astype(BF16)
    column = mm_tn(cls, pick)
    lanes = (lax.broadcasted_iota(jnp.int32, (rb, CLASSES), 1) + 1).astype(F32)
    for a in range(2):
        for j in range(3):
            i = 3 * a + j
            hot_ref[a * rb : (a + 1) * rb, j * CLASSES : (j + 1) * CLASSES] = jnp.where(
                lanes == column[:, i : i + 1], 1.0, 0.0
            ).astype(BF16)

    hot = hot_ref[...]
    mid_hot = hot[:, CLASSES : 2 * CLASSES]
    u = jnp.concatenate(
        [table_ref[:, width + (j + 1) * mid : width + (j + 2) * mid] for j in range(3)]
    )
    u_high = u.astype(BF16)
    act1, slope1 = gelu_pair(mm(hot, u_high) + mm(hot, (u - u_high.astype(F32)).astype(BF16)))
    act1 = act1.astype(BF16)
    act1_ref[...] = act1
    slope1_ref[...] = slope1
    stab = table_ref[:, :width]
    s_high = stab.astype(BF16)
    stream = mm(mid_hot, s_high) + mm(mid_hot, (stab - s_high.astype(F32)).astype(BF16))
    copy_p1.wait()
    stream = stream + mm(act1, pt_ref[0])
    stream_ref[...] = stream
    normed = normal(stream)
    normed_ref[...] = normed
    sides = jnp.concatenate(
        [mm(normed[rb:], w2_ref[2 * width :, :]), mm(normed[:rb], w2_ref[:width, :])]
    )
    act2, slope2 = gelu_pair(mm(normed, w2_ref[width : 2 * width, :]) + sides)
    act2_ref[...] = act2.astype(BF16)
    slope2_ref[...] = slope2
    copy_p2.wait()
    sent_ref[...] = stream_ref[place, :] + mm(act2_ref[place, :], pt_ref[1])
    copy_features = fetch(sent_ref, features_ref, sems.at[4])

    cot_ref[place, :] = own_ref[...]
    cot_ref[far, :] = far_ref[...]
    grad2 = (mm_nt(cot_ref[...], pt_ref[1]) * slope2_ref[...]).astype(BF16)
    grad_ref[...] = grad2
    sides = jnp.concatenate(
        [mm_nt(grad2[rb:], w2_ref[:width, :]), mm_nt(grad2[:rb], w2_ref[2 * width :, :])]
    )
    ng = mm_nt(grad2, w2_ref[width : 2 * width, :]) + sides
    stream = stream_ref[...]
    scale = norm_scale(stream)
    inner = jnp.mean(ng * stream, axis=-1, keepdims=True)
    back = cot_ref[...].astype(F32) + scale * (ng - stream * (scale * scale * inner))
    back = back.astype(BF16)
    back_ref[...] = back
    grad1 = (mm_nt(back, pt_ref[0]) * slope1_ref[...]).astype(BF16)

    h = mm_tn(hot_ref[...], grad1).astype(BF16)
    h_ref[...] = h
    h = [h[j * CLASSES : (j + 1) * CLASSES] for j in range(3)]
    c_ref[...] = mm_tn(hot_ref[:, CLASSES : 2 * CLASSES], back)
    ntab_ref[...] = normal(table_ref[:, :width])

    columns = pl.ds(pl.multiple_of(zh * half, 128), half)
    side_at = pl.ds(pl.multiple_of(zh * half, 16), width)
    center_at = pl.ds(pl.multiple_of((1 - zh) * width, 16), half)
    conv_ref[0, side_at, :] = mm_tn(ntab_ref[...], jnp.where(zh == 0, h[0], h[2]))
    conv_ref[0, center_at, :] = mm_tn(ntab_ref[:, columns], h[1])
    conv_ref[1, side_at, :] = mm_tn(normed_ref[place, :], grad_ref[far, :])
    conv_ref[1, center_at, :] = mm_tn(normed_ref[:, columns], grad_ref[...])
    point_ref[0] = mm_tn(back_ref[:, columns], act1_ref[...])
    point_ref[1] = mm_tn(cot_ref[:, columns], act2_ref[...])
    part = crow + prow
    for target, side in ((mine_ref, core), (other_ref, 1 - core)):
        for m in range(STRIDE // 2):
            tile = 2 * m + side
            crows = pl.ds(pl.multiple_of(tile * crow, 16), crow)
            prows = pl.ds(pl.multiple_of(tile * prow, 16), prow)
            for layer in range(2):
                at = (2 * m + layer) * part
                target[at : at + crow, :] = conv_ref[layer, crows, :].astype(target.dtype)
                target[at + crow : at + part, :] = point_ref[layer, prows, :].astype(target.dtype)
    for copy in (copy_features, copy_w1, copy_p0):
        copy.wait()


def class_kernel(prow, h_ref, c_ref, table_ref, w1_ref, p0_ref, mine_ref, other_ref, bt_ref):
    width, mid = c_ref.shape[1], h_ref.shape[1]
    half = width // 2
    k = lax.axis_index("seq")
    zh, core = k // STRIDE, k % 2
    ng = None
    for j in range(3):
        term = mm_nt(
            h_ref[j * CLASSES : (j + 1) * CLASSES, :], w1_ref[j * width : (j + 1) * width, :]
        )
        ng = term if ng is None else ng + term
    stab = table_ref[:, :width]
    scale = norm_scale(stab)
    inner = jnp.mean(ng * stab, axis=-1, keepdims=True)
    b = c_ref[...] + scale * (ng - stab * (scale * scale * inner))
    s = (mm_nt(b.astype(BF16), p0_ref[...]) * table_ref[:, width : width + mid]).astype(BF16)
    g = mm(digit_rows(), s)
    bt_ref[...] = jnp.transpose(b)
    for target, side in ((mine_ref, core), (other_ref, 1 - core)):
        for m in range(STRIDE // 2):
            for q in range(3):
                at = pl.ds(pl.multiple_of(zh * half + (2 * m + side) * prow + 16 * q, 16), 16)
                target[16 * m : 16 * m + 16, q * CLASSES : (q + 1) * CLASSES] = bt_ref[at, :].astype(
                    target.dtype
                )
        target[8 * STRIDE : 8 * STRIDE + 16, :] = g.astype(target.dtype)


def message_kernel(part, mine_ref, other_ref, mine_small_ref, other_small_ref, *out_refs):
    k, x = lax.axis_index("seq"), lax.axis_index("dp")
    m = (k % STRIDE) // 2
    end = 8 * STRIDE
    g = mine_small_ref[end:, :] + other_small_ref[end:, :].astype(F32)
    for mask, out_ref in enumerate(out_refs):
        target, layer = m ^ (mask // 2), x ^ (mask % 2)
        at = pl.ds(pl.multiple_of((2 * target + layer) * part, 16), part)
        out_ref[:part, :] = (mine_ref[at, :] + other_ref[at, :].astype(F32)).astype(out_ref.dtype)
        at = pl.ds(pl.multiple_of(target * 16, 16), 16)
        small = mine_small_ref[at, :] + other_small_ref[at, :].astype(F32)
        out_ref[part : part + 16, :] = small.astype(out_ref.dtype)
        out_ref[part + 16 :, :] = g.astype(out_ref.dtype)


def sum_kernel(own_ref, *refs):
    got, (total_ref, send_ref, rest_ref) = refs[:-3], refs[-3:]
    part = total_ref.shape[0]
    total = own_ref[...]
    for ref in got:
        total = total + ref[...].astype(F32)
    total_ref[...] = total[:part]
    send_ref[...] = total[:part].astype(BF16)
    rest_ref[...] = total[part:]


def small_kernel(
    rest_ref, total_ref, embed_ref, w_ref, act0_ref, spread_ref,
    conv_ref, point_ref, embed_out_ref, bt_ref, w0_ref, conv0_ref, point0_ref, sems,
):
    copy_w0 = fetch_taps(w_ref, 0, w0_ref, sems, 0)
    width = embed_ref.shape[1]
    crow = conv_ref.shape[1]
    own = lax.axis_index("dp") + 1
    copies = [
        fetch(total_ref.at[pl.ds(0, crow), :], conv_ref.at[own], sems.at[3]),
        fetch(total_ref.at[pl.ds(crow, point_ref.shape[1]), :], point_ref.at[own], sems.at[4]),
    ]
    g = rest_ref[16:, :]
    bt = jnp.concatenate([rest_ref[:16, q * CLASSES : (q + 1) * CLASSES] for q in range(3)])
    bt = bt.astype(BF16)
    g16 = g.astype(BF16)
    conv0_ref[...] = mm(spread_ref[...], g16)
    copies.append(fetch(conv0_ref, conv_ref.at[0], sems.at[5]))
    point0_ref[...] = mm(bt, act0_ref[...])
    copies.append(fetch(point0_ref, point_ref.at[0], sems.at[6]))
    bt_ref[...] = mm_nt(digit_rows(), bt)[4:8]
    stream = embed_ref[...].astype(F32)
    scale = norm_scale(stream)
    ng = None
    for j in range(3):
        copy_w0[j].wait()
        term = mm_nt(g16, w0_ref[j * width : (j + 1) * width, :])[4 * j : 4 * j + 4]
        ng = term if ng is None else ng + term
    inner = jnp.mean(ng * stream, axis=-1, keepdims=True)
    embed_out_ref[...] = scale * (ng - stream * (scale * scale * inner))
    for copy in copies:
        copy.wait()


def finish_kernel(got_ref, _, __, conv_ref, point_ref, held_ref, sems):
    crow = conv_ref.shape[1]
    other = 2 - lax.axis_index("dp")
    held_ref[...] = got_ref[...].astype(F32)
    copies = [
        fetch(held_ref.at[pl.ds(0, crow), :], conv_ref.at[other], sems.at[0]),
        fetch(held_ref.at[pl.ds(crow, point_ref.shape[1]), :], point_ref.at[other], sems.at[1]),
    ]
    for copy in copies:
        copy.wait()


def call(kernel, outs, *args, far=(), whole=(), away=(), scratch=(), limit=24, aliases=None, flops=0, name=None):
    args = [pltpu.with_memory_space_constraint(v, pltpu.HBM) if i in far else v for i, v in enumerate(args)]
    moved = sum(math.prod(v.shape) * jnp.dtype(v.dtype).itemsize for v in list(args) + list(outs))
    return pl.pallas_call(
        kernel,
        out_shape=outs,
        in_specs=[
            pl.BlockSpec(memory_space=pltpu.HBM if i in far and i not in whole else pltpu.VMEM)
            for i in range(len(args))
        ],
        out_specs=[
            pl.BlockSpec(memory_space=pltpu.HBM if i in away else pltpu.VMEM) for i in range(len(outs))
        ],
        scratch_shapes=list(scratch),
        input_output_aliases=aliases or {},
        compiler_params=pltpu.CompilerParams(vmem_limit_bytes=limit * 1024 * 1024),
        cost_estimate=pl.CostEstimate(flops=flops, bytes_accessed=moved, transcendentals=0),
        name=name,
    )(*args)


def on_device(bases, embed, conv_weight, point_weight, cotangent):
    n, dp = lax.axis_size("seq"), lax.axis_size("dp")
    rb, width, mid = bases.shape[1], embed.shape[1], conv_weight.shape[2]
    if n != 2 * STRIDE or dp != 2:
        return general(bases, embed, conv_weight, point_weight, cotangent)
    k = lax.axis_index("seq")
    zh, r = k // STRIDE, k % STRIDE
    rows = 2 * rb
    crow, prow = 3 * width // n, width // n
    part = crow + prow
    shape, near = jax.ShapeDtypeStruct, pltpu.VMEM

    own = cotangent[0]
    far = lax.ppermute(own, "seq", [(s, (s + STRIDE) % n) for s in range(n)])
    (copies,) = call(spread_kernel, [near((n, 1, rb), jnp.int32)], bases, far=(0,), whole=(0,), name="spread")
    gathered = lax.all_to_all(copies, "seq", 0, 0, tiled=True)

    taps = pltpu.VMEM((3 * width, mid), BF16)
    act0, table, w2 = call(
        table_kernel,
        [
            shape((CLASSES, mid), BF16),
            pltpu.VMEM((CLASSES, width + 4 * mid), F32),
            pltpu.VMEM((3 * width, mid), BF16),
        ],
        embed, conv_weight, point_weight,
        far=(0, 1, 2),
        whole=(0,),
        scratch=[taps, taps, pltpu.VMEM((mid, width), BF16), pltpu.SemaphoreType.DMA((8,))],
        limit=20,
        flops=4 * CLASSES * 3 * width * mid,
        name="tables",
    )
    features, mine, other, h, c, w1, p0 = call(
        lambda *refs: main_kernel(crow, prow, *refs),
        [
            shape((rb, width), F32),
            near((STRIDE * part, mid), F32),
            near((STRIDE * part, mid), BF16),
            near((3 * CLASSES, mid), BF16),
            near((CLASSES, width), F32),
            near((3 * width, mid), BF16),
            near((mid, width), BF16),
        ],
        gathered, own, far, conv_weight, point_weight, w2, table,
        far=(3, 4),
        scratch=[
            pltpu.VMEM((rows, 3 * CLASSES), BF16),
            pltpu.VMEM((rows, width), F32),
            pltpu.VMEM((rows, width), BF16),
            pltpu.VMEM((rows, mid), BF16),
            pltpu.VMEM((rows, mid), BF16),
            pltpu.VMEM((rows, mid), F32),
            pltpu.VMEM((rows, mid), F32),
            pltpu.VMEM((rows, width), BF16),
            pltpu.VMEM((rows, mid), BF16),
            pltpu.VMEM((rows, width), BF16),
            pltpu.VMEM((2, STRIDE * crow, mid), F32),
            pltpu.VMEM((2, STRIDE * prow, mid), F32),
            pltpu.VMEM((CLASSES, width), BF16),
            pltpu.VMEM((2, mid, width), BF16),
            pltpu.VMEM((rb, width), F32),
            pltpu.SemaphoreType.DMA((5,)),
        ],
        away=(0,),
        flops=9 * rows * 3 * width * mid,
        name="tower",
    )

    swap = [(s, s ^ 1) for s in range(n)]
    got = lax.ppermute(other, "seq", swap)
    small_rows = 8 * STRIDE + 16
    mine_small, other_small = call(
        lambda *refs: class_kernel(prow, *refs),
        [near((small_rows, mid), F32), near((small_rows, mid), BF16)],
        h, c, table, w1, p0,
        scratch=[pltpu.VMEM((width, CLASSES), F32)],
        flops=4 * CLASSES * 3 * width * mid,
        name="classes",
    )
    got_small = lax.ppermute(other_small, "seq", swap)
    peers = STRIDE // 2 * dp
    pieces = call(
        lambda *refs: message_kernel(part, *refs),
        [shape((part + 32, mid), F32 if i == 0 else BF16) for i in range(peers)],
        mine, got, mine_small, got_small,
        name="messages",
    )
    arrived = []
    for mask in ORDER:
        route = [
            (s * dp + d, (s ^ (2 * (mask // dp))) * dp + (d ^ (mask % dp)))
            for s in range(n)
            for d in range(dp)
        ]
        arrived.append(lax.ppermute(pieces[mask], ("seq", "dp"), route))
    total, send, rest = call(
        sum_kernel,
        [shape((part, mid), F32), shape((part, mid), BF16), shape((32, mid), F32)],
        pieces[0], *arrived,
        name="sums",
    )
    swapped = lax.ppermute(send, "dp", [(d, d ^ 1) for d in range(dp)])

    stream_e = embed.astype(F32)
    normed_e = (stream_e * norm_scale(stream_e)).astype(BF16)
    spread = jnp.concatenate(
        [jnp.pad(normed_e, ((4 * j, 12 - 4 * j), (0, 0))) for j in range(3)], axis=1
    )
    spread = lax.dynamic_slice_in_dim(spread, k * crow, crow, axis=1).T
    conv_grad, point_grad, embed_full, bt = call(
        small_kernel,
        [
            shape((3, crow, mid), F32),
            shape((3, prow, mid), F32),
            shape((4, width), F32),
            shape((4, prow), F32),
        ],
        rest, total, embed, conv_weight, act0, spread,
        far=(3,),
        away=(0, 1),
        scratch=[
            pltpu.VMEM((3 * width, mid), BF16),
            pltpu.VMEM((crow, mid), F32),
            pltpu.VMEM((prow, mid), F32),
            pltpu.SemaphoreType.DMA((7,)),
        ],
        name="layer0",
    )
    embed_grad = bt + lax.dynamic_slice_in_dim(embed_full, k * prow, prow, axis=1)
    conv_grad, point_grad = call(
        finish_kernel,
        [shape((3, crow, mid), F32), shape((3, prow, mid), F32)],
        swapped, conv_grad, point_grad,
        far=(1, 2),
        away=(0, 1),
        aliases={1: 0, 2: 1},
        scratch=[pltpu.VMEM((part, mid), F32), pltpu.SemaphoreType.DMA((2,))],
        name="finish",
    )
    return features[None], conv_grad, point_grad.transpose(0, 2, 1), embed_grad


def solution(mesh):
    in_specs = (P("dp", "seq"), P(), P(), P(), P("dp", "seq", None))
    out_specs = (P("dp", "seq", None), P(None, "seq", None), P(None, None, "seq"), P(None, "seq"))
    return jax.shard_map(
        on_device, mesh=mesh, in_specs=in_specs, out_specs=out_specs, check_vma=False
    )
```

```python
import math

import jax
import jax.numpy as jnp
import numpy as np
from jax import lax
from jax.experimental import pallas as pl
from jax.experimental.pallas import tpu as pltpu
from jax.sharding import PartitionSpec as P

BF16 = jnp.bfloat16
F32 = jnp.float32
CLASSES = 128
STRIDE = 8
ORDER = ((0, 6, 5, 3, 7, 1, 2, 4), (0, 1, 2, 4, 7, 6, 5, 3))


def gelu_pair(v):
    coef = math.sqrt(2.0 / math.pi)
    inner = coef * (v + 0.044715 * v * v * v)
    t = jnp.tanh(inner)
    slope = 0.5 * (1.0 + t) + 0.5 * v * (1.0 - t * t) * coef * (1.0 + 3.0 * 0.044715 * v * v)
    return 0.5 * v * (1.0 + t), slope


def mm(a, b):
    return jnp.dot(a, b, preferred_element_type=F32)


def mm_tn(a, b):
    return lax.dot_general(a, b, (((0,), (0,)), ((), ())), preferred_element_type=F32)


def mm_nt(a, b):
    return lax.dot_general(a, b, (((1,), (1,)), ((), ())), preferred_element_type=F32)


def halves(v):
    high = lax.reduce_precision(v, 8, 7)
    return high.astype(BF16), (v - high).astype(BF16)


def selectors():
    c = np.arange(CLASSES)
    digits = (c // 20, (c // 5) % 4, c % 5)
    valid = (c < 100)[:, None]
    return [((d[:, None] == np.arange(4)[None, :]) & valid).astype(np.float32) for d in digits]


def norm_scale(v):
    return lax.rsqrt(jnp.mean(v * v, axis=-1, keepdims=True) + 1e-06)


def tables(embed, conv_weight, point_weight):
    sel = [jnp.asarray(s, BF16) for s in selectors()]
    stream = embed.astype(F32)
    scale_e = norm_scale(stream)
    normed_e = (stream * scale_e).astype(BF16)
    taps = jnp.concatenate([mm(s, normed_e).astype(BF16) for s in sel], axis=1)
    act0, slope0 = gelu_pair(mm(taps, conv_weight[0]))
    act0 = act0.astype(BF16)
    stab = mm(sel[1], embed) + mm(act0, point_weight[0])
    scale1 = norm_scale(stab)
    ntab = (stab * scale1).astype(BF16)
    width = embed.shape[1]
    u = jnp.concatenate([mm(ntab, conv_weight[1, j * width : (j + 1) * width]) for j in range(3)])
    return stream, scale_e, normed_e, act0, slope0, stab, scale1, ntab, u


def classes(gathered, dil):
    n, rb = gathered.shape
    edge = jnp.full((1, dil), 4, jnp.int32)
    left = jnp.concatenate(
        [jnp.concatenate([edge, gathered[:-1, rb - dil :]]), gathered[:, : rb - dil]], axis=1
    )
    right = jnp.concatenate(
        [gathered[:, dil:], jnp.concatenate([gathered[1:, :dil], edge])], axis=1
    )
    cls = left * 20 + gathered * 5 + right
    none = jnp.full((2, rb), -1, jnp.int32)
    return jnp.concatenate([none, cls, none])


def general(bases, embed, conv_weight, point_weight, cotangent):
    n, dp = lax.axis_size("seq"), lax.axis_size("dp")
    rb, width, mid = bases.shape[1], embed.shape[1], conv_weight.shape[2]
    group = n // STRIDE
    k, x = lax.axis_index("seq"), lax.axis_index("dp")
    zh, r = k // STRIDE, k % STRIDE
    m, core = r // 2, r % 2
    rows = group * rb
    w1, w2 = conv_weight[1], conv_weight[2]
    p0, p1, p2 = point_weight[0], point_weight[1], point_weight[2]

    gathered = lax.all_to_all(jnp.broadcast_to(bases, (n, rb)), "seq", 0, 0, tiled=True)
    own = cotangent[0]
    parts = [own]
    for i in range(1, group):
        parts.append(lax.ppermute(own, "seq", [(s, (s - STRIDE * i) % n) for s in range(n)]))
    cot = lax.dynamic_slice_in_dim(
        jnp.concatenate(parts + parts), ((group - zh) % group) * rb, rows
    )

    stream_e, scale_e, normed_e, act0, slope0, stab, scale1, ntab, u = tables(
        embed, conv_weight, point_weight
    )
    u_high, u_low = halves(u)
    s_high, s_low = halves(stab)

    cls = classes(gathered, rb // 8)
    hots = []
    for j in range(3):
        index = jnp.concatenate(
            [lax.dynamic_slice(cls, (a * STRIDE + r + 2 * j, 0), (1, rb)) for a in range(group)],
            axis=1,
        )
        hots.append((jnp.arange(CLASSES, dtype=jnp.int32)[:, None] == index).astype(BF16))
    hot = jnp.concatenate(hots)

    pre1 = mm_tn(hot, u_high) + mm_tn(hot, u_low)
    act1, slope1 = gelu_pair(pre1)
    act1 = act1.astype(BF16)
    stream2 = mm_tn(hots[1], s_high) + mm_tn(hots[1], s_low) + mm(act1, p1)
    scale2 = norm_scale(stream2)
    normed2 = (stream2 * scale2).astype(BF16)
    nothing = jnp.zeros((rb, width), BF16)
    taps2 = jnp.concatenate(
        [
            jnp.concatenate([nothing, normed2[: rows - rb]]),
            normed2,
            jnp.concatenate([normed2[rb:], nothing]),
        ],
        axis=1,
    )
    pre2 = mm(taps2, w2)
    act2, slope2 = gelu_pair(pre2)
    act2 = act2.astype(BF16)
    features = lax.dynamic_slice_in_dim(stream2, zh * rb, rb) + mm(
        lax.dynamic_slice_in_dim(act2, zh * rb, rb), p2
    )

    grad2 = (mm_nt(cot, p2) * slope2).astype(BF16)
    nothing = jnp.zeros((rb, mid), BF16)
    above = jnp.concatenate([grad2[rb:], nothing])
    below = jnp.concatenate([nothing, grad2[: rows - rb]])
    ng2 = (
        mm_nt(above, w2[:width]) + mm_nt(grad2, w2[width : 2 * width]) + mm_nt(below, w2[2 * width :])
    )
    inner = jnp.mean(ng2 * stream2, axis=-1, keepdims=True)
    back2 = cot.astype(F32) + scale2 * (ng2 - stream2 * scale2 * scale2 * inner)
    back2 = back2.astype(BF16)
    grad1 = (mm_nt(back2, p1) * slope1).astype(BF16)

    h = mm(hot, grad1).astype(BF16)
    ng1 = sum(
        mm_nt(h[j * CLASSES : (j + 1) * CLASSES], w1[j * width : (j + 1) * width]) for j in range(3)
    )
    inner = jnp.mean(ng1 * stab, axis=-1, keepdims=True)
    b = mm(hots[1], back2) + scale1 * (ng1 - stab * scale1 * scale1 * inner)
    b16 = b.astype(BF16)
    s = (mm_nt(b16, p0) * slope0).astype(BF16)
    sel = selectors()
    g = mm(jnp.asarray(np.concatenate([v.T for v in sel]), BF16), s)
    bt = mm(jnp.asarray(sel[1].T, BF16), b16)
    small = jnp.concatenate([g, bt.reshape(2 * 4, mid)])

    crow, prow = 3 * width // n, width // n
    conv1 = jnp.concatenate(
        [mm_tn(ntab, h[j * CLASSES : (j + 1) * CLASSES]) for j in range(3)]
    )
    conv1 = lax.dynamic_slice_in_dim(conv1, zh * STRIDE * crow, STRIDE * crow)
    conv2 = mm_tn(lax.dynamic_slice_in_dim(taps2, zh * STRIDE * crow, STRIDE * crow, axis=1), grad2)

    def share(v):
        return lax.dynamic_slice_in_dim(v, zh * STRIDE * prow, STRIDE * prow, axis=1)

    point = [mm_tn(share(b16), act0), mm_tn(share(back2), act1), mm_tn(share(cot), act2)]
    tile = jnp.concatenate(
        [conv1.reshape(STRIDE, crow, mid), conv2.reshape(STRIDE, crow, mid)]
        + [v.reshape(STRIDE, prow, mid) for v in point],
        axis=1,
    )
    trow = 2 * crow + 3 * prow
    half = STRIDE // 2
    tile = tile.reshape(half, 2, trow, mid)

    swap = [(s, s ^ 1) for s in range(n)]
    mine = lax.dynamic_index_in_dim(tile, core, axis=1, keepdims=False)
    other = lax.dynamic_index_in_dim(tile, 1 - core, axis=1, keepdims=False)
    mine = mine + lax.ppermute(other.astype(BF16), "seq", swap).astype(F32)
    small = small + lax.ppermute(small.astype(BF16), "seq", swap).astype(F32)

    drow = trow // dp
    mine = mine.reshape(half, dp, drow, mid)
    small16 = small.astype(BF16)
    total = lax.dynamic_slice(mine, (m, x, 0, 0), (1, 1, drow, mid))[0, 0]
    for mask in range(half * dp - 1, 0, -1):
        mm_, mx = mask // dp, mask % dp
        piece = lax.dynamic_slice(mine, (m ^ mm_, x ^ mx, 0, 0), (1, 1, drow, mid))[0, 0]
        message = jnp.concatenate([piece.astype(BF16), small16])
        route = [
            (s * dp + d, (s ^ (2 * mm_)) * dp + (d ^ mx)) for s in range(n) for d in range(dp)
        ]
        got = lax.ppermute(message, ("seq", "dp"), route).astype(F32)
        total = total + got[:drow]
        small = small + got[drow:]

    total16 = total.astype(BF16)
    pieces = [total16] + [
        lax.ppermute(total16, "dp", [(d, d ^ i) for d in range(dp)]) for i in range(1, dp)
    ]
    full = jnp.concatenate(
        [
            sum(jnp.where((x ^ i) == d, pieces[i].astype(F32), 0.0) for i in range(dp))
            for d in range(dp)
        ]
    )

    g, bt = small[:12], small[12:].reshape(4, width)
    ng0 = sum(
        mm_nt(g[4 * j : 4 * j + 4].astype(BF16), conv_weight[0, j * width : (j + 1) * width])
        for j in range(3)
    )
    inner = jnp.mean(ng0 * stream_e, axis=-1, keepdims=True)
    embed_grad = bt + scale_e * (ng0 - stream_e * scale_e * scale_e * inner)
    embed_grad = lax.dynamic_slice_in_dim(embed_grad, k * prow, prow, axis=1)
    spread = jnp.concatenate(
        [
            jnp.pad(normed_e, ((4 * j, 8 - 4 * j), (0, 0))) for j in range(3)
        ],
        axis=1,
    )
    spread = lax.dynamic_slice_in_dim(spread, k * crow, crow, axis=1)
    conv0 = mm_tn(spread, g.astype(BF16))
    conv_grad = jnp.stack([conv0, full[:crow], full[crow : 2 * crow]])
    point_grad = full[2 * crow :].reshape(3, prow, mid).transpose(0, 2, 1)
    return features[None], conv_grad, point_grad, embed_grad


def normal(v):
    return (v * norm_scale(v)).astype(BF16)


def spread_kernel(bases_ref, out_ref):
    for i in range(out_ref.shape[0]):
        out_ref[i] = bases_ref[...]


def fetch(source, target, sem):
    copy = pltpu.make_async_copy(source, target, sem)
    copy.start()
    return copy


def fetch_taps(w_ref, layer, held_ref, sems, first, order=(0, 1, 2)):
    width = held_ref.shape[0] // 3
    copies = {}
    for j in order:
        at = pl.ds(j * width, width)
        copies[j] = fetch(w_ref.at[layer, at, :], held_ref.at[at, :], sems.at[first + j])
    return copies


def digits(shape, axis):
    c = lax.broadcasted_iota(jnp.int32, shape, axis).astype(F32)
    left, both = jnp.floor((c + 0.5) / 20.0), jnp.floor((c + 0.5) / 5.0)
    return c < 100.0, (left, both - 4.0 * left, c - 5.0 * both)


def digit_columns():
    valid, values = digits((CLASSES, 4), 0)
    base = lax.broadcasted_iota(jnp.int32, (CLASSES, 4), 1).astype(F32)
    return [jnp.where(valid & (v == base), 1.0, 0.0).astype(BF16) for v in values]


def digit_rows():
    valid, values = digits((16, CLASSES), 1)
    row = lax.broadcasted_iota(jnp.int32, (16, CLASSES), 0).astype(F32)
    hit = (values[0] == row) & (row < 4.0)
    hit |= (values[1] + 4.0 == row) & (row >= 4.0) & (row < 8.0)
    hit |= (values[2] + 8.0 == row) & (row >= 8.0) & (row < 12.0)
    return jnp.where(valid & hit, 1.0, 0.0).astype(BF16)


def table_kernel(embed_ref, w_ref, p_ref, act0_ref, table_ref, w2_ref, w0_ref, w1_ref, p0_ref, sems):
    width, mid = embed_ref.shape[1], act0_ref.shape[1]
    copy_w0 = fetch_taps(w_ref, 0, w0_ref, sems, 0)
    copy_p0 = fetch(p_ref.at[0], p0_ref, sems.at[6])
    copy_w1 = fetch_taps(w_ref, 1, w1_ref, sems, 3)
    copy_w2 = fetch(w_ref.at[2], w2_ref, sems.at[7])
    normed_e = normal(embed_ref[...].astype(F32))
    sel = digit_columns()
    pre = None
    for j in range(3):
        taps = mm(sel[j], normed_e).astype(BF16)
        copy_w0[j].wait()
        term = mm(taps, w0_ref[j * width : (j + 1) * width, :])
        pre = term if pre is None else pre + term
    act0, slope0 = gelu_pair(pre)
    act0 = act0.astype(BF16)
    act0_ref[...] = act0
    copy_p0.wait()
    stab = mm(sel[1], embed_ref[...]) + mm(act0, p0_ref[...])
    table_ref[:, :width] = stab
    table_ref[:, width : width + mid] = slope0
    ntab = normal(stab)
    for j in range(3):
        copy_w1[j].wait()
        at = width + (j + 1) * mid
        table_ref[:, at : at + mid] = mm(ntab, w1_ref[j * width : (j + 1) * width, :])
    copy_w2.wait()


def main_kernel(
    crow, prow, bases_ref, own_ref, far_ref, w_ref, p_ref, w2_ref, table_ref,
    features_ref, mine_ref, other_ref, h_ref, c_ref, w1_ref, p0_ref,
    hot_ref, stream_ref, normed_ref, act1_ref, act2_ref, slope1_ref, slope2_ref,
    cot_ref, grad_ref, back_ref, conv_ref, point_ref, ntab_ref, pt_ref, sent_ref, sems,
):
    n, _, rb = bases_ref.shape
    rows, width = stream_ref.shape
    mid = act1_ref.shape[1]
    dil, half = rb // 8, width // 2
    k = lax.axis_index("seq")
    zh, r, core = k // STRIDE, k % STRIDE, k % 2
    place = pl.ds(pl.multiple_of(zh * rb, 16), rb)
    far = pl.ds(pl.multiple_of((1 - zh) * rb, 16), rb)
    copy_p1 = fetch(p_ref.at[1], pt_ref.at[0], sems.at[0])
    copy_p2 = fetch(p_ref.at[2], pt_ref.at[1], sems.at[1])
    copy_w1 = fetch(w_ref.at[1], w1_ref, sems.at[2])
    copy_p0 = fetch(p_ref.at[0], p0_ref, sems.at[3])
    held = jnp.concatenate([bases_ref[i] for i in range(n)])
    held = (held - 4).astype(F32)
    edge = jnp.zeros((1, rb), F32)
    held = jnp.concatenate(
        [
            jnp.concatenate([edge, held[:-1]]).astype(BF16),
            held.astype(BF16),
            jnp.concatenate([held[1:], edge]).astype(BF16),
        ]
    )
    ahead = lax.broadcasted_iota(jnp.int32, (rb, rb), 0) - lax.broadcasted_iota(jnp.int32, (rb, rb), 1)

    def weight(gap):
        value = jnp.where(gap == -dil, 20.0, jnp.where(gap == 0, 5.0, jnp.where(gap == dil, 1.0, 0.0)))
        return value.astype(BF16)

    cls = (
        mm(held[:n], weight(ahead - rb)) + mm(held[n : 2 * n], weight(ahead)) + mm(held[2 * n :], weight(ahead + rb))
        + 105.0
    ).astype(BF16)
    block = lax.broadcasted_iota(jnp.int32, (n, CLASSES), 0)
    slot = lax.broadcasted_iota(jnp.int32, (n, CLASSES), 1)
    wanted = (slot // 3) * STRIDE + r + 2 * (slot % 3) - 2
    pick = jnp.where((block == wanted) & (slot < 6), 1.0, 0.0).astype(BF16)
    column = mm_tn(cls, pick)
    lanes = (lax.broadcasted_iota(jnp.int32, (rb, CLASSES), 1) + 1).astype(F32)
    for a in range(2):
        for j in range(3):
            i = 3 * a + j
            hot_ref[a * rb : (a + 1) * rb, j * CLASSES : (j + 1) * CLASSES] = jnp.where(
                lanes == column[:, i : i + 1], 1.0, 0.0
            ).astype(BF16)

    hot = hot_ref[...]
    mid_hot = hot[:, CLASSES : 2 * CLASSES]
    u = jnp.concatenate(
        [table_ref[:, width + (j + 1) * mid : width + (j + 2) * mid] for j in range(3)]
    )
    u_high = u.astype(BF16)
    act1, slope1 = gelu_pair(mm(hot, u_high) + mm(hot, (u - u_high.astype(F32)).astype(BF16)))
    act1 = act1.astype(BF16)
    act1_ref[...] = act1
    slope1_ref[...] = slope1
    stab = table_ref[:, :width]
    s_high = stab.astype(BF16)
    stream = mm(mid_hot, s_high) + mm(mid_hot, (stab - s_high.astype(F32)).astype(BF16))
    copy_p1.wait()
    stream = stream + mm(act1, pt_ref[0])
    stream_ref[...] = stream
    normed = normal(stream)
    normed_ref[...] = normed
    sides = jnp.concatenate(
        [mm(normed[rb:], w2_ref[2 * width :, :]), mm(normed[:rb], w2_ref[:width, :])]
    )
    act2, slope2 = gelu_pair(mm(normed, w2_ref[width : 2 * width, :]) + sides)
    act2_ref[...] = act2.astype(BF16)
    slope2_ref[...] = slope2
    copy_p2.wait()
    sent_ref[...] = stream_ref[place, :] + mm(act2_ref[place, :], pt_ref[1])
    copy_features = fetch(sent_ref, features_ref, sems.at[4])

    cot_ref[place, :] = own_ref[...]
    cot_ref[far, :] = far_ref[...]
    grad2 = (mm_nt(cot_ref[...], pt_ref[1]) * slope2_ref[...]).astype(BF16)
    grad_ref[...] = grad2
    sides = jnp.concatenate(
        [mm_nt(grad2[rb:], w2_ref[:width, :]), mm_nt(grad2[:rb], w2_ref[2 * width :, :])]
    )
    ng = mm_nt(grad2, w2_ref[width : 2 * width, :]) + sides
    stream = stream_ref[...]
    scale = norm_scale(stream)
    inner = jnp.mean(ng * stream, axis=-1, keepdims=True)
    back = cot_ref[...].astype(F32) + scale * (ng - stream * (scale * scale * inner))
    back = back.astype(BF16)
    back_ref[...] = back
    grad1 = (mm_nt(back, pt_ref[0]) * slope1_ref[...]).astype(BF16)

    h = mm_tn(hot_ref[...], grad1).astype(BF16)
    h_ref[...] = h
    h = [h[j * CLASSES : (j + 1) * CLASSES] for j in range(3)]
    c_ref[...] = mm_tn(hot_ref[:, CLASSES : 2 * CLASSES], back)
    ntab_ref[...] = normal(table_ref[:, :width])

    columns = pl.ds(pl.multiple_of(zh * half, 128), half)
    side_at = pl.ds(pl.multiple_of(zh * half, 16), width)
    center_at = pl.ds(pl.multiple_of((1 - zh) * width, 16), half)
    conv_ref[0, side_at, :] = mm_tn(ntab_ref[...], jnp.where(zh == 0, h[0], h[2]))
    conv_ref[0, center_at, :] = mm_tn(ntab_ref[:, columns], h[1])
    conv_ref[1, side_at, :] = mm_tn(normed_ref[place, :], grad_ref[far, :])
    conv_ref[1, center_at, :] = mm_tn(normed_ref[:, columns], grad_ref[...])
    point_ref[0] = mm_tn(back_ref[:, columns], act1_ref[...])
    point_ref[1] = mm_tn(cot_ref[:, columns], act2_ref[...])
    part = crow + prow
    for target, side in ((mine_ref, core), (other_ref, 1 - core)):
        for m in range(STRIDE // 2):
            tile = 2 * m + side
            crows = pl.ds(pl.multiple_of(tile * crow, 16), crow)
            prows = pl.ds(pl.multiple_of(tile * prow, 16), prow)
            for layer in range(2):
                at = (2 * m + layer) * part
                target[at : at + crow, :] = conv_ref[layer, crows, :].astype(target.dtype)
                target[at + crow : at + part, :] = point_ref[layer, prows, :].astype(target.dtype)
    for copy in (copy_features, copy_w1, copy_p0):
        copy.wait()


def class_kernel(prow, h_ref, c_ref, table_ref, w1_ref, p0_ref, mine_ref, other_ref, bt_ref):
    width, mid = c_ref.shape[1], h_ref.shape[1]
    half = width // 2
    k = lax.axis_index("seq")
    zh, core = k // STRIDE, k % 2
    ng = None
    for j in range(3):
        term = mm_nt(
            h_ref[j * CLASSES : (j + 1) * CLASSES, :], w1_ref[j * width : (j + 1) * width, :]
        )
        ng = term if ng is None else ng + term
    stab = table_ref[:, :width]
    scale = norm_scale(stab)
    inner = jnp.mean(ng * stab, axis=-1, keepdims=True)
    b = c_ref[...] + scale * (ng - stab * (scale * scale * inner))
    s = (mm_nt(b.astype(BF16), p0_ref[...]) * table_ref[:, width : width + mid]).astype(BF16)
    g = mm(digit_rows(), s)
    bt_ref[...] = jnp.transpose(b)
    for target, side in ((mine_ref, core), (other_ref, 1 - core)):
        for m in range(STRIDE // 2):
            for q in range(3):
                at = pl.ds(pl.multiple_of(zh * half + (2 * m + side) * prow + 16 * q, 16), 16)
                target[16 * m : 16 * m + 16, q * CLASSES : (q + 1) * CLASSES] = bt_ref[at, :].astype(
                    target.dtype
                )
        target[8 * STRIDE : 8 * STRIDE + 16, :] = g.astype(target.dtype)


def message_kernel(part, mine_ref, other_ref, mine_small_ref, other_small_ref, *out_refs):
    k, x = lax.axis_index("seq"), lax.axis_index("dp")
    m = (k % STRIDE) // 2
    end = 8 * STRIDE
    g = mine_small_ref[end:, :] + other_small_ref[end:, :].astype(F32)
    for i, out_ref in enumerate(out_refs):
        mask = jnp.where(k % 2 == 0, ORDER[0][i], ORDER[1][i])
        target, layer = m ^ (mask // 2), x ^ (mask % 2)
        at = pl.ds(pl.multiple_of((2 * target + layer) * part, 16), part)
        out_ref[:part, :] = (mine_ref[at, :] + other_ref[at, :].astype(F32)).astype(out_ref.dtype)
        at = pl.ds(pl.multiple_of(target * 16, 16), 16)
        small = mine_small_ref[at, :] + other_small_ref[at, :].astype(F32)
        out_ref[part : part + 16, :] = small.astype(out_ref.dtype)
        out_ref[part + 16 :, :] = g.astype(out_ref.dtype)


def sum_kernel(own_ref, *refs):
    got, (total_ref, send_ref, rest_ref) = refs[:-3], refs[-3:]
    part = total_ref.shape[0]
    total = own_ref[...]
    for ref in got:
        total = total + ref[...].astype(F32)
    total_ref[...] = total[:part]
    send_ref[...] = total[:part].astype(BF16)
    rest_ref[...] = total[part:]


def small_kernel(
    rest_ref, total_ref, embed_ref, w_ref, act0_ref, spread_ref,
    conv_ref, point_ref, embed_out_ref, bt_ref, w0_ref, conv0_ref, point0_ref, sems,
):
    copy_w0 = fetch_taps(w_ref, 0, w0_ref, sems, 0)
    width = embed_ref.shape[1]
    crow = conv_ref.shape[1]
    own = lax.axis_index("dp") + 1
    copies = [
        fetch(total_ref.at[pl.ds(0, crow), :], conv_ref.at[own], sems.at[3]),
        fetch(total_ref.at[pl.ds(crow, point_ref.shape[1]), :], point_ref.at[own], sems.at[4]),
    ]
    g = rest_ref[16:, :]
    bt = jnp.concatenate([rest_ref[:16, q * CLASSES : (q + 1) * CLASSES] for q in range(3)])
    bt = bt.astype(BF16)
    g16 = g.astype(BF16)
    conv0_ref[...] = mm(spread_ref[...], g16)
    copies.append(fetch(conv0_ref, conv_ref.at[0], sems.at[5]))
    point0_ref[...] = mm(bt, act0_ref[...])
    copies.append(fetch(point0_ref, point_ref.at[0], sems.at[6]))
    bt_ref[...] = mm_nt(digit_rows(), bt)[4:8]
    stream = embed_ref[...].astype(F32)
    scale = norm_scale(stream)
    ng = None
    for j in range(3):
        copy_w0[j].wait()
        term = mm_nt(g16, w0_ref[j * width : (j + 1) * width, :])[4 * j : 4 * j + 4]
        ng = term if ng is None else ng + term
    inner = jnp.mean(ng * stream, axis=-1, keepdims=True)
    embed_out_ref[...] = scale * (ng - stream * (scale * scale * inner))
    for copy in copies:
        copy.wait()


def finish_kernel(got_ref, _, __, conv_ref, point_ref, held_ref, sems):
    crow = conv_ref.shape[1]
    other = 2 - lax.axis_index("dp")
    held_ref[...] = got_ref[...].astype(F32)
    copies = [
        fetch(held_ref.at[pl.ds(0, crow), :], conv_ref.at[other], sems.at[0]),
        fetch(held_ref.at[pl.ds(crow, point_ref.shape[1]), :], point_ref.at[other], sems.at[1]),
    ]
    for copy in copies:
        copy.wait()


def call(kernel, outs, *args, far=(), whole=(), away=(), scratch=(), limit=24, aliases=None, flops=0, name=None):
    args = [pltpu.with_memory_space_constraint(v, pltpu.HBM) if i in far else v for i, v in enumerate(args)]
    moved = sum(math.prod(v.shape) * jnp.dtype(v.dtype).itemsize for v in list(args) + list(outs))
    return pl.pallas_call(
        kernel,
        out_shape=outs,
        in_specs=[
            pl.BlockSpec(memory_space=pltpu.HBM if i in far and i not in whole else pltpu.VMEM)
            for i in range(len(args))
        ],
        out_specs=[
            pl.BlockSpec(memory_space=pltpu.HBM if i in away else pltpu.VMEM) for i in range(len(outs))
        ],
        scratch_shapes=list(scratch),
        input_output_aliases=aliases or {},
        compiler_params=pltpu.CompilerParams(vmem_limit_bytes=limit * 1024 * 1024),
        cost_estimate=pl.CostEstimate(flops=flops, bytes_accessed=moved, transcendentals=0),
        name=name,
    )(*args)


def on_device(bases, embed, conv_weight, point_weight, cotangent):
    n, dp = lax.axis_size("seq"), lax.axis_size("dp")
    rb, width, mid = bases.shape[1], embed.shape[1], conv_weight.shape[2]
    if n != 2 * STRIDE or dp != 2:
        return general(bases, embed, conv_weight, point_weight, cotangent)
    k = lax.axis_index("seq")
    zh, r = k // STRIDE, k % STRIDE
    rows = 2 * rb
    crow, prow = 3 * width // n, width // n
    part = crow + prow
    shape, near = jax.ShapeDtypeStruct, pltpu.VMEM

    own = cotangent[0]
    far = lax.ppermute(own, "seq", [(s, (s + STRIDE) % n) for s in range(n)])
    (copies,) = call(spread_kernel, [near((n, 1, rb), jnp.int32)], bases, far=(0,), whole=(0,), name="spread")
    gathered = lax.all_to_all(copies, "seq", 0, 0, tiled=True)

    taps = pltpu.VMEM((3 * width, mid), BF16)
    act0, table, w2 = call(
        table_kernel,
        [
            shape((CLASSES, mid), BF16),
            pltpu.VMEM((CLASSES, width + 4 * mid), F32),
            pltpu.VMEM((3 * width, mid), BF16),
        ],
        embed, conv_weight, point_weight,
        far=(0, 1, 2),
        whole=(0,),
        scratch=[taps, taps, pltpu.VMEM((mid, width), BF16), pltpu.SemaphoreType.DMA((8,))],
        limit=20,
        flops=4 * CLASSES * 3 * width * mid,
        name="tables",
    )
    features, mine, other, h, c, w1, p0 = call(
        lambda *refs: main_kernel(crow, prow, *refs),
        [
            shape((rb, width), F32),
            near((STRIDE * part, mid), F32),
            near((STRIDE * part, mid), BF16),
            near((3 * CLASSES, mid), BF16),
            near((CLASSES, width), F32),
            near((3 * width, mid), BF16),
            near((mid, width), BF16),
        ],
        gathered, own, far, conv_weight, point_weight, w2, table,
        far=(3, 4),
        scratch=[
            pltpu.VMEM((rows, 3 * CLASSES), BF16),
            pltpu.VMEM((rows, width), F32),
            pltpu.VMEM((rows, width), BF16),
            pltpu.VMEM((rows, mid), BF16),
            pltpu.VMEM((rows, mid), BF16),
            pltpu.VMEM((rows, mid), F32),
            pltpu.VMEM((rows, mid), F32),
            pltpu.VMEM((rows, width), BF16),
            pltpu.VMEM((rows, mid), BF16),
            pltpu.VMEM((rows, width), BF16),
            pltpu.VMEM((2, STRIDE * crow, mid), F32),
            pltpu.VMEM((2, STRIDE * prow, mid), F32),
            pltpu.VMEM((CLASSES, width), BF16),
            pltpu.VMEM((2, mid, width), BF16),
            pltpu.VMEM((rb, width), F32),
            pltpu.SemaphoreType.DMA((5,)),
        ],
        away=(0,),
        flops=9 * rows * 3 * width * mid,
        name="tower",
    )

    swap = [(s, s ^ 1) for s in range(n)]
    got = lax.ppermute(other, "seq", swap)
    small_rows = 8 * STRIDE + 16
    mine_small, other_small = call(
        lambda *refs: class_kernel(prow, *refs),
        [near((small_rows, mid), F32), near((small_rows, mid), BF16)],
        h, c, table, w1, p0,
        scratch=[pltpu.VMEM((width, CLASSES), F32)],
        flops=4 * CLASSES * 3 * width * mid,
        name="classes",
    )
    got_small = lax.ppermute(other_small, "seq", swap)
    peers = STRIDE // 2 * dp
    pieces = call(
        lambda *refs: message_kernel(part, *refs),
        [shape((part + 32, mid), F32 if i == 0 else BF16) for i in range(peers)],
        mine, got, mine_small, got_small,
        name="messages",
    )
    arrived = []
    for i in range(1, peers):
        route = []
        for s in range(n):
            mask = ORDER[s % 2][i]
            route += [
                (s * dp + d, (s ^ (2 * (mask // dp))) * dp + (d ^ (mask % dp))) for d in range(dp)
            ]
        arrived.append(lax.ppermute(pieces[i], ("seq", "dp"), route))
    total, send, rest = call(
        sum_kernel,
        [shape((part, mid), F32), shape((part, mid), BF16), shape((32, mid), F32)],
        pieces[0], *arrived,
        name="sums",
    )
    swapped = lax.ppermute(send, "dp", [(d, d ^ 1) for d in range(dp)])

    stream_e = embed.astype(F32)
    normed_e = (stream_e * norm_scale(stream_e)).astype(BF16)
    spread = jnp.concatenate(
        [jnp.pad(normed_e, ((4 * j, 12 - 4 * j), (0, 0))) for j in range(3)], axis=1
    )
    spread = lax.dynamic_slice_in_dim(spread, k * crow, crow, axis=1).T
    conv_grad, point_grad, embed_full, bt = call(
        small_kernel,
        [
            shape((3, crow, mid), F32),
            shape((3, prow, mid), F32),
            shape((4, width), F32),
            shape((4, prow), F32),
        ],
        rest, total, embed, conv_weight, act0, spread,
        far=(3,),
        away=(0, 1),
        scratch=[
            pltpu.VMEM((3 * width, mid), BF16),
            pltpu.VMEM((crow, mid), F32),
            pltpu.VMEM((prow, mid), F32),
            pltpu.SemaphoreType.DMA((7,)),
        ],
        name="layer0",
    )
    embed_grad = bt + lax.dynamic_slice_in_dim(embed_full, k * prow, prow, axis=1)
    conv_grad, point_grad = call(
        finish_kernel,
        [shape((3, crow, mid), F32), shape((3, prow, mid), F32)],
        swapped, conv_grad, point_grad,
        far=(1, 2),
        away=(0, 1),
        aliases={1: 0, 2: 1},
        scratch=[pltpu.VMEM((part, mid), F32), pltpu.SemaphoreType.DMA((2,))],
        name="finish",
    )
    return features[None], conv_grad, point_grad.transpose(0, 2, 1), embed_grad


def solution(mesh):
    in_specs = (P("dp", "seq"), P(), P(), P(), P("dp", "seq", None))
    out_specs = (P("dp", "seq", None), P(None, "seq", None), P(None, None, "seq"), P(None, "seq"))
    return jax.shard_map(
        on_device, mesh=mesh, in_specs=in_specs, out_specs=out_specs, check_vma=False
    )
```

```python
import math

import jax
import jax.numpy as jnp
import numpy as np
from jax import lax
from jax.experimental import pallas as pl
from jax.experimental.pallas import tpu as pltpu
from jax.sharding import PartitionSpec as P

BF16 = jnp.bfloat16
F32 = jnp.float32
CLASSES = 128
STRIDE = 8
ORDER = (7, 6, 1, 5, 2, 3, 4)


def gelu_pair(v):
    coef = math.sqrt(2.0 / math.pi)
    inner = coef * (v + 0.044715 * v * v * v)
    t = jnp.tanh(inner)
    slope = 0.5 * (1.0 + t) + 0.5 * v * (1.0 - t * t) * coef * (1.0 + 3.0 * 0.044715 * v * v)
    return 0.5 * v * (1.0 + t), slope


def mm(a, b):
    return jnp.dot(a, b, preferred_element_type=F32)


def mm_tn(a, b):
    return lax.dot_general(a, b, (((0,), (0,)), ((), ())), preferred_element_type=F32)


def mm_nt(a, b):
    return lax.dot_general(a, b, (((1,), (1,)), ((), ())), preferred_element_type=F32)


def halves(v):
    high = lax.reduce_precision(v, 8, 7)
    return high.astype(BF16), (v - high).astype(BF16)


def selectors():
    c = np.arange(CLASSES)
    digits = (c // 20, (c // 5) % 4, c % 5)
    valid = (c < 100)[:, None]
    return [((d[:, None] == np.arange(4)[None, :]) & valid).astype(np.float32) for d in digits]


def norm_scale(v):
    return lax.rsqrt(jnp.mean(v * v, axis=-1, keepdims=True) + 1e-06)


def tables(embed, conv_weight, point_weight):
    sel = [jnp.asarray(s, BF16) for s in selectors()]
    stream = embed.astype(F32)
    scale_e = norm_scale(stream)
    normed_e = (stream * scale_e).astype(BF16)
    taps = jnp.concatenate([mm(s, normed_e).astype(BF16) for s in sel], axis=1)
    act0, slope0 = gelu_pair(mm(taps, conv_weight[0]))
    act0 = act0.astype(BF16)
    stab = mm(sel[1], embed) + mm(act0, point_weight[0])
    scale1 = norm_scale(stab)
    ntab = (stab * scale1).astype(BF16)
    width = embed.shape[1]
    u = jnp.concatenate([mm(ntab, conv_weight[1, j * width : (j + 1) * width]) for j in range(3)])
    return stream, scale_e, normed_e, act0, slope0, stab, scale1, ntab, u


def classes(gathered, dil):
    n, rb = gathered.shape
    edge = jnp.full((1, dil), 4, jnp.int32)
    left = jnp.concatenate(
        [jnp.concatenate([edge, gathered[:-1, rb - dil :]]), gathered[:, : rb - dil]], axis=1
    )
    right = jnp.concatenate(
        [gathered[:, dil:], jnp.concatenate([gathered[1:, :dil], edge])], axis=1
    )
    cls = left * 20 + gathered * 5 + right
    none = jnp.full((2, rb), -1, jnp.int32)
    return jnp.concatenate([none, cls, none])


def general(bases, embed, conv_weight, point_weight, cotangent):
    n, dp = lax.axis_size("seq"), lax.axis_size("dp")
    rb, width, mid = bases.shape[1], embed.shape[1], conv_weight.shape[2]
    group = n // STRIDE
    k, x = lax.axis_index("seq"), lax.axis_index("dp")
    zh, r = k // STRIDE, k % STRIDE
    m, core = r // 2, r % 2
    rows = group * rb
    w1, w2 = conv_weight[1], conv_weight[2]
    p0, p1, p2 = point_weight[0], point_weight[1], point_weight[2]

    gathered = lax.all_to_all(jnp.broadcast_to(bases, (n, rb)), "seq", 0, 0, tiled=True)
    own = cotangent[0]
    parts = [own]
    for i in range(1, group):
        parts.append(lax.ppermute(own, "seq", [(s, (s - STRIDE * i) % n) for s in range(n)]))
    cot = lax.dynamic_slice_in_dim(
        jnp.concatenate(parts + parts), ((group - zh) % group) * rb, rows
    )

    stream_e, scale_e, normed_e, act0, slope0, stab, scale1, ntab, u = tables(
        embed, conv_weight, point_weight
    )
    u_high, u_low = halves(u)
    s_high, s_low = halves(stab)

    cls = classes(gathered, rb // 8)
    hots = []
    for j in range(3):
        index = jnp.concatenate(
            [lax.dynamic_slice(cls, (a * STRIDE + r + 2 * j, 0), (1, rb)) for a in range(group)],
            axis=1,
        )
        hots.append((jnp.arange(CLASSES, dtype=jnp.int32)[:, None] == index).astype(BF16))
    hot = jnp.concatenate(hots)

    pre1 = mm_tn(hot, u_high) + mm_tn(hot, u_low)
    act1, slope1 = gelu_pair(pre1)
    act1 = act1.astype(BF16)
    stream2 = mm_tn(hots[1], s_high) + mm_tn(hots[1], s_low) + mm(act1, p1)
    scale2 = norm_scale(stream2)
    normed2 = (stream2 * scale2).astype(BF16)
    nothing = jnp.zeros((rb, width), BF16)
    taps2 = jnp.concatenate(
        [
            jnp.concatenate([nothing, normed2[: rows - rb]]),
            normed2,
            jnp.concatenate([normed2[rb:], nothing]),
        ],
        axis=1,
    )
    pre2 = mm(taps2, w2)
    act2, slope2 = gelu_pair(pre2)
    act2 = act2.astype(BF16)
    features = lax.dynamic_slice_in_dim(stream2, zh * rb, rb) + mm(
        lax.dynamic_slice_in_dim(act2, zh * rb, rb), p2
    )

    grad2 = (mm_nt(cot, p2) * slope2).astype(BF16)
    nothing = jnp.zeros((rb, mid), BF16)
    above = jnp.concatenate([grad2[rb:], nothing])
    below = jnp.concatenate([nothing, grad2[: rows - rb]])
    ng2 = (
        mm_nt(above, w2[:width]) + mm_nt(grad2, w2[width : 2 * width]) + mm_nt(below, w2[2 * width :])
    )
    inner = jnp.mean(ng2 * stream2, axis=-1, keepdims=True)
    back2 = cot.astype(F32) + scale2 * (ng2 - stream2 * scale2 * scale2 * inner)
    back2 = back2.astype(BF16)
    grad1 = (mm_nt(back2, p1) * slope1).astype(BF16)

    h = mm(hot, grad1).astype(BF16)
    ng1 = sum(
        mm_nt(h[j * CLASSES : (j + 1) * CLASSES], w1[j * width : (j + 1) * width]) for j in range(3)
    )
    inner = jnp.mean(ng1 * stab, axis=-1, keepdims=True)
    b = mm(hots[1], back2) + scale1 * (ng1 - stab * scale1 * scale1 * inner)
    b16 = b.astype(BF16)
    s = (mm_nt(b16, p0) * slope0).astype(BF16)
    sel = selectors()
    g = mm(jnp.asarray(np.concatenate([v.T for v in sel]), BF16), s)
    bt = mm(jnp.asarray(sel[1].T, BF16), b16)
    small = jnp.concatenate([g, bt.reshape(2 * 4, mid)])

    crow, prow = 3 * width // n, width // n
    conv1 = jnp.concatenate(
        [mm_tn(ntab, h[j * CLASSES : (j + 1) * CLASSES]) for j in range(3)]
    )
    conv1 = lax.dynamic_slice_in_dim(conv1, zh * STRIDE * crow, STRIDE * crow)
    conv2 = mm_tn(lax.dynamic_slice_in_dim(taps2, zh * STRIDE * crow, STRIDE * crow, axis=1), grad2)

    def share(v):
        return lax.dynamic_slice_in_dim(v, zh * STRIDE * prow, STRIDE * prow, axis=1)

    point = [mm_tn(share(b16), act0), mm_tn(share(back2), act1), mm_tn(share(cot), act2)]
    tile = jnp.concatenate(
        [conv1.reshape(STRIDE, crow, mid), conv2.reshape(STRIDE, crow, mid)]
        + [v.reshape(STRIDE, prow, mid) for v in point],
        axis=1,
    )
    trow = 2 * crow + 3 * prow
    half = STRIDE // 2
    tile = tile.reshape(half, 2, trow, mid)

    swap = [(s, s ^ 1) for s in range(n)]
    mine = lax.dynamic_index_in_dim(tile, core, axis=1, keepdims=False)
    other = lax.dynamic_index_in_dim(tile, 1 - core, axis=1, keepdims=False)
    mine = mine + lax.ppermute(other.astype(BF16), "seq", swap).astype(F32)
    small = small + lax.ppermute(small.astype(BF16), "seq", swap).astype(F32)

    drow = trow // dp
    mine = mine.reshape(half, dp, drow, mid)
    small16 = small.astype(BF16)
    total = lax.dynamic_slice(mine, (m, x, 0, 0), (1, 1, drow, mid))[0, 0]
    for mask in range(half * dp - 1, 0, -1):
        mm_, mx = mask // dp, mask % dp
        piece = lax.dynamic_slice(mine, (m ^ mm_, x ^ mx, 0, 0), (1, 1, drow, mid))[0, 0]
        message = jnp.concatenate([piece.astype(BF16), small16])
        route = [
            (s * dp + d, (s ^ (2 * mm_)) * dp + (d ^ mx)) for s in range(n) for d in range(dp)
        ]
        got = lax.ppermute(message, ("seq", "dp"), route).astype(F32)
        total = total + got[:drow]
        small = small + got[drow:]

    total16 = total.astype(BF16)
    pieces = [total16] + [
        lax.ppermute(total16, "dp", [(d, d ^ i) for d in range(dp)]) for i in range(1, dp)
    ]
    full = jnp.concatenate(
        [
            sum(jnp.where((x ^ i) == d, pieces[i].astype(F32), 0.0) for i in range(dp))
            for d in range(dp)
        ]
    )

    g, bt = small[:12], small[12:].reshape(4, width)
    ng0 = sum(
        mm_nt(g[4 * j : 4 * j + 4].astype(BF16), conv_weight[0, j * width : (j + 1) * width])
        for j in range(3)
    )
    inner = jnp.mean(ng0 * stream_e, axis=-1, keepdims=True)
    embed_grad = bt + scale_e * (ng0 - stream_e * scale_e * scale_e * inner)
    embed_grad = lax.dynamic_slice_in_dim(embed_grad, k * prow, prow, axis=1)
    spread = jnp.concatenate(
        [
            jnp.pad(normed_e, ((4 * j, 8 - 4 * j), (0, 0))) for j in range(3)
        ],
        axis=1,
    )
    spread = lax.dynamic_slice_in_dim(spread, k * crow, crow, axis=1)
    conv0 = mm_tn(spread, g.astype(BF16))
    conv_grad = jnp.stack([conv0, full[:crow], full[crow : 2 * crow]])
    point_grad = full[2 * crow :].reshape(3, prow, mid).transpose(0, 2, 1)
    return features[None], conv_grad, point_grad, embed_grad


def normal(v):
    return (v * norm_scale(v)).astype(BF16)


def spread_kernel(bases_ref, out_ref):
    for i in range(out_ref.shape[0]):
        out_ref[i] = bases_ref[...]


def fetch(source, target, sem):
    copy = pltpu.make_async_copy(source, target, sem)
    copy.start()
    return copy


def fetch_taps(w_ref, layer, held_ref, sems, first, order=(0, 1, 2)):
    width = held_ref.shape[0] // 3
    copies = {}
    for j in order:
        at = pl.ds(j * width, width)
        copies[j] = fetch(w_ref.at[layer, at, :], held_ref.at[at, :], sems.at[first + j])
    return copies


def digits(shape, axis):
    c = lax.broadcasted_iota(jnp.int32, shape, axis).astype(F32)
    left, both = jnp.floor((c + 0.5) / 20.0), jnp.floor((c + 0.5) / 5.0)
    return c < 100.0, (left, both - 4.0 * left, c - 5.0 * both)


def digit_columns():
    valid, values = digits((CLASSES, 4), 0)
    base = lax.broadcasted_iota(jnp.int32, (CLASSES, 4), 1).astype(F32)
    return [jnp.where(valid & (v == base), 1.0, 0.0).astype(BF16) for v in values]


def digit_rows():
    valid, values = digits((16, CLASSES), 1)
    row = lax.broadcasted_iota(jnp.int32, (16, CLASSES), 0).astype(F32)
    hit = (values[0] == row) & (row < 4.0)
    hit |= (values[1] + 4.0 == row) & (row >= 4.0) & (row < 8.0)
    hit |= (values[2] + 8.0 == row) & (row >= 8.0) & (row < 12.0)
    return jnp.where(valid & hit, 1.0, 0.0).astype(BF16)


def table_kernel(embed_ref, w_ref, p_ref, act0_ref, table_ref, w2_ref, w0_ref, w1_ref, p0_ref, sems):
    width, mid = embed_ref.shape[1], act0_ref.shape[1]
    copy_w0 = fetch_taps(w_ref, 0, w0_ref, sems, 0)
    copy_p0 = fetch(p_ref.at[0], p0_ref, sems.at[6])
    copy_w1 = fetch_taps(w_ref, 1, w1_ref, sems, 3)
    copy_w2 = fetch(w_ref.at[2], w2_ref, sems.at[7])
    normed_e = normal(embed_ref[...].astype(F32))
    sel = digit_columns()
    pre = None
    for j in range(3):
        taps = mm(sel[j], normed_e).astype(BF16)
        copy_w0[j].wait()
        term = mm(taps, w0_ref[j * width : (j + 1) * width, :])
        pre = term if pre is None else pre + term
    act0, slope0 = gelu_pair(pre)
    act0 = act0.astype(BF16)
    act0_ref[...] = act0
    copy_p0.wait()
    stab = mm(sel[1], embed_ref[...]) + mm(act0, p0_ref[...])
    table_ref[:, :width] = stab
    table_ref[:, width : width + mid] = slope0
    ntab = normal(stab)
    for j in range(3):
        copy_w1[j].wait()
        at = width + (j + 1) * mid
        table_ref[:, at : at + mid] = mm(ntab, w1_ref[j * width : (j + 1) * width, :])
    copy_w2.wait()


def main_kernel(
    crow, prow, bases_ref, own_ref, far_ref, w_ref, p_ref, w2_ref, table_ref,
    features_ref, mine_ref, other_ref, h_ref, c_ref, w1_ref, p0_ref,
    hot_ref, stream_ref, normed_ref, act1_ref, act2_ref, slope1_ref, slope2_ref,
    cot_ref, grad_ref, back_ref, conv_ref, point_ref, ntab_ref, pt_ref, sent_ref, sems,
):
    n, _, rb = bases_ref.shape
    rows, width = stream_ref.shape
    mid = act1_ref.shape[1]
    dil, half = rb // 8, width // 2
    k = lax.axis_index("seq")
    zh, r, core = k // STRIDE, k % STRIDE, k % 2
    place = pl.ds(pl.multiple_of(zh * rb, 16), rb)
    far = pl.ds(pl.multiple_of((1 - zh) * rb, 16), rb)
    copy_p1 = fetch(p_ref.at[1], pt_ref.at[0], sems.at[0])
    copy_p2 = fetch(p_ref.at[2], pt_ref.at[1], sems.at[1])
    copy_w1 = fetch(w_ref.at[1], w1_ref, sems.at[2])
    copy_p0 = fetch(p_ref.at[0], p0_ref, sems.at[3])
    held = jnp.concatenate([bases_ref[i] for i in range(n)])
    held = (held - 4).astype(F32)
    edge = jnp.zeros((1, rb), F32)
    held = jnp.concatenate(
        [
            jnp.concatenate([edge, held[:-1]]).astype(BF16),
            held.astype(BF16),
            jnp.concatenate([held[1:], edge]).astype(BF16),
        ]
    )
    ahead = lax.broadcasted_iota(jnp.int32, (rb, rb), 0) - lax.broadcasted_iota(jnp.int32, (rb, rb), 1)

    def weight(gap):
        value = jnp.where(gap == -dil, 20.0, jnp.where(gap == 0, 5.0, jnp.where(gap == dil, 1.0, 0.0)))
        return value.astype(BF16)

    cls = (
        mm(held[:n], weight(ahead - rb)) + mm(held[n : 2 * n], weight(ahead)) + mm(held[2 * n :], weight(ahead + rb))
        + 105.0
    ).astype(BF16)
    block = lax.broadcasted_iota(jnp.int32, (n, CLASSES), 0)
    slot = lax.broadcasted_iota(jnp.int32, (n, CLASSES), 1)
    wanted = (slot // 3) * STRIDE + r + 2 * (slot % 3) - 2
    pick = jnp.where((block == wanted) & (slot < 6), 1.0, 0.0).astype(BF16)
    column = mm_tn(cls, pick)
    lanes = (lax.broadcasted_iota(jnp.int32, (rb, CLASSES), 1) + 1).astype(F32)
    for a in range(2):
        for j in range(3):
            i = 3 * a + j
            hot_ref[a * rb : (a + 1) * rb, j * CLASSES : (j + 1) * CLASSES] = jnp.where(
                lanes == column[:, i : i + 1], 1.0, 0.0
            ).astype(BF16)

    hot = hot_ref[...]
    mid_hot = hot[:, CLASSES : 2 * CLASSES]
    u = jnp.concatenate(
        [table_ref[:, width + (j + 1) * mid : width + (j + 2) * mid] for j in range(3)]
    )
    u_high = u.astype(BF16)
    act1, slope1 = gelu_pair(mm(hot, u_high) + mm(hot, (u - u_high.astype(F32)).astype(BF16)))
    act1 = act1.astype(BF16)
    act1_ref[...] = act1
    slope1_ref[...] = slope1
    stab = table_ref[:, :width]
    s_high = stab.astype(BF16)
    stream = mm(mid_hot, s_high) + mm(mid_hot, (stab - s_high.astype(F32)).astype(BF16))
    copy_p1.wait()
    stream = stream + mm(act1, pt_ref[0])
    stream_ref[...] = stream
    normed = normal(stream)
    normed_ref[...] = normed
    sides = jnp.concatenate(
        [mm(normed[rb:], w2_ref[2 * width :, :]), mm(normed[:rb], w2_ref[:width, :])]
    )
    act2, slope2 = gelu_pair(mm(normed, w2_ref[width : 2 * width, :]) + sides)
    act2_ref[...] = act2.astype(BF16)
    slope2_ref[...] = slope2
    copy_p2.wait()
    sent_ref[...] = stream_ref[place, :] + mm(act2_ref[place, :], pt_ref[1])
    copy_features = fetch(sent_ref, features_ref, sems.at[4])

    cot_ref[place, :] = own_ref[...]
    cot_ref[far, :] = far_ref[...]
    grad2 = (mm_nt(cot_ref[...], pt_ref[1]) * slope2_ref[...]).astype(BF16)
    grad_ref[...] = grad2
    sides = jnp.concatenate(
        [mm_nt(grad2[rb:], w2_ref[:width, :]), mm_nt(grad2[:rb], w2_ref[2 * width :, :])]
    )
    ng = mm_nt(grad2, w2_ref[width : 2 * width, :]) + sides
    stream = stream_ref[...]
    scale = norm_scale(stream)
    inner = jnp.mean(ng * stream, axis=-1, keepdims=True)
    back = cot_ref[...].astype(F32) + scale * (ng - stream * (scale * scale * inner))
    back = back.astype(BF16)
    back_ref[...] = back
    grad1 = (mm_nt(back, pt_ref[0]) * slope1_ref[...]).astype(BF16)

    h = mm_tn(hot_ref[...], grad1).astype(BF16)
    h_ref[...] = h
    h = [h[j * CLASSES : (j + 1) * CLASSES] for j in range(3)]
    c_ref[...] = mm_tn(hot_ref[:, CLASSES : 2 * CLASSES], back)
    ntab_ref[...] = normal(table_ref[:, :width])

    columns = pl.ds(pl.multiple_of(zh * half, 128), half)
    side_at = pl.ds(pl.multiple_of(zh * half, 16), width)
    center_at = pl.ds(pl.multiple_of((1 - zh) * width, 16), half)
    conv_ref[0, side_at, :] = mm_tn(ntab_ref[...], jnp.where(zh == 0, h[0], h[2]))
    conv_ref[0, center_at, :] = mm_tn(ntab_ref[:, columns], h[1])
    conv_ref[1, side_at, :] = mm_tn(normed_ref[place, :], grad_ref[far, :])
    conv_ref[1, center_at, :] = mm_tn(normed_ref[:, columns], grad_ref[...])
    point_ref[0] = mm_tn(back_ref[:, columns], act1_ref[...])
    point_ref[1] = mm_tn(cot_ref[:, columns], act2_ref[...])
    part = crow + prow
    for target, side in ((mine_ref, core), (other_ref, 1 - core)):
        for m in range(STRIDE // 2):
            tile = 2 * m + side
            crows = pl.ds(pl.multiple_of(tile * crow, 16), crow)
            prows = pl.ds(pl.multiple_of(tile * prow, 16), prow)
            for layer in range(2):
                at = (2 * m + layer) * part
                target[at : at + crow, :] = conv_ref[layer, crows, :].astype(target.dtype)
                target[at + crow : at + part, :] = point_ref[layer, prows, :].astype(target.dtype)
    for copy in (copy_features, copy_w1, copy_p0):
        copy.wait()


def class_kernel(prow, h_ref, c_ref, table_ref, w1_ref, p0_ref, mine_ref, other_ref, bt_ref):
    width, mid = c_ref.shape[1], h_ref.shape[1]
    half = width // 2
    k = lax.axis_index("seq")
    zh, core = k // STRIDE, k % 2
    ng = None
    for j in range(3):
        term = mm_nt(
            h_ref[j * CLASSES : (j + 1) * CLASSES, :], w1_ref[j * width : (j + 1) * width, :]
        )
        ng = term if ng is None else ng + term
    stab = table_ref[:, :width]
    scale = norm_scale(stab)
    inner = jnp.mean(ng * stab, axis=-1, keepdims=True)
    b = c_ref[...] + scale * (ng - stab * (scale * scale * inner))
    s = (mm_nt(b.astype(BF16), p0_ref[...]) * table_ref[:, width : width + mid]).astype(BF16)
    g = mm(digit_rows(), s)
    bt_ref[...] = jnp.transpose(b)
    for target, side in ((mine_ref, core), (other_ref, 1 - core)):
        for m in range(STRIDE // 2):
            for q in range(3):
                at = pl.ds(pl.multiple_of(zh * half + (2 * m + side) * prow + 16 * q, 16), 16)
                target[16 * m : 16 * m + 16, q * CLASSES : (q + 1) * CLASSES] = bt_ref[at, :].astype(
                    target.dtype
                )
        target[8 * STRIDE : 8 * STRIDE + 16, :] = g.astype(target.dtype)


def message_kernel(part, mine_ref, other_ref, mine_small_ref, other_small_ref, *out_refs):
    k, x = lax.axis_index("seq"), lax.axis_index("dp")
    m = (k % STRIDE) // 2
    end = 8 * STRIDE
    g = mine_small_ref[end:, :] + other_small_ref[end:, :].astype(F32)
    for mask, out_ref in enumerate(out_refs):
        target, layer = m ^ (mask // 2), x ^ (mask % 2)
        at = pl.ds(pl.multiple_of((2 * target + layer) * part, 16), part)
        out_ref[:part, :] = (mine_ref[at, :].astype(F32) + other_ref[at, :].astype(F32)).astype(out_ref.dtype)
        at = pl.ds(pl.multiple_of(target * 16, 16), 16)
        small = mine_small_ref[at, :] + other_small_ref[at, :].astype(F32)
        out_ref[part : part + 16, :] = small.astype(out_ref.dtype)
        out_ref[part + 16 :, :] = g.astype(out_ref.dtype)


def sum_kernel(own_ref, *refs):
    got, (total_ref, send_ref, rest_ref) = refs[:-3], refs[-3:]
    part = total_ref.shape[0]
    total = own_ref[...]
    for ref in got:
        total = total + ref[...].astype(F32)
    total_ref[...] = total[:part]
    send_ref[...] = total[:part].astype(BF16)
    rest_ref[...] = total[part:]


def small_kernel(
    rest_ref, total_ref, embed_ref, w_ref, act0_ref, spread_ref,
    conv_ref, point_ref, embed_out_ref, bt_ref, w0_ref, conv0_ref, point0_ref, sems,
):
    copy_w0 = fetch_taps(w_ref, 0, w0_ref, sems, 0)
    width = embed_ref.shape[1]
    crow = conv_ref.shape[1]
    own = lax.axis_index("dp") + 1
    copies = [
        fetch(total_ref.at[pl.ds(0, crow), :], conv_ref.at[own], sems.at[3]),
        fetch(total_ref.at[pl.ds(crow, point_ref.shape[1]), :], point_ref.at[own], sems.at[4]),
    ]
    g = rest_ref[16:, :]
    bt = jnp.concatenate([rest_ref[:16, q * CLASSES : (q + 1) * CLASSES] for q in range(3)])
    bt = bt.astype(BF16)
    g16 = g.astype(BF16)
    conv0_ref[...] = mm(spread_ref[...], g16)
    copies.append(fetch(conv0_ref, conv_ref.at[0], sems.at[5]))
    point0_ref[...] = mm(bt, act0_ref[...])
    copies.append(fetch(point0_ref, point_ref.at[0], sems.at[6]))
    bt_ref[...] = mm_nt(digit_rows(), bt)[4:8]
    stream = embed_ref[...].astype(F32)
    scale = norm_scale(stream)
    ng = None
    for j in range(3):
        copy_w0[j].wait()
        term = mm_nt(g16, w0_ref[j * width : (j + 1) * width, :])[4 * j : 4 * j + 4]
        ng = term if ng is None else ng + term
    inner = jnp.mean(ng * stream, axis=-1, keepdims=True)
    embed_out_ref[...] = scale * (ng - stream * (scale * scale * inner))
    for copy in copies:
        copy.wait()


def finish_kernel(got_ref, _, __, conv_ref, point_ref, held_ref, sems):
    crow = conv_ref.shape[1]
    other = 2 - lax.axis_index("dp")
    held_ref[...] = got_ref[...].astype(F32)
    copies = [
        fetch(held_ref.at[pl.ds(0, crow), :], conv_ref.at[other], sems.at[0]),
        fetch(held_ref.at[pl.ds(crow, point_ref.shape[1]), :], point_ref.at[other], sems.at[1]),
    ]
    for copy in copies:
        copy.wait()


def call(kernel, outs, *args, far=(), whole=(), away=(), scratch=(), limit=24, aliases=None, flops=0, name=None):
    args = [pltpu.with_memory_space_constraint(v, pltpu.HBM) if i in far else v for i, v in enumerate(args)]
    moved = sum(math.prod(v.shape) * jnp.dtype(v.dtype).itemsize for v in list(args) + list(outs))
    return pl.pallas_call(
        kernel,
        out_shape=outs,
        in_specs=[
            pl.BlockSpec(memory_space=pltpu.HBM if i in far and i not in whole else pltpu.VMEM)
            for i in range(len(args))
        ],
        out_specs=[
            pl.BlockSpec(memory_space=pltpu.HBM if i in away else pltpu.VMEM) for i in range(len(outs))
        ],
        scratch_shapes=list(scratch),
        input_output_aliases=aliases or {},
        compiler_params=pltpu.CompilerParams(vmem_limit_bytes=limit * 1024 * 1024),
        cost_estimate=pl.CostEstimate(flops=flops, bytes_accessed=moved, transcendentals=0),
        name=name,
    )(*args)


def on_device(bases, embed, conv_weight, point_weight, cotangent):
    n, dp = lax.axis_size("seq"), lax.axis_size("dp")
    rb, width, mid = bases.shape[1], embed.shape[1], conv_weight.shape[2]
    if n != 2 * STRIDE or dp != 2:
        return general(bases, embed, conv_weight, point_weight, cotangent)
    k = lax.axis_index("seq")
    zh, r = k // STRIDE, k % STRIDE
    rows = 2 * rb
    crow, prow = 3 * width // n, width // n
    part = crow + prow
    shape, near = jax.ShapeDtypeStruct, pltpu.VMEM

    own = cotangent[0]
    far = lax.ppermute(own, "seq", [(s, (s + STRIDE) % n) for s in range(n)])
    (copies,) = call(spread_kernel, [near((n, 1, rb), jnp.int32)], bases, far=(0,), whole=(0,), name="spread")
    gathered = lax.all_to_all(copies, "seq", 0, 0, tiled=True)

    taps = pltpu.VMEM((3 * width, mid), BF16)
    act0, table, w2 = call(
        table_kernel,
        [
            shape((CLASSES, mid), BF16),
            pltpu.VMEM((CLASSES, width + 4 * mid), F32),
            pltpu.VMEM((3 * width, mid), BF16),
        ],
        embed, conv_weight, point_weight,
        far=(0, 1, 2),
        whole=(0,),
        scratch=[taps, taps, pltpu.VMEM((mid, width), BF16), pltpu.SemaphoreType.DMA((8,))],
        limit=20,
        flops=4 * CLASSES * 3 * width * mid,
        name="tables",
    )
    features, mine, other, h, c, w1, p0 = call(
        lambda *refs: main_kernel(crow, prow, *refs),
        [
            shape((rb, width), F32),
            near((STRIDE * part, mid), BF16),
            near((STRIDE * part, mid), BF16),
            near((3 * CLASSES, mid), BF16),
            near((CLASSES, width), F32),
            near((3 * width, mid), BF16),
            near((mid, width), BF16),
        ],
        gathered, own, far, conv_weight, point_weight, w2, table,
        far=(3, 4),
        scratch=[
            pltpu.VMEM((rows, 3 * CLASSES), BF16),
            pltpu.VMEM((rows, width), F32),
            pltpu.VMEM((rows, width), BF16),
            pltpu.VMEM((rows, mid), BF16),
            pltpu.VMEM((rows, mid), BF16),
            pltpu.VMEM((rows, mid), F32),
            pltpu.VMEM((rows, mid), F32),
            pltpu.VMEM((rows, width), BF16),
            pltpu.VMEM((rows, mid), BF16),
            pltpu.VMEM((rows, width), BF16),
            pltpu.VMEM((2, STRIDE * crow, mid), F32),
            pltpu.VMEM((2, STRIDE * prow, mid), F32),
            pltpu.VMEM((CLASSES, width), BF16),
            pltpu.VMEM((2, mid, width), BF16),
            pltpu.VMEM((rb, width), F32),
            pltpu.SemaphoreType.DMA((5,)),
        ],
        away=(0,),
        flops=9 * rows * 3 * width * mid,
        name="tower",
    )

    swap = [(s, s ^ 1) for s in range(n)]
    got = lax.ppermute(other, "seq", swap)
    small_rows = 8 * STRIDE + 16
    mine_small, other_small = call(
        lambda *refs: class_kernel(prow, *refs),
        [near((small_rows, mid), F32), near((small_rows, mid), BF16)],
        h, c, table, w1, p0,
        scratch=[pltpu.VMEM((width, CLASSES), F32)],
        flops=4 * CLASSES * 3 * width * mid,
        name="classes",
    )
    got_small = lax.ppermute(other_small, "seq", swap)
    peers = STRIDE // 2 * dp
    pieces = call(
        lambda *refs: message_kernel(part, *refs),
        [shape((part + 32, mid), F32 if i == 0 else BF16) for i in range(peers)],
        mine, got, mine_small, got_small,
        name="messages",
    )
    arrived = []
    for mask in ORDER:
        route = [
            (s * dp + d, (s ^ (2 * (mask // dp))) * dp + (d ^ (mask % dp)))
            for s in range(n)
            for d in range(dp)
        ]
        arrived.append(lax.ppermute(pieces[mask], ("seq", "dp"), route))
    total, send, rest = call(
        sum_kernel,
        [shape((part, mid), F32), shape((part, mid), BF16), shape((32, mid), F32)],
        pieces[0], *arrived,
        name="sums",
    )
    swapped = lax.ppermute(send, "dp", [(d, d ^ 1) for d in range(dp)])

    stream_e = embed.astype(F32)
    normed_e = (stream_e * norm_scale(stream_e)).astype(BF16)
    spread = jnp.concatenate(
        [jnp.pad(normed_e, ((4 * j, 12 - 4 * j), (0, 0))) for j in range(3)], axis=1
    )
    spread = lax.dynamic_slice_in_dim(spread, k * crow, crow, axis=1).T
    conv_grad, point_grad, embed_full, bt = call(
        small_kernel,
        [
            shape((3, crow, mid), F32),
            shape((3, prow, mid), F32),
            shape((4, width), F32),
            shape((4, prow), F32),
        ],
        rest, total, embed, conv_weight, act0, spread,
        far=(3,),
        away=(0, 1),
        scratch=[
            pltpu.VMEM((3 * width, mid), BF16),
            pltpu.VMEM((crow, mid), F32),
            pltpu.VMEM((prow, mid), F32),
            pltpu.SemaphoreType.DMA((7,)),
        ],
        name="layer0",
    )
    embed_grad = bt + lax.dynamic_slice_in_dim(embed_full, k * prow, prow, axis=1)
    conv_grad, point_grad = call(
        finish_kernel,
        [shape((3, crow, mid), F32), shape((3, prow, mid), F32)],
        swapped, conv_grad, point_grad,
        far=(1, 2),
        away=(0, 1),
        aliases={1: 0, 2: 1},
        scratch=[pltpu.VMEM((part, mid), F32), pltpu.SemaphoreType.DMA((2,))],
        name="finish",
    )
    return features[None], conv_grad, point_grad.transpose(0, 2, 1), embed_grad


def solution(mesh):
    in_specs = (P("dp", "seq"), P(), P(), P(), P("dp", "seq", None))
    out_specs = (P("dp", "seq", None), P(None, "seq", None), P(None, None, "seq"), P(None, "seq"))
    return jax.shard_map(
        on_device, mesh=mesh, in_specs=in_specs, out_specs=out_specs, check_vma=False
    )
```

```python
import math

import jax
import jax.numpy as jnp
import numpy as np
from jax import lax
from jax.experimental import pallas as pl
from jax.experimental.pallas import tpu as pltpu
from jax.sharding import PartitionSpec as P

BF16 = jnp.bfloat16
F32 = jnp.float32
CLASSES = 128
STRIDE = 8
ORDER = (7, 6, 1, 5, 2, 3, 4)


def gelu_pair(v):
    coef = math.sqrt(2.0 / math.pi)
    inner = coef * (v + 0.044715 * v * v * v)
    t = jnp.tanh(inner)
    slope = 0.5 * (1.0 + t) + 0.5 * v * (1.0 - t * t) * coef * (1.0 + 3.0 * 0.044715 * v * v)
    return 0.5 * v * (1.0 + t), slope


def mm(a, b):
    return jnp.dot(a, b, preferred_element_type=F32)


def mm_tn(a, b):
    return lax.dot_general(a, b, (((0,), (0,)), ((), ())), preferred_element_type=F32)


def mm_nt(a, b):
    return lax.dot_general(a, b, (((1,), (1,)), ((), ())), preferred_element_type=F32)


def halves(v):
    high = lax.reduce_precision(v, 8, 7)
    return high.astype(BF16), (v - high).astype(BF16)


def selectors():
    c = np.arange(CLASSES)
    digits = (c // 20, (c // 5) % 4, c % 5)
    valid = (c < 100)[:, None]
    return [((d[:, None] == np.arange(4)[None, :]) & valid).astype(np.float32) for d in digits]


def norm_scale(v):
    return lax.rsqrt(jnp.mean(v * v, axis=-1, keepdims=True) + 1e-06)


def tables(embed, conv_weight, point_weight):
    sel = [jnp.asarray(s, BF16) for s in selectors()]
    stream = embed.astype(F32)
    scale_e = norm_scale(stream)
    normed_e = (stream * scale_e).astype(BF16)
    taps = jnp.concatenate([mm(s, normed_e).astype(BF16) for s in sel], axis=1)
    act0, slope0 = gelu_pair(mm(taps, conv_weight[0]))
    act0 = act0.astype(BF16)
    stab = mm(sel[1], embed) + mm(act0, point_weight[0])
    scale1 = norm_scale(stab)
    ntab = (stab * scale1).astype(BF16)
    width = embed.shape[1]
    u = jnp.concatenate([mm(ntab, conv_weight[1, j * width : (j + 1) * width]) for j in range(3)])
    return stream, scale_e, normed_e, act0, slope0, stab, scale1, ntab, u


def classes(gathered, dil):
    n, rb = gathered.shape
    edge = jnp.full((1, dil), 4, jnp.int32)
    left = jnp.concatenate(
        [jnp.concatenate([edge, gathered[:-1, rb - dil :]]), gathered[:, : rb - dil]], axis=1
    )
    right = jnp.concatenate(
        [gathered[:, dil:], jnp.concatenate([gathered[1:, :dil], edge])], axis=1
    )
    cls = left * 20 + gathered * 5 + right
    none = jnp.full((2, rb), -1, jnp.int32)
    return jnp.concatenate([none, cls, none])


def general(bases, embed, conv_weight, point_weight, cotangent):
    n, dp = lax.axis_size("seq"), lax.axis_size("dp")
    rb, width, mid = bases.shape[1], embed.shape[1], conv_weight.shape[2]
    group = n // STRIDE
    k, x = lax.axis_index("seq"), lax.axis_index("dp")
    zh, r = k // STRIDE, k % STRIDE
    m, core = r // 2, r % 2
    rows = group * rb
    w1, w2 = conv_weight[1], conv_weight[2]
    p0, p1, p2 = point_weight[0], point_weight[1], point_weight[2]

    gathered = lax.all_to_all(jnp.broadcast_to(bases, (n, rb)), "seq", 0, 0, tiled=True)
    own = cotangent[0]
    parts = [own]
    for i in range(1, group):
        parts.append(lax.ppermute(own, "seq", [(s, (s - STRIDE * i) % n) for s in range(n)]))
    cot = lax.dynamic_slice_in_dim(
        jnp.concatenate(parts + parts), ((group - zh) % group) * rb, rows
    )

    stream_e, scale_e, normed_e, act0, slope0, stab, scale1, ntab, u = tables(
        embed, conv_weight, point_weight
    )
    u_high, u_low = halves(u)
    s_high, s_low = halves(stab)

    cls = classes(gathered, rb // 8)
    hots = []
    for j in range(3):
        index = jnp.concatenate(
            [lax.dynamic_slice(cls, (a * STRIDE + r + 2 * j, 0), (1, rb)) for a in range(group)],
            axis=1,
        )
        hots.append((jnp.arange(CLASSES, dtype=jnp.int32)[:, None] == index).astype(BF16))
    hot = jnp.concatenate(hots)

    pre1 = mm_tn(hot, u_high) + mm_tn(hot, u_low)
    act1, slope1 = gelu_pair(pre1)
    act1 = act1.astype(BF16)
    stream2 = mm_tn(hots[1], s_high) + mm_tn(hots[1], s_low) + mm(act1, p1)
    scale2 = norm_scale(stream2)
    normed2 = (stream2 * scale2).astype(BF16)
    nothing = jnp.zeros((rb, width), BF16)
    taps2 = jnp.concatenate(
        [
            jnp.concatenate([nothing, normed2[: rows - rb]]),
            normed2,
            jnp.concatenate([normed2[rb:], nothing]),
        ],
        axis=1,
    )
    pre2 = mm(taps2, w2)
    act2, slope2 = gelu_pair(pre2)
    act2 = act2.astype(BF16)
    features = lax.dynamic_slice_in_dim(stream2, zh * rb, rb) + mm(
        lax.dynamic_slice_in_dim(act2, zh * rb, rb), p2
    )

    grad2 = (mm_nt(cot, p2) * slope2).astype(BF16)
    nothing = jnp.zeros((rb, mid), BF16)
    above = jnp.concatenate([grad2[rb:], nothing])
    below = jnp.concatenate([nothing, grad2[: rows - rb]])
    ng2 = (
        mm_nt(above, w2[:width]) + mm_nt(grad2, w2[width : 2 * width]) + mm_nt(below, w2[2 * width :])
    )
    inner = jnp.mean(ng2 * stream2, axis=-1, keepdims=True)
    back2 = cot.astype(F32) + scale2 * (ng2 - stream2 * scale2 * scale2 * inner)
    back2 = back2.astype(BF16)
    grad1 = (mm_nt(back2, p1) * slope1).astype(BF16)

    h = mm(hot, grad1).astype(BF16)
    ng1 = sum(
        mm_nt(h[j * CLASSES : (j + 1) * CLASSES], w1[j * width : (j + 1) * width]) for j in range(3)
    )
    inner = jnp.mean(ng1 * stab, axis=-1, keepdims=True)
    b = mm(hots[1], back2) + scale1 * (ng1 - stab * scale1 * scale1 * inner)
    b16 = b.astype(BF16)
    s = (mm_nt(b16, p0) * slope0).astype(BF16)
    sel = selectors()
    g = mm(jnp.asarray(np.concatenate([v.T for v in sel]), BF16), s)
    bt = mm(jnp.asarray(sel[1].T, BF16), b16)
    small = jnp.concatenate([g, bt.reshape(2 * 4, mid)])

    crow, prow = 3 * width // n, width // n
    conv1 = jnp.concatenate(
        [mm_tn(ntab, h[j * CLASSES : (j + 1) * CLASSES]) for j in range(3)]
    )
    conv1 = lax.dynamic_slice_in_dim(conv1, zh * STRIDE * crow, STRIDE * crow)
    conv2 = mm_tn(lax.dynamic_slice_in_dim(taps2, zh * STRIDE * crow, STRIDE * crow, axis=1), grad2)

    def share(v):
        return lax.dynamic_slice_in_dim(v, zh * STRIDE * prow, STRIDE * prow, axis=1)

    point = [mm_tn(share(b16), act0), mm_tn(share(back2), act1), mm_tn(share(cot), act2)]
    tile = jnp.concatenate(
        [conv1.reshape(STRIDE, crow, mid), conv2.reshape(STRIDE, crow, mid)]
        + [v.reshape(STRIDE, prow, mid) for v in point],
        axis=1,
    )
    trow = 2 * crow + 3 * prow
    half = STRIDE // 2
    tile = tile.reshape(half, 2, trow, mid)

    swap = [(s, s ^ 1) for s in range(n)]
    mine = lax.dynamic_index_in_dim(tile, core, axis=1, keepdims=False)
    other = lax.dynamic_index_in_dim(tile, 1 - core, axis=1, keepdims=False)
    mine = mine + lax.ppermute(other.astype(BF16), "seq", swap).astype(F32)
    small = small + lax.ppermute(small.astype(BF16), "seq", swap).astype(F32)

    drow = trow // dp
    mine = mine.reshape(half, dp, drow, mid)
    small16 = small.astype(BF16)
    total = lax.dynamic_slice(mine, (m, x, 0, 0), (1, 1, drow, mid))[0, 0]
    for mask in range(half * dp - 1, 0, -1):
        mm_, mx = mask // dp, mask % dp
        piece = lax.dynamic_slice(mine, (m ^ mm_, x ^ mx, 0, 0), (1, 1, drow, mid))[0, 0]
        message = jnp.concatenate([piece.astype(BF16), small16])
        route = [
            (s * dp + d, (s ^ (2 * mm_)) * dp + (d ^ mx)) for s in range(n) for d in range(dp)
        ]
        got = lax.ppermute(message, ("seq", "dp"), route).astype(F32)
        total = total + got[:drow]
        small = small + got[drow:]

    total16 = total.astype(BF16)
    pieces = [total16] + [
        lax.ppermute(total16, "dp", [(d, d ^ i) for d in range(dp)]) for i in range(1, dp)
    ]
    full = jnp.concatenate(
        [
            sum(jnp.where((x ^ i) == d, pieces[i].astype(F32), 0.0) for i in range(dp))
            for d in range(dp)
        ]
    )

    g, bt = small[:12], small[12:].reshape(4, width)
    ng0 = sum(
        mm_nt(g[4 * j : 4 * j + 4].astype(BF16), conv_weight[0, j * width : (j + 1) * width])
        for j in range(3)
    )
    inner = jnp.mean(ng0 * stream_e, axis=-1, keepdims=True)
    embed_grad = bt + scale_e * (ng0 - stream_e * scale_e * scale_e * inner)
    embed_grad = lax.dynamic_slice_in_dim(embed_grad, k * prow, prow, axis=1)
    spread = jnp.concatenate(
        [
            jnp.pad(normed_e, ((4 * j, 8 - 4 * j), (0, 0))) for j in range(3)
        ],
        axis=1,
    )
    spread = lax.dynamic_slice_in_dim(spread, k * crow, crow, axis=1)
    conv0 = mm_tn(spread, g.astype(BF16))
    conv_grad = jnp.stack([conv0, full[:crow], full[crow : 2 * crow]])
    point_grad = full[2 * crow :].reshape(3, prow, mid).transpose(0, 2, 1)
    return features[None], conv_grad, point_grad, embed_grad


def normal(v):
    return (v * norm_scale(v)).astype(BF16)


def spread_kernel(bases_ref, out_ref):
    for i in range(out_ref.shape[0]):
        out_ref[i] = bases_ref[...]


def fetch(source, target, sem):
    copy = pltpu.make_async_copy(source, target, sem)
    copy.start()
    return copy


def fetch_taps(w_ref, layer, held_ref, sems, first, order=(0, 1, 2)):
    width = held_ref.shape[0] // 3
    copies = {}
    for j in order:
        at = pl.ds(j * width, width)
        copies[j] = fetch(w_ref.at[layer, at, :], held_ref.at[at, :], sems.at[first + j])
    return copies


def digits(shape, axis):
    c = lax.broadcasted_iota(jnp.int32, shape, axis).astype(F32)
    left, both = jnp.floor((c + 0.5) / 20.0), jnp.floor((c + 0.5) / 5.0)
    return c < 100.0, (left, both - 4.0 * left, c - 5.0 * both)


def digit_columns():
    valid, values = digits((CLASSES, 4), 0)
    base = lax.broadcasted_iota(jnp.int32, (CLASSES, 4), 1).astype(F32)
    return [jnp.where(valid & (v == base), 1.0, 0.0).astype(BF16) for v in values]


def digit_rows():
    valid, values = digits((16, CLASSES), 1)
    row = lax.broadcasted_iota(jnp.int32, (16, CLASSES), 0).astype(F32)
    hit = (values[0] == row) & (row < 4.0)
    hit |= (values[1] + 4.0 == row) & (row >= 4.0) & (row < 8.0)
    hit |= (values[2] + 8.0 == row) & (row >= 8.0) & (row < 12.0)
    return jnp.where(valid & hit, 1.0, 0.0).astype(BF16)


def table_kernel(embed_ref, w_ref, p_ref, act0_ref, table_ref, w2_ref, w0_ref, w1_ref, p0_ref, sems):
    width, mid = embed_ref.shape[1], act0_ref.shape[1]
    copy_w0 = fetch_taps(w_ref, 0, w0_ref, sems, 0)
    copy_p0 = fetch(p_ref.at[0], p0_ref, sems.at[6])
    copy_w1 = fetch_taps(w_ref, 1, w1_ref, sems, 3)
    copy_w2 = fetch(w_ref.at[2], w2_ref, sems.at[7])
    normed_e = normal(embed_ref[...].astype(F32))
    sel = digit_columns()
    pre = None
    for j in range(3):
        taps = mm(sel[j], normed_e).astype(BF16)
        copy_w0[j].wait()
        term = mm(taps, w0_ref[j * width : (j + 1) * width, :])
        pre = term if pre is None else pre + term
    act0, slope0 = gelu_pair(pre)
    act0 = act0.astype(BF16)
    act0_ref[...] = act0
    copy_p0.wait()
    stab = mm(sel[1], embed_ref[...]) + mm(act0, p0_ref[...])
    table_ref[:, :width] = stab
    table_ref[:, width : width + mid] = slope0
    ntab = normal(stab)
    for j in range(3):
        copy_w1[j].wait()
        at = width + (j + 1) * mid
        table_ref[:, at : at + mid] = mm(ntab, w1_ref[j * width : (j + 1) * width, :])
    copy_w2.wait()


def main_kernel(
    crow, prow, bases_ref, own_ref, far_ref, w_ref, p_ref, w2_ref, table_ref,
    features_ref, mine_ref, other_ref, h_ref, c_ref, w1_ref, p0_ref,
    hot_ref, stream_ref, normed_ref, act1_ref, act2_ref, slope1_ref, slope2_ref,
    cot_ref, grad_ref, back_ref, conv_ref, point_ref, ntab_ref, pt_ref, sent_ref, sems,
):
    n, _, rb = bases_ref.shape
    rows, width = stream_ref.shape
    mid = act1_ref.shape[1]
    dil, half = rb // 8, width // 2
    k = lax.axis_index("seq")
    zh, r, core = k // STRIDE, k % STRIDE, k % 2
    place = pl.ds(pl.multiple_of(zh * rb, 16), rb)
    far = pl.ds(pl.multiple_of((1 - zh) * rb, 16), rb)
    copy_p1 = fetch(p_ref.at[1], pt_ref.at[0], sems.at[0])
    copy_p2 = fetch(p_ref.at[2], pt_ref.at[1], sems.at[1])
    copy_w1 = fetch(w_ref.at[1], w1_ref, sems.at[2])
    copy_p0 = fetch(p_ref.at[0], p0_ref, sems.at[3])
    held = jnp.concatenate([bases_ref[i] for i in range(n)])
    held = (held - 4).astype(F32)
    edge = jnp.zeros((1, rb), F32)
    held = jnp.concatenate(
        [
            jnp.concatenate([edge, held[:-1]]).astype(BF16),
            held.astype(BF16),
            jnp.concatenate([held[1:], edge]).astype(BF16),
        ]
    )
    ahead = lax.broadcasted_iota(jnp.int32, (rb, rb), 0) - lax.broadcasted_iota(jnp.int32, (rb, rb), 1)

    def weight(gap):
        value = jnp.where(gap == -dil, 20.0, jnp.where(gap == 0, 5.0, jnp.where(gap == dil, 1.0, 0.0)))
        return value.astype(BF16)

    cls = (
        mm(held[:n], weight(ahead - rb)) + mm(held[n : 2 * n], weight(ahead)) + mm(held[2 * n :], weight(ahead + rb))
        + 105.0
    ).astype(BF16)
    block = lax.broadcasted_iota(jnp.int32, (n, CLASSES), 0)
    slot = lax.broadcasted_iota(jnp.int32, (n, CLASSES), 1)
    wanted = (slot // 3) * STRIDE + r + 2 * (slot % 3) - 2
    pick = jnp.where((block == wanted) & (slot < 6), 1.0, 0.0).astype(BF16)
    column = mm_tn(cls, pick)
    lanes = (lax.broadcasted_iota(jnp.int32, (rb, CLASSES), 1) + 1).astype(F32)
    for a in range(2):
        for j in range(3):
            i = 3 * a + j
            hot_ref[a * rb : (a + 1) * rb, j * CLASSES : (j + 1) * CLASSES] = jnp.where(
                lanes == column[:, i : i + 1], 1.0, 0.0
            ).astype(BF16)

    hot = hot_ref[...]
    mid_hot = hot[:, CLASSES : 2 * CLASSES]
    u = jnp.concatenate(
        [table_ref[:, width + (j + 1) * mid : width + (j + 2) * mid] for j in range(3)]
    )
    u_high = u.astype(BF16)
    act1, slope1 = gelu_pair(mm(hot, u_high) + mm(hot, (u - u_high.astype(F32)).astype(BF16)))
    act1 = act1.astype(BF16)
    act1_ref[...] = act1
    slope1_ref[...] = slope1
    stab = table_ref[:, :width]
    s_high = stab.astype(BF16)
    stream = mm(mid_hot, s_high) + mm(mid_hot, (stab - s_high.astype(F32)).astype(BF16))
    copy_p1.wait()
    stream = stream + mm(act1, pt_ref[0])
    stream_ref[...] = stream
    normed = normal(stream)
    normed_ref[...] = normed
    sides = jnp.concatenate(
        [mm(normed[rb:], w2_ref[2 * width :, :]), mm(normed[:rb], w2_ref[:width, :])]
    )
    act2, slope2 = gelu_pair(mm(normed, w2_ref[width : 2 * width, :]) + sides)
    act2_ref[...] = act2.astype(BF16)
    slope2_ref[...] = slope2
    copy_p2.wait()
    sent_ref[...] = stream_ref[place, :] + mm(act2_ref[place, :], pt_ref[1])
    copy_features = fetch(sent_ref, features_ref, sems.at[4])

    cot_ref[place, :] = own_ref[...]
    cot_ref[far, :] = far_ref[...]
    grad2 = (mm_nt(cot_ref[...], pt_ref[1]) * slope2_ref[...]).astype(BF16)
    grad_ref[...] = grad2
    sides = jnp.concatenate(
        [mm_nt(grad2[rb:], w2_ref[:width, :]), mm_nt(grad2[:rb], w2_ref[2 * width :, :])]
    )
    ng = mm_nt(grad2, w2_ref[width : 2 * width, :]) + sides
    stream = stream_ref[...]
    scale = norm_scale(stream)
    inner = jnp.mean(ng * stream, axis=-1, keepdims=True)
    back = cot_ref[...].astype(F32) + scale * (ng - stream * (scale * scale * inner))
    back = back.astype(BF16)
    back_ref[...] = back
    grad1 = (mm_nt(back, pt_ref[0]) * slope1_ref[...]).astype(BF16)

    h = mm_tn(hot_ref[...], grad1).astype(BF16)
    h_ref[...] = h
    h = [h[j * CLASSES : (j + 1) * CLASSES] for j in range(3)]
    c_ref[...] = mm_tn(hot_ref[:, CLASSES : 2 * CLASSES], back)
    ntab_ref[...] = normal(table_ref[:, :width])

    columns = pl.ds(pl.multiple_of(zh * half, 128), half)
    side_at = pl.ds(pl.multiple_of(zh * half, 16), width)
    center_at = pl.ds(pl.multiple_of((1 - zh) * width, 16), half)
    conv_ref[0, side_at, :] = mm_tn(ntab_ref[...], jnp.where(zh == 0, h[0], h[2]))
    conv_ref[0, center_at, :] = mm_tn(ntab_ref[:, columns], h[1])
    conv_ref[1, side_at, :] = mm_tn(normed_ref[place, :], grad_ref[far, :])
    conv_ref[1, center_at, :] = mm_tn(normed_ref[:, columns], grad_ref[...])
    point_ref[0] = mm_tn(back_ref[:, columns], act1_ref[...])
    point_ref[1] = mm_tn(cot_ref[:, columns], act2_ref[...])
    part = crow + prow
    for target, side in ((mine_ref, core), (other_ref, 1 - core)):
        for m in range(STRIDE // 2):
            tile = 2 * m + side
            crows = pl.ds(pl.multiple_of(tile * crow, 16), crow)
            prows = pl.ds(pl.multiple_of(tile * prow, 16), prow)
            for layer in range(2):
                at = (2 * m + layer) * part
                target[at : at + crow, :] = conv_ref[layer, crows, :].astype(target.dtype)
                target[at + crow : at + part, :] = point_ref[layer, prows, :].astype(target.dtype)
    for copy in (copy_features, copy_w1, copy_p0):
        copy.wait()


def class_kernel(prow, h_ref, c_ref, table_ref, w1_ref, p0_ref, mine_ref, other_ref, b_ref, bt_ref):
    width, mid = c_ref.shape[1], h_ref.shape[1]
    half = width // 2
    k = lax.axis_index("seq")
    zh, core = k // STRIDE, k % 2
    ng = None
    for j in range(3):
        term = mm_nt(
            h_ref[j * CLASSES : (j + 1) * CLASSES, :], w1_ref[j * width : (j + 1) * width, :]
        )
        ng = term if ng is None else ng + term
    stab = table_ref[:, :width]
    scale = norm_scale(stab)
    inner = jnp.mean(ng * stab, axis=-1, keepdims=True)
    b = c_ref[...] + scale * (ng - stab * (scale * scale * inner))
    s = (mm_nt(b.astype(BF16), p0_ref[...]) * table_ref[:, width : width + mid]).astype(BF16)
    g = mm(digit_rows(), s)
    b_ref[...] = b
    bt_ref[...] = jnp.transpose(b_ref[:, pl.ds(pl.multiple_of(zh * half, 128), half)])
    for target, side in ((mine_ref, core), (other_ref, 1 - core)):
        for m in range(STRIDE // 2):
            for q in range(3):
                at = pl.ds(pl.multiple_of((2 * m + side) * prow + 16 * q, 16), 16)
                target[16 * m : 16 * m + 16, q * CLASSES : (q + 1) * CLASSES] = bt_ref[at, :].astype(
                    target.dtype
                )
        target[8 * STRIDE : 8 * STRIDE + 16, :] = g.astype(target.dtype)


def message_kernel(part, mine_ref, other_ref, mine_small_ref, other_small_ref, *out_refs):
    k, x = lax.axis_index("seq"), lax.axis_index("dp")
    m = (k % STRIDE) // 2
    end = 8 * STRIDE
    g = mine_small_ref[end:, :] + other_small_ref[end:, :].astype(F32)
    for mask, out_ref in enumerate(out_refs):
        target, layer = m ^ (mask // 2), x ^ (mask % 2)
        at = pl.ds(pl.multiple_of((2 * target + layer) * part, 16), part)
        out_ref[:part, :] = (mine_ref[at, :] + other_ref[at, :].astype(F32)).astype(out_ref.dtype)
        at = pl.ds(pl.multiple_of(target * 16, 16), 16)
        small = mine_small_ref[at, :] + other_small_ref[at, :].astype(F32)
        out_ref[part : part + 16, :] = small.astype(out_ref.dtype)
        out_ref[part + 16 :, :] = g.astype(out_ref.dtype)


def sum_kernel(own_ref, *refs):
    got, (total_ref, send_ref, rest_ref) = refs[:-3], refs[-3:]
    part = total_ref.shape[0]
    total = own_ref[...]
    for ref in got:
        total = total + ref[...].astype(F32)
    total_ref[...] = total[:part]
    send_ref[...] = total[:part].astype(BF16)
    rest_ref[...] = total[part:]


def small_kernel(
    rest_ref, total_ref, embed_ref, w_ref, act0_ref, spread_ref,
    conv_ref, point_ref, embed_out_ref, bt_ref, w0_ref, conv0_ref, point0_ref, sems,
):
    copy_w0 = fetch_taps(w_ref, 0, w0_ref, sems, 0)
    width = embed_ref.shape[1]
    crow = conv_ref.shape[1]
    own = lax.axis_index("dp") + 1
    copies = [
        fetch(total_ref.at[pl.ds(0, crow), :], conv_ref.at[own], sems.at[3]),
        fetch(total_ref.at[pl.ds(crow, point_ref.shape[1]), :], point_ref.at[own], sems.at[4]),
    ]
    g = rest_ref[16:, :]
    bt = jnp.concatenate([rest_ref[:16, q * CLASSES : (q + 1) * CLASSES] for q in range(3)])
    bt = bt.astype(BF16)
    g16 = g.astype(BF16)
    conv0_ref[...] = mm(spread_ref[...], g16)
    copies.append(fetch(conv0_ref, conv_ref.at[0], sems.at[5]))
    point0_ref[...] = mm(bt, act0_ref[...])
    copies.append(fetch(point0_ref, point_ref.at[0], sems.at[6]))
    bt_ref[...] = mm_nt(digit_rows(), bt)[4:8]
    stream = embed_ref[...].astype(F32)
    scale = norm_scale(stream)
    ng = None
    for j in range(3):
        copy_w0[j].wait()
        term = mm_nt(g16, w0_ref[j * width : (j + 1) * width, :])[4 * j : 4 * j + 4]
        ng = term if ng is None else ng + term
    inner = jnp.mean(ng * stream, axis=-1, keepdims=True)
    embed_out_ref[...] = scale * (ng - stream * (scale * scale * inner))
    for copy in copies:
        copy.wait()


def finish_kernel(got_ref, _, __, conv_ref, point_ref, held_ref, sems):
    crow = conv_ref.shape[1]
    other = 2 - lax.axis_index("dp")
    held_ref[...] = got_ref[...].astype(F32)
    copies = [
        fetch(held_ref.at[pl.ds(0, crow), :], conv_ref.at[other], sems.at[0]),
        fetch(held_ref.at[pl.ds(crow, point_ref.shape[1]), :], point_ref.at[other], sems.at[1]),
    ]
    for copy in copies:
        copy.wait()


def call(kernel, outs, *args, far=(), whole=(), away=(), scratch=(), limit=24, aliases=None, flops=0, name=None):
    args = [pltpu.with_memory_space_constraint(v, pltpu.HBM) if i in far else v for i, v in enumerate(args)]
    moved = sum(math.prod(v.shape) * jnp.dtype(v.dtype).itemsize for v in list(args) + list(outs))
    return pl.pallas_call(
        kernel,
        out_shape=outs,
        in_specs=[
            pl.BlockSpec(memory_space=pltpu.HBM if i in far and i not in whole else pltpu.VMEM)
            for i in range(len(args))
        ],
        out_specs=[
            pl.BlockSpec(memory_space=pltpu.HBM if i in away else pltpu.VMEM) for i in range(len(outs))
        ],
        scratch_shapes=list(scratch),
        input_output_aliases=aliases or {},
        compiler_params=pltpu.CompilerParams(vmem_limit_bytes=limit * 1024 * 1024),
        cost_estimate=pl.CostEstimate(flops=flops, bytes_accessed=moved, transcendentals=0),
        name=name,
    )(*args)


def on_device(bases, embed, conv_weight, point_weight, cotangent):
    n, dp = lax.axis_size("seq"), lax.axis_size("dp")
    rb, width, mid = bases.shape[1], embed.shape[1], conv_weight.shape[2]
    if n != 2 * STRIDE or dp != 2:
        return general(bases, embed, conv_weight, point_weight, cotangent)
    k = lax.axis_index("seq")
    zh, r = k // STRIDE, k % STRIDE
    rows = 2 * rb
    crow, prow = 3 * width // n, width // n
    part = crow + prow
    shape, near = jax.ShapeDtypeStruct, pltpu.VMEM

    own = cotangent[0]
    far = lax.ppermute(own, "seq", [(s, (s + STRIDE) % n) for s in range(n)])
    (copies,) = call(spread_kernel, [near((n, 1, rb), jnp.int32)], bases, far=(0,), whole=(0,), name="spread")
    gathered = lax.all_to_all(copies, "seq", 0, 0, tiled=True)

    taps = pltpu.VMEM((3 * width, mid), BF16)
    act0, table, w2 = call(
        table_kernel,
        [
            shape((CLASSES, mid), BF16),
            pltpu.VMEM((CLASSES, width + 4 * mid), F32),
            pltpu.VMEM((3 * width, mid), BF16),
        ],
        embed, conv_weight, point_weight,
        far=(0, 1, 2),
        whole=(0,),
        scratch=[taps, taps, pltpu.VMEM((mid, width), BF16), pltpu.SemaphoreType.DMA((8,))],
        limit=20,
        flops=4 * CLASSES * 3 * width * mid,
        name="tables",
    )
    features, mine, other, h, c, w1, p0 = call(
        lambda *refs: main_kernel(crow, prow, *refs),
        [
            shape((rb, width), F32),
            near((STRIDE * part, mid), F32),
            near((STRIDE * part, mid), BF16),
            near((3 * CLASSES, mid), BF16),
            near((CLASSES, width), F32),
            near((3 * width, mid), BF16),
            near((mid, width), BF16),
        ],
        gathered, own, far, conv_weight, point_weight, w2, table,
        far=(3, 4),
        scratch=[
            pltpu.VMEM((rows, 3 * CLASSES), BF16),
            pltpu.VMEM((rows, width), F32),
            pltpu.VMEM((rows, width), BF16),
            pltpu.VMEM((rows, mid), BF16),
            pltpu.VMEM((rows, mid), BF16),
            pltpu.VMEM((rows, mid), F32),
            pltpu.VMEM((rows, mid), F32),
            pltpu.VMEM((rows, width), BF16),
            pltpu.VMEM((rows, mid), BF16),
            pltpu.VMEM((rows, width), BF16),
            pltpu.VMEM((2, STRIDE * crow, mid), F32),
            pltpu.VMEM((2, STRIDE * prow, mid), F32),
            pltpu.VMEM((CLASSES, width), BF16),
            pltpu.VMEM((2, mid, width), BF16),
            pltpu.VMEM((rb, width), F32),
            pltpu.SemaphoreType.DMA((5,)),
        ],
        away=(0,),
        flops=9 * rows * 3 * width * mid,
        name="tower",
    )

    swap = [(s, s ^ 1) for s in range(n)]
    got = lax.ppermute(other, "seq", swap)
    small_rows = 8 * STRIDE + 16
    mine_small, other_small = call(
        lambda *refs: class_kernel(prow, *refs),
        [near((small_rows, mid), F32), near((small_rows, mid), BF16)],
        h, c, table, w1, p0,
        scratch=[pltpu.VMEM((CLASSES, width), F32), pltpu.VMEM((width // 2, CLASSES), F32)],
        flops=4 * CLASSES * 3 * width * mid,
        name="classes",
    )
    got_small = lax.ppermute(other_small, "seq", swap)
    peers = STRIDE // 2 * dp
    pieces = call(
        lambda *refs: message_kernel(part, *refs),
        [shape((part + 32, mid), F32 if i == 0 else BF16) for i in range(peers)],
        mine, got, mine_small, got_small,
        name="messages",
    )
    arrived = []
    for mask in ORDER:
        route = [
            (s * dp + d, (s ^ (2 * (mask // dp))) * dp + (d ^ (mask % dp)))
            for s in range(n)
            for d in range(dp)
        ]
        arrived.append(lax.ppermute(pieces[mask], ("seq", "dp"), route))
    total, send, rest = call(
        sum_kernel,
        [shape((part, mid), F32), shape((part, mid), BF16), shape((32, mid), F32)],
        pieces[0], *arrived,
        name="sums",
    )
    swapped = lax.ppermute(send, "dp", [(d, d ^ 1) for d in range(dp)])

    stream_e = embed.astype(F32)
    normed_e = (stream_e * norm_scale(stream_e)).astype(BF16)
    spread = jnp.concatenate(
        [jnp.pad(normed_e, ((4 * j, 12 - 4 * j), (0, 0))) for j in range(3)], axis=1
    )
    spread = lax.dynamic_slice_in_dim(spread, k * crow, crow, axis=1).T
    conv_grad, point_grad, embed_full, bt = call(
        small_kernel,
        [
            shape((3, crow, mid), F32),
            shape((3, prow, mid), F32),
            shape((4, width), F32),
            shape((4, prow), F32),
        ],
        rest, total, embed, conv_weight, act0, spread,
        far=(3,),
        away=(0, 1),
        scratch=[
            pltpu.VMEM((3 * width, mid), BF16),
            pltpu.VMEM((crow, mid), F32),
            pltpu.VMEM((prow, mid), F32),
            pltpu.SemaphoreType.DMA((7,)),
        ],
        name="layer0",
    )
    embed_grad = bt + lax.dynamic_slice_in_dim(embed_full, k * prow, prow, axis=1)
    conv_grad, point_grad = call(
        finish_kernel,
        [shape((3, crow, mid), F32), shape((3, prow, mid), F32)],
        swapped, conv_grad, point_grad,
        far=(1, 2),
        away=(0, 1),
        aliases={1: 0, 2: 1},
        scratch=[pltpu.VMEM((part, mid), F32), pltpu.SemaphoreType.DMA((2,))],
        name="finish",
    )
    return features[None], conv_grad, point_grad.transpose(0, 2, 1), embed_grad


def solution(mesh):
    in_specs = (P("dp", "seq"), P(), P(), P(), P("dp", "seq", None))
    out_specs = (P("dp", "seq", None), P(None, "seq", None), P(None, None, "seq"), P(None, "seq"))
    return jax.shard_map(
        on_device, mesh=mesh, in_specs=in_specs, out_specs=out_specs, check_vma=False
    )
```
